32 devices in a mesh: mem: 4 (over y, x), col: 8 (over z, core).
Axes of the slice: x: 2, y: 2, z: 4, core: 2. Of those that a mesh axis runs over, the one named last changes fastest.
Arguments:
- adj_final: float32 [16, 137, 4096], P('mem', None, 'col'), parts along dimension 0, may hold values from -60 to 60
- inverses: float32 [8, 32, 137, 137], P('mem', 'col'), parts along dimension 0, may hold values from 0 to 1
- dep_lists: int32 [8, 32, 5], P('mem', 'col'), parts along dimension 0, may hold values from 0 to 31, as said below
- dep_points: int32 [8, 4, 4096], P('mem', None, 'col'), parts along dimension 0, may hold values from 0 to 639, as said below
- weights: float32 [8, 4, 4096], P('mem', None, 'col'), parts along dimension 0, may hold values from 0 to 1, as said below
Outputs:
- adj_mid: float32 [16, 137, 4096], P('mem', None, 'col'), parts along dimension 0
- lanczos: float32 [16, 137, 4096], P('mem', None, 'col'), parts along dimension 0
The draws below stay inside these ranges and needn't reach their ends.
There are 4 independent parts, one for each index of `mem`. The reference program is written for one: setup_inputs(seed, part) draws one part's arguments, and reference() takes and returns one part's arrays. A program takes and returns all parts, laid end to end along the dimension named above; each array names one. Nothing has to cross between parts.
Inputs may be any that keep to these rules, and one draw needn't show every extreme that they name: `dep_lists`: every entry of a block's list is a block within 2 blocks of that block, counting cyclically over all 32 blocks; the list's first entries are distinct and the rest repeat the block itself. `dep_points`: the slot of every point indexes one of the first entries of its arrival block's list. The 4 weights of a column are bilinear weights and sum to one.
All inputs are finite; a program needn't handle non-finite values.
Results may differ from the reference program's by a relative error of at most 0.0003.
Values sent between devices are 32-bit elements; how exact they have to be, the bound alone decides.
No kernel may reach another device: no remote copies, remote signals or barrier semaphores. Data moves between devices by JAX's collectives and lax.ppermute only.
A program may use at most 64 MiB of HBM per device.

```python
import math
import jax
import jax.numpy as jnp
from jax import lax

LEVELS = 137
VARS = 4
BCOLS = 128
REACH = 2
SLOTS = 5
POINTS = 4
STEPS = 2
NBLK = 32
COLS = 4096


def slot_counts(key):
    key_counts = jax.random.fold_in(key, 17)
    key_start, key_strong, key_drawn = jax.random.split(key_counts, 3)
    blocks = jnp.arange(NBLK, dtype=jnp.int32)
    start = jax.random.randint(key_start, (STEPS, 1), 0, NBLK)
    band = (blocks[None, :] - start) % NBLK < max(NBLK // 4, 1)
    strong = jax.random.randint(key_strong, (STEPS, NBLK), 3, SLOTS + 1)
    drawn = jax.random.randint(key_drawn, (STEPS, NBLK), 1, 3)
    counts = jnp.where(band, strong, drawn).astype(jnp.int32)
    return counts.at[:, 0].set(SLOTS)


def draw_dep_lists(key, part):
    counts = slot_counts(key)
    key_lists = jax.random.fold_in(key, 29)
    width = 2 * REACH + 1
    scores = jax.random.randint(key_lists, (STEPS, NBLK, width), 0, 1 << 20) * width + jnp.arange(width, dtype=jnp.int32)
    order = jnp.argsort(scores, axis=-1).astype(jnp.int32)
    offsets = order[:, :, :SLOTS] - REACH
    used = jnp.arange(SLOTS, dtype=jnp.int32)[None, None, :] < counts[:, :, None]
    offsets = jnp.where(used, offsets, 0)
    blocks = jnp.arange(NBLK, dtype=jnp.int32)[None, :, None]
    return ((blocks + offsets) % NBLK).astype(jnp.int32)


def draw_dep_points(key, part):
    counts = slot_counts(key)
    key_points = jax.random.fold_in(key, 41)
    key_slot, key_within = jax.random.split(key_points, 2)
    per_column = jnp.repeat(counts, BCOLS, axis=1)
    raw = jax.random.randint(key_slot, (STEPS, POINTS, COLS), 0, 1 << 20)
    slot_ids = raw % per_column[:, None, :]
    within = jax.random.randint(key_within, (STEPS, POINTS, COLS), 0, BCOLS)
    points = (slot_ids * BCOLS + within).astype(jnp.int32)
    points = points.at[:, 0, 0].set((SLOTS - 1) * BCOLS + BCOLS - 1)
    points = points.at[:, 1, 0].set(0)
    return points


def draw_weights(key, part):
    key_east, key_north = jax.random.split(key, 2)
    east = jax.random.uniform(key_east, (STEPS, COLS), jnp.float32)
    north = jax.random.uniform(key_north, (STEPS, COLS), jnp.float32)
    stacked = jnp.stack([(1.0 - east) * (1.0 - north), east * (1.0 - north), (1.0 - east) * north, east * north], axis=1)
    return stacked.astype(jnp.float32)


def draw_adj_final(key, part):
    key_base, key_level = jax.random.split(key, 2)
    position = jnp.arange(COLS, dtype=jnp.float32) / COLS
    col_scale = jnp.exp(math.log(10.0) * (position - 0.5))[None, None, :]
    level_scale = jnp.exp(math.log(10.0) * (jax.random.uniform(key_level, (VARS, LEVELS, 1), jnp.float32) - 0.5))
    base = jnp.clip(jax.random.normal(key_base, (VARS, LEVELS, COLS), jnp.float32), -6.0, 6.0)
    return (base * col_scale * level_scale).astype(jnp.float32)


def draw_inverses(key, part):
    key_length, key_diag, key_spread = jax.random.split(key, 3)
    length = jnp.exp(jax.random.uniform(key_length, (STEPS, NBLK, 1, 1), jnp.float32, math.log(2.0), math.log(20.0)))
    level_rows = jnp.arange(LEVELS, dtype=jnp.float32)[:, None]
    level_cols = jnp.arange(LEVELS, dtype=jnp.float32)[None, :]
    distance = jnp.abs(level_rows - level_cols)
    diagonal = 1.0 + 0.3 * jax.random.uniform(key_diag, (STEPS, NBLK, LEVELS, 1), jnp.float32, -1.0, 1.0)
    spread = jax.random.uniform(key_spread, (STEPS, NBLK, LEVELS, LEVELS), jnp.float32, 0.0, 1.0)
    offdiag = 0.3 * jnp.exp(-distance / length) * spread
    matrix = jnp.where(distance == 0.0, diagonal, offdiag) / (1.0 + 0.3 * length)
    return matrix.astype(jnp.float32)


def setup_inputs(seed: int = 0, part: int = 0) -> dict:
    key_of = jax.random.split(jax.random.key(seed), 6)
    part_splits = jax.random.split(jax.random.fold_in(key_of[5], part), 6)
    adj_final = draw_adj_final(jax.random.fold_in(jax.random.fold_in(key_of[5], part), 71), part)
    inverses = draw_inverses(jax.random.fold_in(jax.random.fold_in(key_of[5], part), 71), part)
    dep_lists = draw_dep_lists(jax.random.fold_in(jax.random.fold_in(key_of[5], part), 71), part)
    dep_points = draw_dep_points(jax.random.fold_in(jax.random.fold_in(key_of[5], part), 71), part)
    weights = draw_weights(jax.random.fold_in(jax.random.fold_in(key_of[5], part), 71), part)
    return {"adj_final": adj_final, "inverses": inverses, "dep_lists": dep_lists, "dep_points": dep_points, "weights": weights}


eps_energy = 1e-06

def adjoint_step(adjoint, inverse, routes, points, weights):
    variables, levels, col_count = adjoint.shape
    block_count = col_count // BCOLS
    blocked = adjoint.reshape(variables, levels, block_count, BCOLS)
    diffused = jnp.einsum('blk,vlbc->vkbc', inverse, blocked, precision=lax.Precision.HIGHEST)
    columns_first = diffused.reshape(variables * levels, col_count).T
    slot_ids = points // BCOLS
    within = points % BCOLS
    arrival = jnp.arange(col_count, dtype=jnp.int32) // BCOLS
    target = (routes[arrival[None, :], slot_ids] * BCOLS + within).astype(jnp.int32)
    accumulated = jnp.zeros_like(columns_first)
    for point_index in range(POINTS):
        accumulated = accumulated.at[target[point_index]].add(weights[point_index][:, None] * columns_first)
    return accumulated.T.reshape(variables, levels, col_count)

def reference(adj_final, inverses, dep_lists, dep_points, weights):
    adjoint = adj_final
    adj_mid = adj_final
    for step_index in range(STEPS - 1, -1, -1):
        adjoint = adjoint_step(adjoint, inverses[step_index], dep_lists[step_index], dep_points[step_index], weights[step_index])
        if step_index == STEPS - 1:
            adj_mid = adjoint
    energy = jnp.mean(adjoint * adjoint)
    lanczos = adjoint / jnp.sqrt(energy + eps_energy)
    return (adj_mid, lanczos)
```

```python
import functools

import jax
import jax.numpy as jnp
from jax import lax
from jax.experimental import pallas as pl
from jax.experimental.pallas import tpu as pltpu
from jax.sharding import PartitionSpec as P

BCOLS = 128
REACH = 2
SLOTS = 5
POINTS = 4
STEPS = 2
EDGE = REACH * BCOLS
CHUNKS = 2
VMEM_LIMIT = 32 * 1024 * 1024

eps_energy = 1e-06

F32 = jnp.float32
BF16 = jnp.bfloat16
ANY = pl.BlockSpec(memory_space=pl.ANY)


def padded(count):
    return -(-count // 8) * 8


def z_side(block_count):
    follows = lax.rem(lax.axis_index("col"), 2)
    first = follows * (block_count - REACH)
    return follows, first, follows * (block_count + REACH) - REACH


def core_side(block_count):
    follows = 1 - lax.rem(lax.axis_index("col"), 2)
    first = follows * (block_count - REACH)
    return follows, first, follows * (block_count + REACH) - REACH


def lanes(block, count):
    return pl.ds(pl.multiple_of(block * BCOLS, BCOLS), count * BCOLS)


def split(value):
    high = value.astype(BF16)
    return high, (value - high.astype(F32)).astype(BF16)


def dot3(left, right, dims):
    def one(a, b):
        return lax.dot_general(a, b, (dims, ((), ())), preferred_element_type=F32)

    return one(left[0], right[0]) + (one(left[0], right[1]) + one(left[1], right[0]))


def target_columns(points, routes, step, block, block_count, all_blocks):
    slots = points // BCOLS
    here = lax.axis_index("col") * block_count + block
    found = jnp.zeros_like(points)
    for slot in range(SLOTS):
        offset = lax.rem(routes[step, block, slot] - here + REACH + all_blocks, all_blocks) - REACH
        found = jnp.where(slots == slot, (block + offset) * BCOLS, found)
    return found + points % BCOLS


def spread_matrix(targets, weights, first_target, rows):
    row = lax.broadcasted_iota(jnp.int32, (rows, targets.shape[1]), 0) + first_target
    total = jnp.zeros(row.shape, F32)
    for point in range(POINTS):
        total += jnp.where(row == targets[point : point + 1], weights[point : point + 1], 0.0)
    return split(total)


def diffuse(inverse, fields):
    turned = split(inverse.T)
    return dot3(turned, split(jnp.concatenate(fields, axis=1)), ((1,), (0,)))


def pack(sums, variables, levels, tall, out):
    even = levels // 8 * 8
    rest = levels - even
    for number in range(variables * REACH):
        variable, block = divmod(number, REACH)
        cols = slice(block * BCOLS, (block + 1) * BCOLS)
        out[number * even : (number + 1) * even] = sums[variable * tall : variable * tall + even, cols]
        tail = variables * REACH * even + number * rest
        out[tail : tail + rest] = sums[variable * tall + even : variable * tall + levels, cols]


def add_packed(packed, variables, levels, where, first_variable, first_block):
    even = levels // 8 * 8
    rest = levels - even
    for number in range(variables * REACH):
        variable, block = divmod(number, REACH)
        cols = lanes(first_block + block, 1)
        tail = variables * REACH * even + number * rest
        at = first_variable + variable
        where[at, :even, cols] += packed[number * even : (number + 1) * even]
        where[at, even:, cols] += packed[tail : tail + rest]


def edge_kernel(step, chunk, all_blocks, has_halo, *refs):
    fields, inverses, routes, points, weights = refs[:5]
    halo = refs[5] if has_halo else None
    out, field, inverse, route, point, weight, tall, incoming, sems = refs[5 + has_halo :]
    variables, levels, _ = field.shape
    block_count = inverses.shape[1]
    _, first, first_target = z_side(block_count)
    copies = [
        pltpu.make_async_copy(routes, route, sems.at[0]),
        pltpu.make_async_copy(points.at[step, :, lanes(first, REACH)], point, sems.at[1]),
        pltpu.make_async_copy(weights.at[step, :, lanes(first, REACH)], weight, sems.at[2]),
        pltpu.make_async_copy(inverses.at[step, pl.ds(first, REACH)], inverse, sems.at[3]),
        pltpu.make_async_copy(
            fields.at[pl.ds(chunk * variables, variables), :, lanes(first, REACH)], field, sems.at[4]
        ),
    ]
    if has_halo:
        copies.append(pltpu.make_async_copy(halo, incoming, sems.at[5]))
    for copy in copies:
        copy.start()
    for copy in copies[:3]:
        copy.wait()
    targets = jnp.concatenate(
        [
            target_columns(
                point[:, j * BCOLS : (j + 1) * BCOLS], route, step, first + j, block_count, all_blocks
            )
            for j in range(REACH)
        ],
        axis=1,
    )
    matrix = spread_matrix(targets, weight[...], first_target * BCOLS, EDGE)
    for copy in copies[3:]:
        copy.wait()
    if has_halo:
        add_packed(incoming, variables, levels, field, 0, 0)
    tall[:, levels // 8 * 8 :, :] = jnp.zeros((variables, 8, EDGE), F32)
    for j in range(REACH):
        cols = slice(j * BCOLS, (j + 1) * BCOLS)
        diffused = diffuse(inverse[j], [field[v, :, cols] for v in range(variables)])
        for v in range(variables):
            tall[v, :levels, cols] = diffused[:, v * BCOLS : (v + 1) * BCOLS]
    high = tall.shape[1]
    sums = dot3(split(tall[...].reshape(variables * high, EDGE)), matrix, ((1,), (1,)))
    pack(sums, variables, levels, high, out)


def edge(step, chunk, all_blocks, fields, inverses, routes, points, weights, halo=None):
    variables = fields.shape[0] // CHUNKS
    levels = fields.shape[1]
    has_halo = halo is not None
    packed = jax.ShapeDtypeStruct((variables * REACH * levels, BCOLS), F32)
    operands = (fields, inverses, routes, points, weights) + ((halo,) if has_halo else ())
    return pl.pallas_call(
        functools.partial(edge_kernel, step, chunk, all_blocks, has_halo),
        out_shape=packed,
        in_specs=[ANY] * len(operands),
        out_specs=pl.BlockSpec(memory_space=pltpu.VMEM),
        scratch_shapes=[
            pltpu.VMEM((variables, levels, EDGE), F32),
            pltpu.VMEM((REACH, levels, levels), F32),
            pltpu.SMEM(routes.shape, jnp.int32),
            pltpu.VMEM((POINTS, EDGE), jnp.int32),
            pltpu.VMEM((POINTS, EDGE), F32),
            pltpu.VMEM((variables, padded(levels), EDGE), F32),
            pltpu.VMEM(packed.shape, F32),
            pltpu.SemaphoreType.DMA((6,)),
        ],
        compiler_params=pltpu.CompilerParams(vmem_limit_bytes=VMEM_LIMIT),
        cost_estimate=pl.CostEstimate(flops=400_000_000, bytes_accessed=2_000_000, transcendentals=0),
        name=f"edge_step{step}_chunk{chunk}",
    )(*operands)


def rest_kernel(step, all_blocks, has_halo, *refs):
    fields, inverses, routes, points, weights = refs[:5]
    count = (1 + CHUNKS) if has_halo else 0
    halos = refs[5 : 5 + count]
    refs = refs[5 + count :]
    own, core_out = refs[:2]
    mid = refs[2] if has_halo else None
    refs = refs[2 + has_halo :]
    field, inverse, route, point, weight, tall, core_in, z_in, sems = refs
    variables, levels, columns = field.shape
    block_count = inverses.shape[1]
    _, z_first, _ = z_side(block_count)
    _, core_first, core_target = core_side(block_count)
    copies = [
        pltpu.make_async_copy(routes, route, sems.at[0]),
        pltpu.make_async_copy(points.at[step], point, sems.at[1]),
        pltpu.make_async_copy(weights.at[step], weight, sems.at[2]),
        pltpu.make_async_copy(inverses.at[step], inverse, sems.at[3]),
        pltpu.make_async_copy(fields, field, sems.at[4]),
    ]
    if has_halo:
        copies.append(pltpu.make_async_copy(halos[0], core_in, sems.at[5]))
        for chunk in range(CHUNKS):
            copies.append(pltpu.make_async_copy(halos[1 + chunk], z_in.at[chunk], sems.at[6 + chunk]))
    for copy in copies:
        copy.start()
    for copy in copies[:3]:
        copy.wait()
    targets = jnp.concatenate(
        [
            target_columns(
                point[:, j * BCOLS : (j + 1) * BCOLS], route, step, j, block_count, all_blocks
            )
            for j in range(block_count)
        ],
        axis=1,
    )
    point[...] = targets
    inner = spread_matrix(targets, weight[...], 0, columns)
    side = lanes(core_first, REACH)
    outer = spread_matrix(point[:, side], weight[:, side], core_target * BCOLS, EDGE)
    for copy in copies[3:]:
        copy.wait()
    if has_halo:
        add_packed(core_in, variables, levels, field, 0, core_first)
        per = variables // CHUNKS
        for chunk in range(CHUNKS):
            add_packed(z_in.at[chunk], per, levels, field, chunk * per, z_first)
        mid_copy = pltpu.make_async_copy(field, mid, sems.at[8])
        mid_copy.start()
    tall[:, levels // 8 * 8 :, :] = jnp.zeros((variables, 8, columns), F32)
    for j in range(block_count):
        cols = slice(j * BCOLS, (j + 1) * BCOLS)
        diffused = diffuse(inverse[j], [field[v, :, cols] for v in range(variables)])
        for v in range(variables):
            tall[v, :levels, cols] = diffused[:, v * BCOLS : (v + 1) * BCOLS]
    high = tall.shape[1]
    edge_sums = dot3(split(tall[:, :, side].reshape(variables * high, EDGE)), outer, ((1,), (1,)))
    pack(edge_sums, variables, levels, high, core_out)
    sums = dot3(split(tall[...].reshape(variables * high, columns)), inner, ((1,), (1,)))
    for v in range(variables):
        own[v] = sums[v * high : v * high + levels]
    if has_halo:
        mid_copy.wait()


def rest(step, all_blocks, fields, inverses, routes, points, weights, halos=()):
    variables, levels, columns = fields.shape
    has_halo = bool(halos)
    whole = jax.ShapeDtypeStruct(fields.shape, F32)
    packed = jax.ShapeDtypeStruct((variables * REACH * levels, BCOLS), F32)
    part = jax.ShapeDtypeStruct((variables // CHUNKS * REACH * levels, BCOLS), F32)
    operands = (fields, inverses, routes, points, weights) + tuple(halos)
    vmem = pl.BlockSpec(memory_space=pltpu.VMEM)
    return pl.pallas_call(
        functools.partial(rest_kernel, step, all_blocks, has_halo),
        out_shape=(whole, packed) + ((whole,) if has_halo else ()),
        in_specs=[ANY] * len(operands),
        out_specs=(vmem, vmem) + ((ANY,) if has_halo else ()),
        scratch_shapes=[
            pltpu.VMEM(fields.shape, F32),
            pltpu.VMEM(inverses.shape[1:], F32),
            pltpu.SMEM(routes.shape, jnp.int32),
            pltpu.VMEM((POINTS, columns), jnp.int32),
            pltpu.VMEM((POINTS, columns), F32),
            pltpu.VMEM((variables, padded(levels), columns), F32),
            pltpu.VMEM(packed.shape, F32),
            pltpu.VMEM((CHUNKS,) + part.shape, F32),
            pltpu.SemaphoreType.DMA((9,)),
        ],
        compiler_params=pltpu.CompilerParams(vmem_limit_bytes=VMEM_LIMIT),
        cost_estimate=pl.CostEstimate(flops=2_000_000_000, bytes_accessed=5_000_000, transcendentals=0),
        name=f"rest_step{step}",
    )(*operands)


def total_kernel(count, own, core_in, *refs):
    z_in, (start, share) = refs[:CHUNKS], refs[CHUNKS:]
    variables, levels, columns = own.shape
    block_count = columns // BCOLS
    _, z_first, _ = z_side(block_count)
    _, core_first, _ = core_side(block_count)
    start[...] = own[...]
    add_packed(core_in, variables, levels, start, 0, core_first)
    per = variables // CHUNKS
    for chunk in range(CHUNKS):
        add_packed(z_in[chunk], per, levels, start, chunk * per, z_first)
    lane_sums = jnp.zeros((1, BCOLS), F32)
    for j in range(block_count):
        part = start[:, :, j * BCOLS : (j + 1) * BCOLS]
        lane_sums += jnp.sum(part * part, axis=(0, 1)).reshape(1, BCOLS)
    share[...] = jnp.broadcast_to(lane_sums, (count, BCOLS))


def total(count, own, core_in, z_in):
    vmem = pl.BlockSpec(memory_space=pltpu.VMEM)
    return pl.pallas_call(
        functools.partial(total_kernel, count),
        out_shape=(jax.ShapeDtypeStruct(own.shape, F32), jax.ShapeDtypeStruct((count, BCOLS), F32)),
        in_specs=[vmem] * (2 + CHUNKS),
        out_specs=(vmem, vmem),
        compiler_params=pltpu.CompilerParams(vmem_limit_bytes=VMEM_LIMIT),
        cost_estimate=pl.CostEstimate(flops=1_000_000, bytes_accessed=4_000_000, transcendentals=0),
        name="add_halos_and_square",
    )(own, core_in, *z_in)


def scale_kernel(cells, start, shares, out):
    energy = jnp.sum(shares[...]) / cells
    out[...] = start[...] / jnp.sqrt(jnp.full((1, 1, 1), energy + eps_energy, F32))


def scale(start, shares, cells):
    vmem = pl.BlockSpec(memory_space=pltpu.VMEM)
    return pl.pallas_call(
        functools.partial(scale_kernel, cells),
        out_shape=jax.ShapeDtypeStruct(start.shape, F32),
        in_specs=[vmem, vmem],
        out_specs=vmem,
        compiler_params=pltpu.CompilerParams(vmem_limit_bytes=VMEM_LIMIT),
        cost_estimate=pl.CostEstimate(flops=1_000_000, bytes_accessed=2_000_000, transcendentals=0),
        name="scale_start",
    )(start, shares)


def core_exchange(value):
    count = lax.axis_size("col")
    return lax.ppermute(value, "col", [(i, i ^ 1) for i in range(count)])


def z_exchange(value):
    count = lax.axis_size("col")
    pairs = [(i, (i + 1) % count if i % 2 else (i - 1) % count) for i in range(count)]
    return lax.ppermute(value, "col", pairs)


def shards(adj_final, inverses, dep_lists, dep_points, weights):
    count = lax.axis_size("col")
    all_blocks = count * inverses.shape[1]
    tables = (inverses, dep_lists, dep_points, weights)
    fields, halos, mid = adj_final, (), None
    for step in range(STEPS - 1, -1, -1):
        z_halos = []
        for chunk in range(CHUNKS):
            halo = halos[1 + chunk] if halos else None
            z_halos.append(z_exchange(edge(step, chunk, all_blocks, fields, *tables, halo=halo)))
        own, core_out, *written = rest(step, all_blocks, fields, *tables, halos=halos)
        if written:
            mid = written[0]
        fields, halos = own, (core_exchange(core_out), *z_halos)
    start, shares = total(count, fields, halos[0], halos[1:])
    shares = lax.all_to_all(shares, "col", 0, 0, tiled=True)
    return mid, scale(start, shares, adj_final.size * count)


def solution(mesh):
    in_specs = (
        P("mem", None, "col"),
        P("mem", "col", None, None),
        P("mem", "col", None),
        P("mem", None, "col"),
        P("mem", None, "col"),
    )
    out_specs = (P("mem", None, "col"), P("mem", None, "col"))
    return jax.shard_map(shards, mesh=mesh, in_specs=in_specs, out_specs=out_specs, check_vma=False)
```

```python
import functools

import jax
import jax.numpy as jnp
from jax import lax
from jax.experimental import pallas as pl
from jax.experimental.pallas import tpu as pltpu
from jax.sharding import PartitionSpec as P

BCOLS = 128
REACH = 2
SLOTS = 5
POINTS = 4
STEPS = 2
VMEM_LIMIT = 32 * 1024 * 1024

eps_energy = 1e-06

F32 = jnp.float32
BF16 = jnp.bfloat16
ANY = pl.BlockSpec(memory_space=pl.ANY)
HBM = pl.BlockSpec(memory_space=pltpu.HBM)
VMEM = pl.BlockSpec(memory_space=pltpu.VMEM)


def z_blocks(block_count):
    follows = lax.rem(lax.axis_index("col"), 2)
    near = follows * (block_count - 1)
    away = 2 * follows - 1
    return near, near - away, near + away, near + 2 * away


def core_side(block_count):
    follows = 1 - lax.rem(lax.axis_index("col"), 2)
    return follows * (block_count - REACH), follows * (block_count + REACH) - REACH


def lanes(block, count=1):
    return pl.ds(pl.multiple_of(block * BCOLS, BCOLS), count * BCOLS)


def split(value):
    high = value.astype(BF16)
    return high, (value - high.astype(F32)).astype(BF16)


def dot3(left, right, dims):
    def one(a, b):
        return lax.dot_general(a, b, (dims, ((), ())), preferred_element_type=F32)

    return one(left[0], right[0]) + (one(left[0], right[1]) + one(left[1], right[0]))


def target_columns(points, routes, step, block, block_count, all_blocks):
    slots = points // BCOLS
    here = lax.axis_index("col") * block_count + block
    found = jnp.zeros_like(points)
    for slot in range(SLOTS):
        offset = lax.rem(routes[step, block, slot] - here + REACH + all_blocks, all_blocks) - REACH
        found = jnp.where(slots == slot, (block + offset) * BCOLS, found)
    return found + points % BCOLS


def spread_matrix(targets, weights, first_column, rows=BCOLS):
    row = lax.broadcasted_iota(jnp.int32, (rows, targets.shape[1]), 0) + first_column
    total = jnp.zeros(row.shape, F32)
    for point in range(POINTS):
        total += jnp.where(row == targets[point : point + 1], weights[point : point + 1], 0.0)
    return split(total)


def diffuse(inverse, field, out, cols):
    variables = field.shape[1]
    wide = jnp.concatenate([field[:, v, :] for v in range(variables)], axis=1)
    result = dot3(split(inverse.T), split(wide), ((1,), (0,)))
    for v in range(variables):
        out[:, v, cols] = result[:, v * BCOLS : (v + 1) * BCOLS]


def rows_of(value):
    return value.reshape(value.shape[0] * value.shape[1], value.shape[2])


def spread(diffused, matrix):
    levels, variables, _ = diffused.shape
    sums = dot3(split(rows_of(diffused)), matrix, ((1,), (1,)))
    return sums.reshape(levels, variables, sums.shape[1])


def fetch(sems, pairs):
    copies = [pltpu.make_async_copy(source, target, sems.at[i]) for i, (source, target) in enumerate(pairs)]
    for copy in copies:
        copy.start()
    return copies


def call(kernel, operands, in_specs, outs, out_specs, scratch, flops, name):
    return pl.pallas_call(
        kernel,
        out_shape=outs,
        in_specs=in_specs,
        out_specs=out_specs,
        scratch_shapes=scratch,
        compiler_params=pltpu.CompilerParams(vmem_limit_bytes=VMEM_LIMIT),
        cost_estimate=pl.CostEstimate(flops=flops, bytes_accessed=1_000_000, transcendentals=0),
        name=name,
    )(*operands)


def first_edge_kernel(step, all_blocks, *refs):
    fields, inverses, routes, points, weights, to_near, to_far = refs[:7]
    field, inverse, route, point, weight, tall, sems = refs[7:]
    block_count = inverses.shape[2]
    near, far, target_near, target_far = z_blocks(block_count)
    copies = fetch(
        sems,
        [
            (routes, route),
            (points.at[step], point),
            (weights.at[step], weight),
            (inverses.at[step], inverse),
            (fields.at[:, :, lanes(near)], field.at[0]),
            (fields.at[:, :, lanes(far)], field.at[1]),
        ],
    )
    for copy in copies[:3]:
        copy.wait()
    matrices = []
    for block in (near, far):
        targets = target_columns(point[:, lanes(block)], route, step, block, block_count, all_blocks)
        halves = [
            spread_matrix(targets, weight[:, lanes(block)], target * BCOLS) for target in (target_near, target_far)
        ]
        matrices.append([jnp.concatenate(parts, axis=0) for parts in zip(*halves)])
    matrix = [jnp.concatenate(parts, axis=1) for parts in zip(*matrices)]
    for copy in copies[3:]:
        copy.wait()
    for j, block in enumerate((near, far)):
        diffuse(inverse[:, block, :], field.at[j], tall, slice(j * BCOLS, (j + 1) * BCOLS))
    sums = spread(tall[...], matrix)
    to_near[...] = sums[:, :, :BCOLS]
    to_far[...] = sums[:, :, BCOLS:]


def tables_scratch(inverses, routes):
    levels, block_count = inverses.shape[1:3]
    return [
        pltpu.VMEM((levels, block_count, levels), F32),
        pltpu.SMEM(routes.shape, jnp.int32),
        pltpu.VMEM((POINTS, block_count * BCOLS), jnp.int32),
        pltpu.VMEM((POINTS, block_count * BCOLS), F32),
    ]


def first_edge(step, all_blocks, fields, tables):
    levels, variables, _ = fields.shape
    one = jax.ShapeDtypeStruct((levels, variables, BCOLS), F32)
    return call(
        functools.partial(first_edge_kernel, step, all_blocks),
        (fields, *tables),
        [HBM] * 5,
        (one, one),
        (VMEM, VMEM),
        [
            pltpu.VMEM((2, levels, variables, BCOLS), F32),
            *tables_scratch(*tables[:2]),
            pltpu.VMEM((levels, variables, 2 * BCOLS), F32),
            pltpu.SemaphoreType.DMA((6,)),
        ],
        400_000_000,
        f"first_edge_step{step}",
    )


def near_edge_kernel(step, all_blocks, *refs):
    own, halo, inverses, routes, points, weights, to_far, to_near = refs[:8]
    inverse, route, point, weight, field, tall, sems = refs[8:]
    block_count = inverses.shape[2]
    near, _, target_near, target_far = z_blocks(block_count)
    copies = fetch(
        sems, [(routes, route), (points.at[step], point), (weights.at[step], weight), (inverses.at[step], inverse)]
    )
    field[...] = own[:, :, lanes(near)] + halo[...]
    for copy in copies:
        copy.wait()
    targets = target_columns(point[:, lanes(near)], route, step, near, block_count, all_blocks)
    halves = [spread_matrix(targets, weight[:, lanes(near)], target * BCOLS) for target in (target_far, target_near)]
    matrix = [jnp.concatenate(parts, axis=0) for parts in zip(*halves)]
    diffuse(inverse[:, near, :], field, tall, slice(0, BCOLS))
    sums = spread(tall[...], matrix)
    to_far[...] = sums[:, :, :BCOLS]
    to_near[...] = sums[:, :, BCOLS:]


def near_edge(step, all_blocks, own, halo, tables):
    one = jax.ShapeDtypeStruct(halo.shape, F32)
    return call(
        functools.partial(near_edge_kernel, step, all_blocks),
        (own, halo, *tables),
        [VMEM, VMEM] + [HBM] * 4,
        (one, one),
        (VMEM, VMEM),
        [
            *tables_scratch(*tables[:2]),
            pltpu.VMEM(halo.shape, F32),
            pltpu.VMEM(halo.shape, F32),
            pltpu.SemaphoreType.DMA((4,)),
        ],
        300_000_000,
        f"near_edge_step{step}",
    )


def far_edge_kernel(step, all_blocks, *refs):
    own, halo, partial, inverses, routes, points, weights, to_near = refs[:8]
    inverse, route, point, weight, field, tall, sems = refs[8:]
    block_count = inverses.shape[2]
    _, far, target_near, _ = z_blocks(block_count)
    copies = fetch(
        sems, [(routes, route), (points.at[step], point), (weights.at[step], weight), (inverses.at[step], inverse)]
    )
    field[...] = own[:, :, lanes(far)] + halo[...]
    for copy in copies:
        copy.wait()
    targets = target_columns(point[:, lanes(far)], route, step, far, block_count, all_blocks)
    matrix = spread_matrix(targets, weight[:, lanes(far)], target_near * BCOLS)
    diffuse(inverse[:, far, :], field, tall, slice(0, BCOLS))
    to_near[...] = partial[...] + spread(tall[...], matrix)


def far_edge(step, all_blocks, own, halo, partial, tables):
    return call(
        functools.partial(far_edge_kernel, step, all_blocks),
        (own, halo, partial, *tables),
        [VMEM] * 3 + [HBM] * 4,
        jax.ShapeDtypeStruct(halo.shape, F32),
        VMEM,
        [
            *tables_scratch(*tables[:2]),
            pltpu.VMEM(halo.shape, F32),
            pltpu.VMEM(halo.shape, F32),
            pltpu.SemaphoreType.DMA((4,)),
        ],
        300_000_000,
        f"far_edge_step{step}",
    )


def rest_kernel(step, all_blocks, has_halo, *refs):
    fields, inverses, routes, points, weights, _ = refs[:6]
    halos = refs[6 : 6 + 3 * has_halo]
    refs = refs[6 + 3 * has_halo :]
    own, core_out = refs[:2]
    mid = refs[2] if has_halo else None
    inverse, route, point, weight, field, tall, sems = refs[2 + has_halo :]
    block_count = inverses.shape[2]
    near, far, _, _ = z_blocks(block_count)
    core_first, core_target = core_side(block_count)
    pairs = [(routes, route), (points.at[step], point), (weights.at[step], weight), (inverses.at[step], inverse)]
    if not has_halo:
        pairs.append((fields, field))
    copies = fetch(sems, pairs)
    if has_halo:
        core_in, near_in, far_in = halos
        field[:, :, lanes(core_first, REACH)] = fields[:, :, lanes(core_first, REACH)] + core_in[...]
        field[:, :, lanes(near)] = fields[:, :, lanes(near)] + near_in[...]
        field[:, :, lanes(far)] = fields[:, :, lanes(far)] + far_in[...]
        mid_copy = pltpu.make_async_copy(field, mid, sems.at[5])
        mid_copy.start()
    for copy in copies[:3]:
        copy.wait()
    for j in range(block_count):
        cols = slice(j * BCOLS, (j + 1) * BCOLS)
        point[:, cols] = target_columns(point[:, cols], route, step, j, block_count, all_blocks)
    side = lanes(core_first, REACH)
    outer = spread_matrix(point[:, side], weight[:, side], core_target * BCOLS, REACH * BCOLS)
    inner = spread_matrix(point[...], weight[...], 0, block_count * BCOLS)
    for copy in copies[3:]:
        copy.wait()
    for j in range(block_count):
        cols = slice(j * BCOLS, (j + 1) * BCOLS)
        diffuse(inverse[:, j, :], field.at[:, :, cols], tall, cols)
    core_out[...] = spread(tall[:, :, side], outer)
    own[...] = spread(tall[...], inner)
    if has_halo:
        mid_copy.wait()


def rest(step, all_blocks, fields, tables, behind, halos=()):
    levels, variables, _ = fields.shape
    has_halo = bool(halos)
    whole = jax.ShapeDtypeStruct(fields.shape, F32)
    side = jax.ShapeDtypeStruct((levels, variables, REACH * BCOLS), F32)
    return call(
        functools.partial(rest_kernel, step, all_blocks, has_halo),
        (fields, *tables, behind, *halos),
        [VMEM if has_halo else HBM] + [HBM] * 4 + [ANY] + [VMEM] * len(halos),
        (whole, side) + ((whole,) if has_halo else ()),
        (VMEM, VMEM) + ((HBM,) if has_halo else ()),
        [
            *tables_scratch(*tables[:2]),
            pltpu.VMEM(fields.shape, F32),
            pltpu.VMEM(fields.shape, F32),
            pltpu.SemaphoreType.DMA((6,)),
        ],
        2_000_000_000,
        f"rest_step{step}",
    )


def squares(value):
    return jnp.sum(rows_of(value * value), axis=0, keepdims=True)


def most_kernel(own, core_in, far_in, start, lane_sums):
    block_count = own.shape[2] // BCOLS
    near, far, _, _ = z_blocks(block_count)
    side = lanes(core_side(block_count)[0], REACH)
    core = own[:, :, side] + core_in[...]
    behind = own[:, :, lanes(far)] + far_in[...]
    start[:, :, side] = core
    start[:, :, lanes(far)] = behind
    start[:, :, lanes(near)] = own[:, :, lanes(near)]
    core = squares(core)
    lane_sums[...] = core[:, :BCOLS] + core[:, BCOLS:] + squares(behind)


def most(own, core_in, far_in):
    return call(
        most_kernel,
        (own, core_in, far_in),
        [VMEM] * 3,
        (jax.ShapeDtypeStruct(own.shape, F32), jax.ShapeDtypeStruct((1, BCOLS), F32)),
        (VMEM, VMEM),
        [],
        1_000_000,
        "squares_of_most_blocks",
    )


def last_kernel(start, near_in, lane_sums, shares):
    near = z_blocks(start.shape[2] // BCOLS)[0]
    sums = lane_sums[...] + squares(start[:, :, lanes(near)] + near_in[...])
    shares[...] = jnp.broadcast_to(sums, shares.shape)


def last(count, start, near_in, lane_sums):
    return call(
        last_kernel,
        (start, near_in, lane_sums),
        [VMEM] * 3,
        jax.ShapeDtypeStruct((count, BCOLS), F32),
        VMEM,
        [],
        1_000_000,
        "squares_of_last_block",
    )


def scale_kernel(cells, start, near_in, shares, out, held, sems):
    block_count = start.shape[2] // BCOLS
    near = z_blocks(block_count)[0]
    energy = jnp.sum(shares[...]) / cells
    root = jnp.sqrt(jnp.full((1, 1, 1), energy + eps_energy, F32))
    copies = []
    for j in range(block_count):
        cols = slice(j * BCOLS, (j + 1) * BCOLS)
        held[:, :, cols] = (start[:, :, cols] + jnp.where(near == j, near_in[...], 0.0)) / root
        copies.append(pltpu.make_async_copy(held.at[:, :, cols], out.at[:, :, cols], sems.at[j]))
        copies[-1].start()
    for copy in copies:
        copy.wait()


def scale(start, near_in, shares, cells):
    return call(
        functools.partial(scale_kernel, cells),
        (start, near_in, shares),
        [VMEM] * 3,
        jax.ShapeDtypeStruct(start.shape, F32),
        HBM,
        [pltpu.VMEM(start.shape, F32), pltpu.SemaphoreType.DMA((start.shape[2] // BCOLS,))],
        1_000_000,
        "scale_start",
    )


def core_exchange(value):
    count = lax.axis_size("col")
    return lax.ppermute(value, "col", [(i, i ^ 1) for i in range(count)])


def z_exchange(value):
    count = lax.axis_size("col")
    pairs = [(i, (i + 1) % count if i % 2 else (i - 1) % count) for i in range(count)]
    return lax.ppermute(value, "col", pairs)


def shards(adj_final, inverses, dep_lists, dep_points, weights):
    count = lax.axis_size("col")
    all_blocks = count * inverses.shape[1]
    fields = jnp.transpose(adj_final, (1, 0, 2))
    tables = (jnp.transpose(inverses, (0, 2, 1, 3)), dep_lists, dep_points, weights)

    to_near, to_far = first_edge(1, all_blocks, fields, tables)
    near_in = z_exchange(to_near)
    far_in = z_exchange(to_far)
    own, core_out = rest(1, all_blocks, fields, tables, to_near)
    core_in = core_exchange(core_out)

    to_far, partial = near_edge(0, all_blocks, own, near_in, tables)
    next_far_in = z_exchange(to_far)
    to_near = far_edge(0, all_blocks, own, far_in, partial, tables)
    next_near_in = z_exchange(to_near)
    own, core_out, mid = rest(0, all_blocks, own, tables, to_near, (core_in, near_in, far_in))
    core_in = core_exchange(core_out)

    start, lane_sums = most(own, core_in, next_far_in)
    shares = last(count, start, next_near_in, lane_sums)
    shares = lax.all_to_all(shares, "col", 0, 0, tiled=True)
    lanczos = scale(start, next_near_in, shares, adj_final.size * count)
    return jnp.transpose(mid, (1, 0, 2)), jnp.transpose(lanczos, (1, 0, 2))


def solution(mesh):
    in_specs = (
        P("mem", None, "col"),
        P("mem", "col", None, None),
        P("mem", "col", None),
        P("mem", None, "col"),
        P("mem", None, "col"),
    )
    out_specs = (P("mem", None, "col"), P("mem", None, "col"))
    return jax.shard_map(shards, mesh=mesh, in_specs=in_specs, out_specs=out_specs, check_vma=False)
```

```python
import functools

import jax
import jax.numpy as jnp
from jax import lax
from jax.experimental import pallas as pl
from jax.experimental.pallas import tpu as pltpu
from jax.sharding import PartitionSpec as P

BCOLS = 128
REACH = 2
SLOTS = 5
POINTS = 4
STEPS = 2
VMEM_LIMIT = 32 * 1024 * 1024
FIRST_LIMIT = 62 * 1024 * 1024

eps_energy = 1e-06

F32 = jnp.float32
BF16 = jnp.bfloat16
ANY = pl.BlockSpec(memory_space=pl.ANY)
HBM = pl.BlockSpec(memory_space=pltpu.HBM)
VMEM = pl.BlockSpec(memory_space=pltpu.VMEM)


def z_blocks(block_count):
    follows = lax.rem(lax.axis_index("col"), 2)
    near = follows * (block_count - 1)
    away = 2 * follows - 1
    return near, near - away, near + away, near + 2 * away


def core_side(block_count):
    follows = 1 - lax.rem(lax.axis_index("col"), 2)
    return follows * (block_count - REACH), follows * (block_count + REACH) - REACH


def lanes(block, count=1):
    return pl.ds(pl.multiple_of(block * BCOLS, BCOLS), count * BCOLS)


def split(value):
    high = value.astype(BF16)
    return high, (value - high.astype(F32)).astype(BF16)


def dot3(left, right, dims):
    def one(a, b):
        return lax.dot_general(a, b, (dims, ((), ())), preferred_element_type=F32)

    return one(left[0], right[0]) + (one(left[0], right[1]) + one(left[1], right[0]))


def target_columns(points, routes, step, block, block_count, all_blocks):
    slots = points // BCOLS
    here = lax.axis_index("col") * block_count + block
    found = jnp.zeros_like(points)
    for slot in range(SLOTS):
        offset = lax.rem(routes[step, block, slot] - here + REACH + all_blocks, all_blocks) - REACH
        found = jnp.where(slots == slot, (block + offset) * BCOLS, found)
    return found + points % BCOLS


def spread_matrix(targets, weights, first_column, rows=BCOLS):
    row = lax.broadcasted_iota(jnp.int32, (rows, targets.shape[1]), 0) + first_column
    total = jnp.zeros(row.shape, F32)
    for point in range(POINTS):
        total += jnp.where(row == targets[point : point + 1], weights[point : point + 1], 0.0)
    return split(total)


def diffuse(inverse, field, out, cols):
    variables = field.shape[1]
    wide = jnp.concatenate([field[:, v, :] for v in range(variables)], axis=1)
    result = dot3(split(inverse.T), split(wide), ((1,), (0,)))
    for v in range(variables):
        out[:, v, cols] = result[:, v * BCOLS : (v + 1) * BCOLS]


def rows_of(value):
    return value.reshape(value.shape[0] * value.shape[1], value.shape[2])


def spread(diffused, matrix):
    levels, variables, _ = diffused.shape
    sums = dot3(split(rows_of(diffused)), matrix, ((1,), (1,)))
    return sums.reshape(levels, variables, sums.shape[1])


def fetch(sems, pairs):
    copies = [pltpu.make_async_copy(source, target, sems.at[i]) for i, (source, target) in enumerate(pairs)]
    for copy in copies:
        copy.start()
    return copies


def call(kernel, operands, in_specs, outs, out_specs, scratch, flops, name, limit=VMEM_LIMIT):
    return pl.pallas_call(
        kernel,
        out_shape=outs,
        in_specs=in_specs,
        out_specs=out_specs,
        scratch_shapes=scratch,
        compiler_params=pltpu.CompilerParams(vmem_limit_bytes=limit),
        cost_estimate=pl.CostEstimate(flops=flops, bytes_accessed=1_000_000, transcendentals=0),
        name=name,
    )(*operands)


def first_edge_kernel(step, all_blocks, *refs):
    fields, inverses, routes, points, weights, to_near, to_far, to_core = refs[:8]
    field, inverse, route, point, weight, tall, sems = refs[8:]
    block_count = inverses.shape[2]
    near, far, target_near, target_far = z_blocks(block_count)
    first, first_target = core_side(block_count)
    copies = fetch(
        sems,
        [
            (routes, route),
            (points.at[step], point),
            (weights.at[step], weight),
            (inverses.at[step], inverse),
            (fields.at[:, :, lanes(near)], field.at[0]),
            (fields.at[:, :, lanes(far)], field.at[1]),
            (fields.at[:, :, lanes(first)], field.at[2]),
            (fields.at[:, :, lanes(first + 1)], field.at[3]),
        ],
    )
    for copy in copies[:3]:
        copy.wait()
    def matrix_of(blocks, first_columns):
        parts = []
        for block in blocks:
            targets = target_columns(point[:, lanes(block)], route, step, block, block_count, all_blocks)
            halves = [spread_matrix(targets, weight[:, lanes(block)], column) for column in first_columns]
            parts.append([jnp.concatenate(half, axis=0) for half in zip(*halves)])
        return [jnp.concatenate(part, axis=1) for part in zip(*parts)]

    z_matrix = matrix_of((near, far), (target_near * BCOLS, target_far * BCOLS))
    core_matrix = matrix_of((first, first + 1), (first_target * BCOLS, (first_target + 1) * BCOLS))
    for copy in copies[3:]:
        copy.wait()
    for j, block in enumerate((near, far, first, first + 1)):
        diffuse(inverse[:, block, :], field.at[j], tall, slice(j * BCOLS, (j + 1) * BCOLS))
    sums = spread(tall[:, :, : 2 * BCOLS], z_matrix)
    to_near[...] = sums[:, :, :BCOLS]
    to_far[...] = sums[:, :, BCOLS:]
    to_core[...] = spread(tall[:, :, 2 * BCOLS :], core_matrix)


def tables_scratch(inverses, routes):
    levels, block_count = inverses.shape[1:3]
    return [
        pltpu.VMEM((levels, block_count, levels), F32),
        pltpu.SMEM(routes.shape, jnp.int32),
        pltpu.VMEM((POINTS, block_count * BCOLS), jnp.int32),
        pltpu.VMEM((POINTS, block_count * BCOLS), F32),
    ]


def first_edge(step, all_blocks, fields, tables):
    levels, variables, _ = fields.shape
    one = jax.ShapeDtypeStruct((levels, variables, BCOLS), F32)
    return call(
        functools.partial(first_edge_kernel, step, all_blocks),
        (fields, *tables),
        [HBM] * 5,
        (one, one, jax.ShapeDtypeStruct((levels, variables, REACH * BCOLS), F32)),
        (VMEM, VMEM, VMEM),
        [
            pltpu.VMEM((4, levels, variables, BCOLS), F32),
            *tables_scratch(*tables[:2]),
            pltpu.VMEM((levels, variables, 4 * BCOLS), F32),
            pltpu.SemaphoreType.DMA((8,)),
        ],
        400_000_000,
        f"first_edge_step{step}",
        FIRST_LIMIT,
    )


def near_edge_kernel(step, all_blocks, *refs):
    own, halo, inverses, routes, points, weights, to_far, to_near = refs[:8]
    inverse, route, point, weight, field, tall, sems = refs[8:]
    block_count = inverses.shape[2]
    near, _, target_near, target_far = z_blocks(block_count)
    copies = fetch(
        sems, [(routes, route), (points.at[step], point), (weights.at[step], weight), (inverses.at[step], inverse)]
    )
    field[...] = own[:, :, lanes(near)] + halo[...]
    for copy in copies:
        copy.wait()
    targets = target_columns(point[:, lanes(near)], route, step, near, block_count, all_blocks)
    halves = [spread_matrix(targets, weight[:, lanes(near)], target * BCOLS) for target in (target_far, target_near)]
    matrix = [jnp.concatenate(parts, axis=0) for parts in zip(*halves)]
    diffuse(inverse[:, near, :], field, tall, slice(0, BCOLS))
    sums = spread(tall[...], matrix)
    to_far[...] = sums[:, :, :BCOLS]
    to_near[...] = sums[:, :, BCOLS:]


def near_edge(step, all_blocks, own, halo, tables):
    one = jax.ShapeDtypeStruct(halo.shape, F32)
    return call(
        functools.partial(near_edge_kernel, step, all_blocks),
        (own, halo, *tables),
        [VMEM, VMEM] + [HBM] * 4,
        (one, one),
        (VMEM, VMEM),
        [
            *tables_scratch(*tables[:2]),
            pltpu.VMEM(halo.shape, F32),
            pltpu.VMEM(halo.shape, F32),
            pltpu.SemaphoreType.DMA((4,)),
        ],
        300_000_000,
        f"near_edge_step{step}",
    )


def far_edge_kernel(step, all_blocks, *refs):
    own, halo, partial, inverses, routes, points, weights, to_near = refs[:8]
    inverse, route, point, weight, field, tall, sems = refs[8:]
    block_count = inverses.shape[2]
    _, far, target_near, _ = z_blocks(block_count)
    copies = fetch(
        sems, [(routes, route), (points.at[step], point), (weights.at[step], weight), (inverses.at[step], inverse)]
    )
    field[...] = own[:, :, lanes(far)] + halo[...]
    for copy in copies:
        copy.wait()
    targets = target_columns(point[:, lanes(far)], route, step, far, block_count, all_blocks)
    matrix = spread_matrix(targets, weight[:, lanes(far)], target_near * BCOLS)
    diffuse(inverse[:, far, :], field, tall, slice(0, BCOLS))
    to_near[...] = partial[...] + spread(tall[...], matrix)


def far_edge(step, all_blocks, own, halo, partial, tables):
    return call(
        functools.partial(far_edge_kernel, step, all_blocks),
        (own, halo, partial, *tables),
        [VMEM] * 3 + [HBM] * 4,
        jax.ShapeDtypeStruct(halo.shape, F32),
        VMEM,
        [
            *tables_scratch(*tables[:2]),
            pltpu.VMEM(halo.shape, F32),
            pltpu.VMEM(halo.shape, F32),
            pltpu.SemaphoreType.DMA((4,)),
        ],
        300_000_000,
        f"far_edge_step{step}",
    )


def inner_kernel(step, all_blocks, fields, inverses, routes, points, weights, core_in, own, *scratch):
    inverse, route, point, weight, field, tall, sems = scratch
    block_count = inverses.shape[2]
    copies = fetch(
        sems,
        [
            (routes, route),
            (points.at[step], point),
            (weights.at[step], weight),
            (inverses.at[step], inverse),
            (fields, field),
        ],
    )
    for copy in copies[:3]:
        copy.wait()
    diffuse_and_spread(step, all_blocks, copies[3:], inverse, route, point, weight, field, tall, own)
    side = lanes(core_side(block_count)[0], REACH)
    own[:, :, side] += core_in[...]


def diffuse_and_spread(step, all_blocks, copies, inverse, route, point, weight, field, tall, own):
    block_count = inverse.shape[1]
    for j in range(block_count):
        cols = slice(j * BCOLS, (j + 1) * BCOLS)
        point[:, cols] = target_columns(point[:, cols], route, step, j, block_count, all_blocks)
    matrix = spread_matrix(point[...], weight[...], 0, block_count * BCOLS)
    for copy in copies:
        copy.wait()
    for j in range(block_count):
        cols = slice(j * BCOLS, (j + 1) * BCOLS)
        diffuse(inverse[:, j, :], field.at[:, :, cols], tall, cols)
    own[...] = spread(tall[...], matrix)


def inner(step, all_blocks, fields, tables, core_in):
    return call(
        functools.partial(inner_kernel, step, all_blocks),
        (fields, *tables, core_in),
        [HBM] * 5 + [VMEM],
        jax.ShapeDtypeStruct(fields.shape, F32),
        VMEM,
        [
            *tables_scratch(*tables[:2]),
            pltpu.VMEM(fields.shape, F32),
            pltpu.VMEM(fields.shape, F32),
            pltpu.SemaphoreType.DMA((5,)),
        ],
        2_000_000_000,
        f"inner_step{step}",
    )


def core_edge_kernel(step, all_blocks, fields, inverses, routes, points, weights, to_core, *scratch):
    inverse, route, point, weight, tall, sems = scratch
    block_count = inverses.shape[2]
    first, first_target = core_side(block_count)
    copies = fetch(
        sems, [(routes, route), (points.at[step], point), (weights.at[step], weight), (inverses.at[step], inverse)]
    )
    for copy in copies:
        copy.wait()
    parts = []
    for j in range(REACH):
        block = first + j
        targets = target_columns(point[:, lanes(block)], route, step, block, block_count, all_blocks)
        parts.append(spread_matrix(targets, weight[:, lanes(block)], first_target * BCOLS, REACH * BCOLS))
        cols = slice(j * BCOLS, (j + 1) * BCOLS)
        diffuse(inverse[:, block, :], fields.at[:, :, lanes(block)], tall, cols)
    matrix = [jnp.concatenate(part, axis=1) for part in zip(*parts)]
    to_core[...] = spread(tall[...], matrix)


def core_edge(step, all_blocks, fields, tables):
    levels, variables, _ = fields.shape
    side = (levels, variables, REACH * BCOLS)
    return call(
        functools.partial(core_edge_kernel, step, all_blocks),
        (fields, *tables),
        [VMEM] + [HBM] * 4,
        jax.ShapeDtypeStruct(side, F32),
        VMEM,
        [*tables_scratch(*tables[:2]), pltpu.VMEM(side, F32), pltpu.SemaphoreType.DMA((4,))],
        400_000_000,
        f"core_edge_step{step}",
    )


def outer_kernel(step, all_blocks, fields, near_in, far_in, inverses, routes, points, weights, _, own, mid, *scratch):
    inverse, route, point, weight, field, tall, sems = scratch
    block_count = inverses.shape[2]
    near, far, _, _ = z_blocks(block_count)
    first = core_side(block_count)[0]
    copies = fetch(
        sems, [(routes, route), (points.at[step], point), (weights.at[step], weight), (inverses.at[step], inverse)]
    )
    field[:, :, lanes(first, REACH)] = fields[:, :, lanes(first, REACH)]
    field[:, :, lanes(near)] = fields[:, :, lanes(near)] + near_in[...]
    field[:, :, lanes(far)] = fields[:, :, lanes(far)] + far_in[...]
    mid_copy = pltpu.make_async_copy(field, mid, sems.at[4])
    mid_copy.start()
    for copy in copies[:3]:
        copy.wait()
    diffuse_and_spread(step, all_blocks, copies[3:], inverse, route, point, weight, field, tall, own)
    mid_copy.wait()


def outer(step, all_blocks, fields, near_in, far_in, tables, behind):
    whole = jax.ShapeDtypeStruct(fields.shape, F32)
    return call(
        functools.partial(outer_kernel, step, all_blocks),
        (fields, near_in, far_in, *tables, behind),
        [VMEM] * 3 + [HBM] * 4 + [ANY],
        (whole, whole),
        (VMEM, HBM),
        [
            *tables_scratch(*tables[:2]),
            pltpu.VMEM(fields.shape, F32),
            pltpu.VMEM(fields.shape, F32),
            pltpu.SemaphoreType.DMA((5,)),
        ],
        2_000_000_000,
        f"outer_step{step}",
    )


def squares(value):
    return jnp.sum(rows_of(value * value), axis=0, keepdims=True)


def most_kernel(own, core_in, far_in, start, lane_sums):
    block_count = own.shape[2] // BCOLS
    near, far, _, _ = z_blocks(block_count)
    side = lanes(core_side(block_count)[0], REACH)
    core = own[:, :, side] + core_in[...]
    behind = own[:, :, lanes(far)] + far_in[...]
    start[:, :, side] = core
    start[:, :, lanes(far)] = behind
    start[:, :, lanes(near)] = own[:, :, lanes(near)]
    core = squares(core)
    lane_sums[...] = core[:, :BCOLS] + core[:, BCOLS:] + squares(behind)


def most(own, core_in, far_in):
    return call(
        most_kernel,
        (own, core_in, far_in),
        [VMEM] * 3,
        (jax.ShapeDtypeStruct(own.shape, F32), jax.ShapeDtypeStruct((1, BCOLS), F32)),
        (VMEM, VMEM),
        [],
        1_000_000,
        "squares_of_most_blocks",
    )


def last_kernel(start, near_in, lane_sums, shares):
    near = z_blocks(start.shape[2] // BCOLS)[0]
    sums = lane_sums[...] + squares(start[:, :, lanes(near)] + near_in[...])
    shares[...] = jnp.broadcast_to(sums, shares.shape)


def last(count, start, near_in, lane_sums):
    return call(
        last_kernel,
        (start, near_in, lane_sums),
        [VMEM] * 3,
        jax.ShapeDtypeStruct((count, BCOLS), F32),
        VMEM,
        [],
        1_000_000,
        "squares_of_last_block",
    )


def scale_kernel(cells, start, near_in, shares, out, held, sems):
    block_count = start.shape[2] // BCOLS
    near = z_blocks(block_count)[0]
    energy = jnp.sum(shares[...]) / cells
    root = jnp.sqrt(jnp.full((1, 1, 1), energy + eps_energy, F32))
    copies = []
    for j in range(block_count):
        cols = slice(j * BCOLS, (j + 1) * BCOLS)
        held[:, :, cols] = (start[:, :, cols] + jnp.where(near == j, near_in[...], 0.0)) / root
        copies.append(pltpu.make_async_copy(held.at[:, :, cols], out.at[:, :, cols], sems.at[j]))
        copies[-1].start()
    for copy in copies:
        copy.wait()


def scale(start, near_in, shares, cells):
    return call(
        functools.partial(scale_kernel, cells),
        (start, near_in, shares),
        [VMEM] * 3,
        jax.ShapeDtypeStruct(start.shape, F32),
        HBM,
        [pltpu.VMEM(start.shape, F32), pltpu.SemaphoreType.DMA((start.shape[2] // BCOLS,))],
        1_000_000,
        "scale_start",
    )


def core_exchange(value):
    count = lax.axis_size("col")
    return lax.ppermute(value, "col", [(i, i ^ 1) for i in range(count)])


def z_exchange(value):
    count = lax.axis_size("col")
    pairs = [(i, (i + 1) % count if i % 2 else (i - 1) % count) for i in range(count)]
    return lax.ppermute(value, "col", pairs)


def shards(adj_final, inverses, dep_lists, dep_points, weights):
    count = lax.axis_size("col")
    all_blocks = count * inverses.shape[1]
    fields = jnp.transpose(adj_final, (1, 0, 2))
    tables = (jnp.transpose(inverses, (0, 2, 1, 3)), dep_lists, dep_points, weights)

    to_near, to_far, to_core = first_edge(1, all_blocks, fields, tables)
    near_in = z_exchange(to_near)
    far_in = z_exchange(to_far)
    own = inner(1, all_blocks, fields, tables, core_exchange(to_core))

    next_core_in = core_exchange(core_edge(0, all_blocks, own, tables))
    to_far, partial = near_edge(0, all_blocks, own, near_in, tables)
    next_far_in = z_exchange(to_far)
    to_near = far_edge(0, all_blocks, own, far_in, partial, tables)
    next_near_in = z_exchange(to_near)
    own, mid = outer(0, all_blocks, own, near_in, far_in, tables, to_near)

    start, lane_sums = most(own, next_core_in, next_far_in)
    shares = last(count, start, next_near_in, lane_sums)
    shares = lax.all_to_all(shares, "col", 0, 0, tiled=True)
    lanczos = scale(start, next_near_in, shares, adj_final.size * count)
    return jnp.transpose(mid, (1, 0, 2)), jnp.transpose(lanczos, (1, 0, 2))


def solution(mesh):
    in_specs = (
        P("mem", None, "col"),
        P("mem", "col", None, None),
        P("mem", "col", None),
        P("mem", None, "col"),
        P("mem", None, "col"),
    )
    out_specs = (P("mem", None, "col"), P("mem", None, "col"))
    return jax.shard_map(shards, mesh=mesh, in_specs=in_specs, out_specs=out_specs, check_vma=False)
```

```python
import functools

import jax
import jax.numpy as jnp
from jax import lax
from jax.experimental import pallas as pl
from jax.experimental.pallas import tpu as pltpu
from jax.sharding import PartitionSpec as P

BCOLS = 128
REACH = 2
SLOTS = 5
POINTS = 4
STEPS = 2
VMEM_LIMIT = 32 * 1024 * 1024
NOWHERE = -(1 << 14)

eps_energy = 1e-06

F32 = jnp.float32
BF16 = jnp.bfloat16
HBM = pl.BlockSpec(memory_space=pltpu.HBM)
VMEM = pl.BlockSpec(memory_space=pltpu.VMEM)


def z_blocks(block_count):
    follows = lax.rem(lax.axis_index("col"), 2)
    near = follows * (block_count - 1)
    away = 2 * follows - 1
    return near, near - away, near + away, near + 2 * away


def core_side(block_count):
    follows = 1 - lax.rem(lax.axis_index("col"), 2)
    return follows * (block_count - REACH), follows * (block_count + REACH) - REACH


def lanes(block, count=1):
    return pl.ds(pl.multiple_of(block * BCOLS, BCOLS), count * BCOLS)


def split(value):
    high = value.astype(BF16)
    return high, (value - high.astype(F32)).astype(BF16)


def target_columns(points, routes, step, block, block_count, all_blocks):
    slots = points // BCOLS
    here = lax.axis_index("col") * block_count + block
    found = jnp.zeros_like(points)
    for slot in range(SLOTS):
        offset = lax.rem(routes[step, block, slot] - here + REACH + all_blocks, all_blocks) - REACH
        found = jnp.where(slots == slot, (block + offset) * BCOLS, found)
    return found + points % BCOLS


def merge_points(targets, weights):
    targets = [targets[p : p + 1] for p in range(POINTS)]
    weights = [weights[p : p + 1] for p in range(POINTS)]
    for point in range(1, POINTS):
        for earlier in range(point):
            same = targets[point] == targets[earlier]
            weights[earlier] = weights[earlier] + jnp.where(same, weights[point], 0.0)
            targets[point] = jnp.where(same, NOWHERE, targets[point])
    return jnp.concatenate(targets, axis=0), jnp.concatenate(weights, axis=0)


def spread_matrix(targets, weights, first_column, rows=BCOLS):
    row = lax.broadcasted_iota(jnp.int32, (rows, targets.shape[1]), 0) + first_column
    total = jnp.zeros(row.shape, F32)
    for point in range(POINTS):
        total = jnp.where(row == targets[point : point + 1], weights[point : point + 1], total)
    return split(total)


def product(left, right, dims):
    return lax.dot_general(left, right, (dims, ((), ())), preferred_element_type=F32)


def diffuse(inverse, field, out, cols):
    variables = field.shape[1]
    wide = split(jnp.concatenate([field[:, v, :] for v in range(variables)], axis=1))
    turned = split(inverse.T)
    dims = ((1,), (0,))
    result = product(turned[0], wide[0], dims) + (
        product(turned[0], wide[1], dims) + product(turned[1], wide[0], dims)
    )
    for v in range(variables):
        out[:, v, cols] = result[:, v * BCOLS : (v + 1) * BCOLS]


def rows_of(value):
    return value.reshape(value.shape[0] * value.shape[1], value.shape[2])


def spread(diffused, matrix):
    levels, variables, _ = diffused.shape
    high, low = split(rows_of(diffused))
    left = jnp.concatenate([high, low, high], axis=1)
    right = jnp.concatenate([matrix[0], matrix[0], matrix[1]], axis=1)
    sums = product(left, right, ((1,), (1,)))
    return sums.reshape(levels, variables, sums.shape[1])


def side_matrix(targets, weights, step, blocks, first_columns):
    parts = []
    for block in blocks:
        cols = lanes(block)
        halves = [spread_matrix(targets[step, :, cols], weights[step, :, cols], column) for column in first_columns]
        parts.append([jnp.concatenate(half, axis=0) for half in zip(*halves)])
    return [jnp.concatenate(part, axis=1) for part in zip(*parts)]


def call(kernel, operands, in_specs, outs, out_specs, scratch, flops, name, limit=VMEM_LIMIT):
    return pl.pallas_call(
        kernel,
        out_shape=outs,
        in_specs=in_specs,
        out_specs=out_specs,
        scratch_shapes=scratch,
        compiler_params=pltpu.CompilerParams(vmem_limit_bytes=limit),
        cost_estimate=pl.CostEstimate(flops=flops, bytes_accessed=1_000_000, transcendentals=0),
        name=name,
    )(*operands)


def start_copies(sems, pairs):
    copies = [pltpu.make_async_copy(source, target, sems.at[i]) for i, (source, target) in enumerate(pairs)]
    for copy in copies:
        copy.start()
    return copies


def first_kernel(
    step, all_blocks, fields, inverses, routes, points, weights,
    to_near, to_far, to_core, diffused, targets, merged, field, inverse, route, point, weight, tall, sems,
):
    block_count = inverses.shape[2]
    near, far, target_near, target_far = z_blocks(block_count)
    first, first_target = core_side(block_count)
    copies = start_copies(
        sems,
        [
            (routes, route),
            (points, point),
            (weights, weight),
            (inverses.at[step], inverse),
            (fields, field),
        ],
    )
    for copy in copies[:3]:
        copy.wait()
    for number in range(STEPS):
        for j in range(block_count):
            cols = slice(j * BCOLS, (j + 1) * BCOLS)
            found = target_columns(point[number, :, cols], route, number, j, block_count, all_blocks)
            targets[number, :, cols], merged[number, :, cols] = merge_points(found, weight[number, :, cols])
    z_matrix = side_matrix(targets, merged, step, (near, far), (target_near * BCOLS, target_far * BCOLS))
    core_columns = (first_target * BCOLS, (first_target + 1) * BCOLS)
    core_matrix = side_matrix(targets, merged, step, (first, first + 1), core_columns)
    for copy in copies[3:]:
        copy.wait()
    for j in range(block_count):
        cols = slice(j * BCOLS, (j + 1) * BCOLS)
        diffuse(inverse[:, j, :], field.at[:, :, cols], diffused, cols)
    tall[:, :, :BCOLS] = diffused[:, :, lanes(near)]
    tall[:, :, BCOLS:] = diffused[:, :, lanes(far)]
    sums = spread(tall[...], z_matrix)
    to_near[...] = sums[:, :, :BCOLS]
    to_far[...] = sums[:, :, BCOLS:]
    to_core[...] = spread(diffused[:, :, lanes(first, REACH)], core_matrix)


def shape(like, columns):
    return jax.ShapeDtypeStruct((like.shape[0], like.shape[1], columns), F32)


def first(step, all_blocks, fields, inverses, routes, points, weights):
    one, two, whole = (shape(fields, n) for n in (BCOLS, REACH * BCOLS, fields.shape[2]))
    return call(
        functools.partial(first_kernel, step, all_blocks),
        (fields, inverses, routes, points, weights),
        [HBM] * 5,
        (
            one,
            one,
            two,
            whole,
            jax.ShapeDtypeStruct(points.shape, jnp.int32),
            jax.ShapeDtypeStruct(weights.shape, F32),
        ),
        (VMEM,) * 6,
        [
            pltpu.VMEM(fields.shape, F32),
            pltpu.VMEM(inverses.shape[1:], F32),
            pltpu.SMEM(routes.shape, jnp.int32),
            pltpu.VMEM(points.shape, jnp.int32),
            pltpu.VMEM(weights.shape, F32),
            pltpu.VMEM(two.shape, F32),
            pltpu.SemaphoreType.DMA((5,)),
        ],
        400_000_000,
        f"first_step{step}",
    )


def inner_kernel(
    step, diffused, targets, weights, core_in, inverses, own, inverse, to_core, diffused_core, sems
):
    block_count = inverses.shape[2]
    side_first, first_target = core_side(block_count)
    (copy,) = start_copies(sems, [(inverses.at[step - 1], inverse)])
    matrix = spread_matrix(targets[step], weights[step], 0, own.shape[2])
    own[...] = spread(diffused[...], matrix)
    side = lanes(side_first, REACH)
    own[:, :, side] += core_in[...]
    columns = (first_target * BCOLS, (first_target + 1) * BCOLS)
    matrix = side_matrix(targets, weights, step - 1, (side_first, side_first + 1), columns)
    copy.wait()
    for j in range(REACH):
        cols = slice(j * BCOLS, (j + 1) * BCOLS)
        diffuse(inverse[:, side_first + j, :], own.at[:, :, lanes(side_first + j)], diffused_core, cols)
    to_core[...] = spread(diffused_core[...], matrix)


def inner(step, diffused, targets, weights, core_in, inverses):
    two = shape(diffused, REACH * BCOLS)
    return call(
        functools.partial(inner_kernel, step),
        (diffused, targets, weights, core_in, inverses),
        [VMEM] * 4 + [HBM],
        (shape(diffused, diffused.shape[2]), jax.ShapeDtypeStruct(inverses.shape[1:], F32), two, two),
        (VMEM,) * 4,
        [pltpu.SemaphoreType.DMA((1,))],
        2_000_000_000,
        f"inner_step{step}",
    )


def near_kernel(step, own, near_in, inverse, targets, weights, to_far, to_near, diffused, field):
    block_count = inverse.shape[1]
    near, _, target_near, target_far = z_blocks(block_count)
    cols = lanes(near)
    field[...] = own[:, :, cols] + near_in[...]
    diffuse(inverse[:, near, :], field, diffused, slice(0, BCOLS))
    halves = [
        spread_matrix(targets[step, :, cols], weights[step, :, cols], target * BCOLS)
        for target in (target_far, target_near)
    ]
    sums = spread(diffused[...], [jnp.concatenate(half, axis=0) for half in zip(*halves)])
    to_far[...] = sums[:, :, :BCOLS]
    to_near[...] = sums[:, :, BCOLS:]


def near(step, own, near_in, inverse, targets, weights):
    one = shape(own, BCOLS)
    return call(
        functools.partial(near_kernel, step),
        (own, near_in, inverse, targets, weights),
        [VMEM] * 5,
        (one, one, one),
        (VMEM,) * 3,
        [pltpu.VMEM(one.shape, F32)],
        300_000_000,
        f"near_step{step}",
    )


def far_kernel(step, own, far_in, partial, inverse, targets, weights, to_near, diffused, field):
    block_count = inverse.shape[1]
    _, far, target_near, _ = z_blocks(block_count)
    cols = lanes(far)
    field[...] = own[:, :, cols] + far_in[...]
    diffuse(inverse[:, far, :], field, diffused, slice(0, BCOLS))
    matrix = spread_matrix(targets[step, :, cols], weights[step, :, cols], target_near * BCOLS)
    to_near[...] = partial[...] + spread(diffused[...], matrix)


def far(step, own, far_in, partial, inverse, targets, weights):
    one = shape(own, BCOLS)
    return call(
        functools.partial(far_kernel, step),
        (own, far_in, partial, inverse, targets, weights),
        [VMEM] * 6,
        (one, one),
        (VMEM,) * 2,
        [pltpu.VMEM(one.shape, F32)],
        300_000_000,
        f"far_step{step}",
    )


def outer_kernel(
    step, own, near_in, far_in, diffused_core, diffused_near, diffused_far, targets, weights,
    sums, mid, field, tall, sems,
):
    block_count = own.shape[2] // BCOLS
    near, far, _, _ = z_blocks(block_count)
    side = lanes(core_side(block_count)[0], REACH)
    field[:, :, side] = own[:, :, side]
    field[:, :, lanes(near)] = own[:, :, lanes(near)] + near_in[...]
    field[:, :, lanes(far)] = own[:, :, lanes(far)] + far_in[...]
    (copy,) = start_copies(sems, [(field, mid)])
    tall[:, :, side] = diffused_core[...]
    tall[:, :, lanes(near)] = diffused_near[...]
    tall[:, :, lanes(far)] = diffused_far[...]
    sums[...] = spread(tall[...], spread_matrix(targets[step], weights[step], 0, own.shape[2]))
    copy.wait()


def outer(step, own, near_in, far_in, diffused, targets, weights):
    whole = shape(own, own.shape[2])
    return call(
        functools.partial(outer_kernel, step),
        (own, near_in, far_in, *diffused, targets, weights),
        [VMEM] * 8,
        (whole, whole),
        (VMEM, HBM),
        [pltpu.VMEM(own.shape, F32), pltpu.VMEM(own.shape, F32), pltpu.SemaphoreType.DMA((1,))],
        2_000_000_000,
        f"outer_step{step}",
    )


def squares(value):
    return jnp.sum(rows_of(value * value), axis=0, keepdims=True)


def most_kernel(own, core_in, far_in, start, lane_sums):
    block_count = own.shape[2] // BCOLS
    near, far, _, _ = z_blocks(block_count)
    side = lanes(core_side(block_count)[0], REACH)
    core = own[:, :, side] + core_in[...]
    behind = own[:, :, lanes(far)] + far_in[...]
    start[:, :, side] = core
    start[:, :, lanes(far)] = behind
    start[:, :, lanes(near)] = own[:, :, lanes(near)]
    core = squares(core)
    lane_sums[...] = core[:, :BCOLS] + core[:, BCOLS:] + squares(behind)


def most(own, core_in, far_in):
    return call(
        most_kernel,
        (own, core_in, far_in),
        [VMEM] * 3,
        (jax.ShapeDtypeStruct(own.shape, F32), jax.ShapeDtypeStruct((1, BCOLS), F32)),
        (VMEM, VMEM),
        [],
        1_000_000,
        "squares_of_most_blocks",
    )


def last_kernel(start, near_in, lane_sums, shares):
    near = z_blocks(start.shape[2] // BCOLS)[0]
    sums = lane_sums[...] + squares(start[:, :, lanes(near)] + near_in[...])
    shares[...] = jnp.broadcast_to(sums, shares.shape)


def last(count, start, near_in, lane_sums):
    return call(
        last_kernel,
        (start, near_in, lane_sums),
        [VMEM] * 3,
        jax.ShapeDtypeStruct((count, BCOLS), F32),
        VMEM,
        [],
        1_000_000,
        "squares_of_last_block",
    )


def scale_kernel(cells, start, near_in, shares, out, held, sems):
    block_count = start.shape[2] // BCOLS
    near = z_blocks(block_count)[0]
    energy = jnp.sum(shares[...]) / cells
    root = jnp.sqrt(jnp.full((1, 1, 1), energy + eps_energy, F32))
    copies = []
    for j in range(block_count):
        cols = slice(j * BCOLS, (j + 1) * BCOLS)
        held[:, :, cols] = (start[:, :, cols] + jnp.where(near == j, near_in[...], 0.0)) / root
        copies.append(pltpu.make_async_copy(held.at[:, :, cols], out.at[:, :, cols], sems.at[j]))
        copies[-1].start()
    for copy in copies:
        copy.wait()


def scale(start, near_in, shares, cells):
    return call(
        functools.partial(scale_kernel, cells),
        (start, near_in, shares),
        [VMEM] * 3,
        jax.ShapeDtypeStruct(start.shape, F32),
        HBM,
        [pltpu.VMEM(start.shape, F32), pltpu.SemaphoreType.DMA((start.shape[2] // BCOLS,))],
        1_000_000,
        "scale_start",
    )


def core_exchange(value):
    count = lax.axis_size("col")
    return lax.ppermute(value, "col", [(i, i ^ 1) for i in range(count)])


def z_exchange(value):
    count = lax.axis_size("col")
    pairs = [(i, (i + 1) % count if i % 2 else (i - 1) % count) for i in range(count)]
    return lax.ppermute(value, "col", pairs)


def shards(adj_final, inverses, dep_lists, dep_points, weights):
    count = lax.axis_size("col")
    all_blocks = count * inverses.shape[1]
    fields = jnp.transpose(adj_final, (1, 0, 2))
    inverses = jnp.transpose(inverses, (0, 2, 1, 3))
    fields, inverses, dep_lists, dep_points, weights = (
        pltpu.with_memory_space_constraint(value, pltpu.HBM)
        for value in (fields, inverses, dep_lists, dep_points, weights)
    )

    to_near, to_far, to_core, diffused, targets, merged = first(
        1, all_blocks, fields, inverses, dep_lists, dep_points, weights
    )
    near_in = z_exchange(to_near)
    far_in = z_exchange(to_far)
    own, inverse, to_core, diffused_core = inner(1, diffused, targets, merged, core_exchange(to_core), inverses)

    next_core_in = core_exchange(to_core)
    to_far, partial, diffused_near = near(0, own, near_in, inverse, targets, merged)
    next_far_in = z_exchange(to_far)
    to_near, diffused_far = far(0, own, far_in, partial, inverse, targets, merged)
    next_near_in = z_exchange(to_near)
    own, mid = outer(
        0, own, near_in, far_in, (diffused_core, diffused_near, diffused_far), targets, merged
    )

    start, lane_sums = most(own, next_core_in, next_far_in)
    shares = last(count, start, next_near_in, lane_sums)
    shares = lax.all_to_all(shares, "col", 0, 0, tiled=True)
    lanczos = scale(start, next_near_in, shares, adj_final.size * count)
    return jnp.transpose(mid, (1, 0, 2)), jnp.transpose(lanczos, (1, 0, 2))


def solution(mesh):
    in_specs = (
        P("mem", None, "col"),
        P("mem", "col", None, None),
        P("mem", "col", None),
        P("mem", None, "col"),
        P("mem", None, "col"),
    )
    out_specs = (P("mem", None, "col"), P("mem", None, "col"))
    return jax.shard_map(shards, mesh=mesh, in_specs=in_specs, out_specs=out_specs, check_vma=False)
```

```python
import functools

import jax
import jax.numpy as jnp
from jax import lax
from jax.experimental import pallas as pl
from jax.experimental.pallas import tpu as pltpu
from jax.sharding import PartitionSpec as P

BCOLS = 128
REACH = 2
SLOTS = 5
POINTS = 4
STEPS = 2
VMEM_LIMIT = 32 * 1024 * 1024
NOWHERE = -(1 << 14)

eps_energy = 1e-06

F32 = jnp.float32
BF16 = jnp.bfloat16
HBM = pl.BlockSpec(memory_space=pltpu.HBM)
VMEM = pl.BlockSpec(memory_space=pltpu.VMEM)


def z_blocks(block_count):
    follows = lax.rem(lax.axis_index("col"), 2)
    near = follows * (block_count - 1)
    away = 2 * follows - 1
    return near, near - away, near + away, near + 2 * away


def core_side(block_count):
    follows = 1 - lax.rem(lax.axis_index("col"), 2)
    return follows * (block_count - REACH), follows * (block_count + REACH) - REACH


def lanes(block, count=1):
    return pl.ds(pl.multiple_of(block * BCOLS, BCOLS), count * BCOLS)


def split(value):
    high = value.astype(BF16)
    return high, (value - high.astype(F32)).astype(BF16)


def target_columns(points, routes, step, block, block_count, all_blocks):
    slots = points // BCOLS
    here = lax.axis_index("col") * block_count + block
    found = jnp.zeros_like(points)
    for slot in range(SLOTS):
        offset = lax.rem(routes[step, block, slot] - here + REACH + all_blocks, all_blocks) - REACH
        found = jnp.where(slots == slot, (block + offset) * BCOLS, found)
    return found + points % BCOLS


def merge_points(targets, weights):
    targets = [targets[p : p + 1] for p in range(POINTS)]
    weights = [weights[p : p + 1] for p in range(POINTS)]
    for point in range(1, POINTS):
        for earlier in range(point):
            same = targets[point] == targets[earlier]
            weights[earlier] = weights[earlier] + jnp.where(same, weights[point], 0.0)
            targets[point] = jnp.where(same, NOWHERE, targets[point])
    return jnp.concatenate(targets, axis=0), jnp.concatenate(weights, axis=0)


def spread_matrix(targets, weights, first_column, rows=BCOLS):
    row = lax.broadcasted_iota(jnp.int32, (rows, targets.shape[1]), 0) + first_column
    total = jnp.zeros(row.shape, F32)
    for point in range(POINTS):
        total = jnp.where(row == targets[point : point + 1], weights[point : point + 1], total)
    return split(total)


def product(left, right, dims):
    return lax.dot_general(left, right, (dims, ((), ())), preferred_element_type=F32)


def rows_of(ref):
    levels, variables, columns = ref.shape
    return ref.reshape(levels * variables, columns)


def diffuse(inverse, field, out):
    levels, variables, columns = field.shape
    source, result = rows_of(field), rows_of(out)
    every = [pl.ds(v, levels, stride=variables) for v in range(variables)]
    wide = split(jnp.concatenate([source[rows, :] for rows in every], axis=1))
    turned = split(inverse.T)
    dims = ((1,), (0,))
    total = product(turned[0], wide[0], dims) + (
        product(turned[0], wide[1], dims) + product(turned[1], wide[0], dims)
    )
    for v, rows in enumerate(every):
        result[rows, :] = total[:, v * columns : (v + 1) * columns]


def spread(diffused, matrix):
    high, low = split(jnp.concatenate([rows_of(block)[...] for block in diffused], axis=1))
    left = jnp.concatenate([high, low, high], axis=1)
    right = jnp.concatenate([matrix[0], matrix[0], matrix[1]], axis=1)
    return product(left, right, ((1,), (1,)))


def side_matrix(targets, weights, step, blocks, first_columns):
    parts = []
    for block in blocks:
        cols = lanes(block)
        halves = [spread_matrix(targets[step, :, cols], weights[step, :, cols], column) for column in first_columns]
        parts.append([jnp.concatenate(half, axis=0) for half in zip(*halves)])
    return [jnp.concatenate(part, axis=1) for part in zip(*parts)]


def call(kernel, operands, in_specs, outs, out_specs, scratch, flops, name, limit=VMEM_LIMIT):
    return pl.pallas_call(
        kernel,
        out_shape=outs,
        in_specs=in_specs,
        out_specs=out_specs,
        scratch_shapes=scratch,
        compiler_params=pltpu.CompilerParams(vmem_limit_bytes=limit),
        cost_estimate=pl.CostEstimate(flops=flops, bytes_accessed=1_000_000, transcendentals=0),
        name=name,
    )(*operands)


def start_copies(sems, pairs):
    copies = [pltpu.make_async_copy(source, target, sems.at[i]) for i, (source, target) in enumerate(pairs)]
    for copy in copies:
        copy.start()
    return copies


def first_kernel(
    step, all_blocks, fields, inverses, routes, points, weights,
    to_near, to_far, to_core, diffused, targets, merged, field, inverse, route, point, weight, sems,
):
    block_count = inverses.shape[2]
    near, far, target_near, target_far = z_blocks(block_count)
    first, first_target = core_side(block_count)
    copies = start_copies(
        sems,
        [
            (routes, route),
            (points, point),
            (weights, weight),
            (inverses.at[step], inverse),
        ]
        + [(fields.at[:, :, lanes(j)], field.at[j]) for j in range(block_count)],
    )
    for copy in copies[:3]:
        copy.wait()
    for number in range(STEPS):
        for j in range(block_count):
            cols = slice(j * BCOLS, (j + 1) * BCOLS)
            found = target_columns(point[number, :, cols], route, number, j, block_count, all_blocks)
            targets[number, :, cols], merged[number, :, cols] = merge_points(found, weight[number, :, cols])
    z_matrix = side_matrix(targets, merged, step, (near, far), (target_near * BCOLS, target_far * BCOLS))
    core_columns = (first_target * BCOLS, (first_target + 1) * BCOLS)
    core_matrix = side_matrix(targets, merged, step, (first, first + 1), core_columns)
    copies[3].wait()
    for j in range(block_count):
        copies[4 + j].wait()
        diffuse(inverse[:, j, :], field.at[j], diffused.at[j])
    sums = spread([diffused.at[near], diffused.at[far]], z_matrix)
    rows_of(to_near)[...] = sums[:, :BCOLS]
    rows_of(to_far)[...] = sums[:, BCOLS:]
    sums = spread([diffused.at[first], diffused.at[first + 1]], core_matrix)
    for j in range(REACH):
        rows_of(to_core.at[j])[...] = sums[:, j * BCOLS : (j + 1) * BCOLS]


def blocks(like, *count):
    return jax.ShapeDtypeStruct((*count, *like.shape[-3:-1], BCOLS), F32)


def first(step, all_blocks, fields, inverses, routes, points, weights):
    one, two, whole = blocks(fields), blocks(fields, REACH), blocks(fields, inverses.shape[2])
    return call(
        functools.partial(first_kernel, step, all_blocks),
        (fields, inverses, routes, points, weights),
        [HBM] * 5,
        (
            one,
            one,
            two,
            whole,
            jax.ShapeDtypeStruct(points.shape, jnp.int32),
            jax.ShapeDtypeStruct(weights.shape, F32),
        ),
        (VMEM,) * 6,
        [
            pltpu.VMEM(whole.shape, F32),
            pltpu.VMEM(inverses.shape[1:], F32),
            pltpu.SMEM(routes.shape, jnp.int32),
            pltpu.VMEM(points.shape, jnp.int32),
            pltpu.VMEM(weights.shape, F32),
            pltpu.SemaphoreType.DMA((4 + inverses.shape[2],)),
        ],
        400_000_000,
        f"first_step{step}",
    )


def inner_kernel(
    step, diffused, targets, weights, core_in, inverses, own, inverse, to_core, diffused_core, sems
):
    block_count = inverses.shape[2]
    side_first, first_target = core_side(block_count)
    (copy,) = start_copies(sems, [(inverses.at[step - 1], inverse)])
    matrix = spread_matrix(targets[step], weights[step], 0, block_count * BCOLS)
    sums = spread([diffused.at[j] for j in range(block_count)], matrix)
    for j in range(block_count):
        rows_of(own.at[j])[...] = sums[:, j * BCOLS : (j + 1) * BCOLS]
    for j in range(REACH):
        own[side_first + j] += core_in[j]
    columns = (first_target * BCOLS, (first_target + 1) * BCOLS)
    matrix = side_matrix(targets, weights, step - 1, (side_first, side_first + 1), columns)
    copy.wait()
    for j in range(REACH):
        diffuse(inverse[:, side_first + j, :], own.at[side_first + j], diffused_core.at[j])
    sums = spread([diffused_core.at[j] for j in range(REACH)], matrix)
    for j in range(REACH):
        rows_of(to_core.at[j])[...] = sums[:, j * BCOLS : (j + 1) * BCOLS]


def inner(step, diffused, targets, weights, core_in, inverses):
    two = blocks(diffused, REACH)
    return call(
        functools.partial(inner_kernel, step),
        (diffused, targets, weights, core_in, inverses),
        [VMEM] * 4 + [HBM],
        (blocks(diffused, diffused.shape[0]), jax.ShapeDtypeStruct(inverses.shape[1:], F32), two, two),
        (VMEM,) * 4,
        [pltpu.SemaphoreType.DMA((1,))],
        2_000_000_000,
        f"inner_step{step}",
    )


def near_kernel(step, own, near_in, inverse, targets, weights, to_far, to_near, diffused, field):
    block_count = inverse.shape[1]
    near, _, target_near, target_far = z_blocks(block_count)
    cols = lanes(near)
    field[...] = own[near] + near_in[...]
    diffuse(inverse[:, near, :], field, diffused)
    halves = [
        spread_matrix(targets[step, :, cols], weights[step, :, cols], target * BCOLS)
        for target in (target_far, target_near)
    ]
    sums = spread([diffused], [jnp.concatenate(half, axis=0) for half in zip(*halves)])
    rows_of(to_far)[...] = sums[:, :BCOLS]
    rows_of(to_near)[...] = sums[:, BCOLS:]


def near(step, own, near_in, inverse, targets, weights):
    one = blocks(own)
    return call(
        functools.partial(near_kernel, step),
        (own, near_in, inverse, targets, weights),
        [VMEM] * 5,
        (one, one, one),
        (VMEM,) * 3,
        [pltpu.VMEM(one.shape, F32)],
        300_000_000,
        f"near_step{step}",
    )


def far_kernel(step, own, far_in, partial, inverse, targets, weights, to_near, diffused, field):
    block_count = inverse.shape[1]
    _, far, target_near, _ = z_blocks(block_count)
    cols = lanes(far)
    field[...] = own[far] + far_in[...]
    diffuse(inverse[:, far, :], field, diffused)
    matrix = spread_matrix(targets[step, :, cols], weights[step, :, cols], target_near * BCOLS)
    rows_of(to_near)[...] = rows_of(partial)[...] + spread([diffused], matrix)


def far(step, own, far_in, partial, inverse, targets, weights):
    one = blocks(own)
    return call(
        functools.partial(far_kernel, step),
        (own, far_in, partial, inverse, targets, weights),
        [VMEM] * 6,
        (one, one),
        (VMEM,) * 2,
        [pltpu.VMEM(one.shape, F32)],
        300_000_000,
        f"far_step{step}",
    )


def outer_kernel(
    step, own, near_in, far_in, diffused_core, diffused_near, diffused_far, targets, weights,
    sums, mid, field, tall, sems,
):
    block_count = own.shape[0]
    near, far, _, _ = z_blocks(block_count)
    side = core_side(block_count)[0]
    for j in range(REACH):
        field[side + j] = own[side + j]
        tall[side + j] = diffused_core[j]
    field[near] = own[near] + near_in[...]
    field[far] = own[far] + far_in[...]
    tall[near] = diffused_near[...]
    tall[far] = diffused_far[...]
    copies = start_copies(sems, [(field.at[j], mid.at[:, :, lanes(j)]) for j in range(block_count)])
    matrix = spread_matrix(targets[step], weights[step], 0, block_count * BCOLS)
    total = spread([tall.at[j] for j in range(block_count)], matrix)
    for j in range(block_count):
        rows_of(sums.at[j])[...] = total[:, j * BCOLS : (j + 1) * BCOLS]
    for copy in copies:
        copy.wait()


def outer(step, own, near_in, far_in, diffused, targets, weights):
    block_count, levels, variables, _ = own.shape
    return call(
        functools.partial(outer_kernel, step),
        (own, near_in, far_in, *diffused, targets, weights),
        [VMEM] * 8,
        (
            blocks(own, block_count),
            jax.ShapeDtypeStruct((levels, variables, block_count * BCOLS), F32),
        ),
        (VMEM, HBM),
        [
            pltpu.VMEM(own.shape, F32),
            pltpu.VMEM(own.shape, F32),
            pltpu.SemaphoreType.DMA((block_count,)),
        ],
        2_000_000_000,
        f"outer_step{step}",
    )


def squares(value):
    rows = value.reshape(value.shape[0] * value.shape[1], value.shape[2])
    return jnp.sum(rows * rows, axis=0, keepdims=True)


def most_kernel(own, core_in, far_in, start, lane_sums):
    block_count = own.shape[0]
    near, far, _, _ = z_blocks(block_count)
    side = core_side(block_count)[0]
    value = own[far] + far_in[...]
    start[far] = value
    start[near] = own[near]
    total = squares(value)
    for j in range(REACH):
        value = own[side + j] + core_in[j]
        start[side + j] = value
        total += squares(value)
    lane_sums[...] = total


def most(own, core_in, far_in):
    return call(
        most_kernel,
        (own, core_in, far_in),
        [VMEM] * 3,
        (jax.ShapeDtypeStruct(own.shape, F32), jax.ShapeDtypeStruct((1, BCOLS), F32)),
        (VMEM, VMEM),
        [],
        1_000_000,
        "squares_of_most_blocks",
    )


def last_kernel(start, near_in, lane_sums, shares):
    near = z_blocks(start.shape[0])[0]
    sums = lane_sums[...] + squares(start[near] + near_in[...])
    shares[...] = jnp.broadcast_to(sums, shares.shape)


def last(count, start, near_in, lane_sums):
    return call(
        last_kernel,
        (start, near_in, lane_sums),
        [VMEM] * 3,
        jax.ShapeDtypeStruct((count, BCOLS), F32),
        VMEM,
        [],
        1_000_000,
        "squares_of_last_block",
    )


def scale_kernel(cells, start, near_in, shares, out, held, sems):
    block_count = start.shape[0]
    near = z_blocks(block_count)[0]
    energy = jnp.sum(shares[...]) / cells
    root = jnp.sqrt(jnp.full((1, 1, 1), energy + eps_energy, F32))
    copies = []
    for j in range(block_count):
        held[j] = (start[j] + jnp.where(near == j, near_in[...], 0.0)) / root
        copies.append(pltpu.make_async_copy(held.at[j], out.at[:, :, lanes(j)], sems.at[j]))
        copies[-1].start()
    for copy in copies:
        copy.wait()


def scale(start, near_in, shares, cells):
    return call(
        functools.partial(scale_kernel, cells),
        (start, near_in, shares),
        [VMEM] * 3,
        jax.ShapeDtypeStruct((*start.shape[1:3], start.shape[0] * BCOLS), F32),
        HBM,
        [pltpu.VMEM(start.shape, F32), pltpu.SemaphoreType.DMA(start.shape[:1])],
        1_000_000,
        "scale_start",
    )


def core_exchange(value):
    count = lax.axis_size("col")
    return lax.ppermute(value, "col", [(i, i ^ 1) for i in range(count)])


def z_exchange(value):
    count = lax.axis_size("col")
    pairs = [(i, (i + 1) % count if i % 2 else (i - 1) % count) for i in range(count)]
    return lax.ppermute(value, "col", pairs)


def shards(adj_final, inverses, dep_lists, dep_points, weights):
    count = lax.axis_size("col")
    all_blocks = count * inverses.shape[1]
    fields = jnp.transpose(adj_final, (1, 0, 2))
    inverses = jnp.transpose(inverses, (0, 2, 1, 3))
    fields, inverses, dep_lists, dep_points, weights = (
        pltpu.with_memory_space_constraint(value, pltpu.HBM)
        for value in (fields, inverses, dep_lists, dep_points, weights)
    )

    to_near, to_far, to_core, diffused, targets, merged = first(
        1, all_blocks, fields, inverses, dep_lists, dep_points, weights
    )
    near_in = z_exchange(to_near)
    far_in = z_exchange(to_far)
    own, inverse, to_core, diffused_core = inner(1, diffused, targets, merged, core_exchange(to_core), inverses)

    next_core_in = core_exchange(to_core)
    to_far, partial, diffused_near = near(0, own, near_in, inverse, targets, merged)
    next_far_in = z_exchange(to_far)
    to_near, diffused_far = far(0, own, far_in, partial, inverse, targets, merged)
    next_near_in = z_exchange(to_near)
    own, mid = outer(
        0, own, near_in, far_in, (diffused_core, diffused_near, diffused_far), targets, merged
    )

    start, lane_sums = most(own, next_core_in, next_far_in)
    shares = last(count, start, next_near_in, lane_sums)
    shares = lax.all_to_all(shares, "col", 0, 0, tiled=True)
    lanczos = scale(start, next_near_in, shares, adj_final.size * count)
    return jnp.transpose(mid, (1, 0, 2)), jnp.transpose(lanczos, (1, 0, 2))


def solution(mesh):
    in_specs = (
        P("mem", None, "col"),
        P("mem", "col", None, None),
        P("mem", "col", None),
        P("mem", None, "col"),
        P("mem", None, "col"),
    )
    out_specs = (P("mem", None, "col"), P("mem", None, "col"))
    return jax.shard_map(shards, mesh=mesh, in_specs=in_specs, out_specs=out_specs, check_vma=False)
```

```python
import functools

import jax
import jax.numpy as jnp
from jax import lax
from jax.experimental import pallas as pl
from jax.experimental.pallas import tpu as pltpu
from jax.sharding import PartitionSpec as P

BCOLS = 128
REACH = 2
SLOTS = 5
POINTS = 4
STEPS = 2
VMEM_LIMIT = 32 * 1024 * 1024
NOWHERE = -(1 << 14)
PIECES = 3

eps_energy = 1e-06

F32 = jnp.float32
BF16 = jnp.bfloat16
ANY = pl.BlockSpec(memory_space=pl.ANY)
HBM = pl.BlockSpec(memory_space=pltpu.HBM)
VMEM = pl.BlockSpec(memory_space=pltpu.VMEM)


def z_blocks(block_count):
    follows = lax.rem(lax.axis_index("col"), 2)
    near = follows * (block_count - 1)
    away = 2 * follows - 1
    return near, near - away, near + away, near + 2 * away


def core_side(block_count):
    follows = 1 - lax.rem(lax.axis_index("col"), 2)
    return follows * (block_count - REACH), follows * (block_count + REACH) - REACH


def lanes(block, count=1):
    return pl.ds(pl.multiple_of(block * BCOLS, BCOLS), count * BCOLS)


def split(value):
    high = value.astype(BF16)
    return high, (value - high.astype(F32)).astype(BF16)


def target_columns(points, routes, step, block, block_count, all_blocks):
    slots = points // BCOLS
    here = lax.axis_index("col") * block_count + block
    found = jnp.zeros_like(points)
    for slot in range(SLOTS):
        offset = lax.rem(routes[step, block, slot] - here + REACH + all_blocks, all_blocks) - REACH
        found = jnp.where(slots == slot, (block + offset) * BCOLS, found)
    return found + points % BCOLS


def merge_points(targets, weights):
    targets = [targets[p : p + 1] for p in range(POINTS)]
    weights = [weights[p : p + 1] for p in range(POINTS)]
    for point in range(1, POINTS):
        for earlier in range(point):
            same = targets[point] == targets[earlier]
            weights[earlier] = weights[earlier] + jnp.where(same, weights[point], 0.0)
            targets[point] = jnp.where(same, NOWHERE, targets[point])
    return jnp.concatenate(targets, axis=0), jnp.concatenate(weights, axis=0)


def spread_matrix(targets, weights, first_column, rows=BCOLS):
    row = lax.broadcasted_iota(jnp.int32, (rows, targets.shape[1]), 0) + first_column
    total = jnp.zeros(row.shape, F32)
    for point in range(POINTS):
        total = jnp.where(row == targets[point : point + 1], weights[point : point + 1], total)
    return split(total)


def product(left, right, dims):
    return lax.dot_general(left, right, (dims, ((), ())), preferred_element_type=F32)


def rows_of(ref):
    levels, variables, columns = ref.shape
    return ref.reshape(levels * variables, columns)


def diffuse(inverse, field, out):
    levels, variables, columns = field.shape
    source, result = rows_of(field), rows_of(out)
    every = [pl.ds(v, levels, stride=variables) for v in range(variables)]
    wide = split(jnp.concatenate([source[rows, :] for rows in every], axis=1))
    turned = split(inverse.T)
    dims = ((1,), (0,))
    total = product(turned[0], wide[0], dims) + (
        product(turned[0], wide[1], dims) + product(turned[1], wide[0], dims)
    )
    for v, rows in enumerate(every):
        result[rows, :] = total[:, v * columns : (v + 1) * columns]


def spread(diffused, matrix):
    high, low = split(jnp.concatenate([rows_of(block)[...] for block in diffused], axis=1))
    left = jnp.concatenate([high, low, high], axis=1)
    right = jnp.concatenate([matrix[0], matrix[0], matrix[1]], axis=1)
    return product(left, right, ((1,), (1,)))


def side_matrix(targets, weights, step, blocks, first_columns):
    parts = []
    for block in blocks:
        cols = lanes(block)
        halves = [spread_matrix(targets[step, :, cols], weights[step, :, cols], column) for column in first_columns]
        parts.append([jnp.concatenate(half, axis=0) for half in zip(*halves)])
    return [jnp.concatenate(part, axis=1) for part in zip(*parts)]


def call(kernel, operands, in_specs, outs, out_specs, scratch, flops, name, limit=VMEM_LIMIT):
    return pl.pallas_call(
        kernel,
        out_shape=outs,
        in_specs=in_specs,
        out_specs=out_specs,
        scratch_shapes=scratch,
        compiler_params=pltpu.CompilerParams(vmem_limit_bytes=limit),
        cost_estimate=pl.CostEstimate(flops=flops, bytes_accessed=1_000_000, transcendentals=0),
        name=name,
    )(*operands)


def start_copies(sems, pairs):
    copies = [pltpu.make_async_copy(source, target, sems.at[i]) for i, (source, target) in enumerate(pairs)]
    for copy in copies:
        copy.start()
    return copies


def first_kernel(
    step, all_blocks, fields, inverses, routes, points, weights,
    to_near, to_far, diffused, inverse, targets, merged, field, route, point, weight, sems,
):
    block_count = inverses.shape[2]
    near, far, target_near, target_far = z_blocks(block_count)
    copies = start_copies(
        sems,
        [
            (routes, route),
            (points, point),
            (weights, weight),
            (inverses.at[step], inverse),
            (fields.at[:, :, lanes(near)], field.at[0]),
            (fields.at[:, :, lanes(far)], field.at[1]),
        ],
    )
    for copy in copies[:3]:
        copy.wait()
    for number in range(STEPS):
        for j in range(block_count):
            cols = slice(j * BCOLS, (j + 1) * BCOLS)
            found = target_columns(point[number, :, cols], route, number, j, block_count, all_blocks)
            targets[number, :, cols], merged[number, :, cols] = merge_points(found, weight[number, :, cols])
    matrix = side_matrix(targets, merged, step, (near, far), (target_near * BCOLS, target_far * BCOLS))
    copies[3].wait()
    for j, block in enumerate((near, far)):
        copies[4 + j].wait()
        diffuse(inverse[:, block, :], field.at[j], diffused.at[j])
    sums = spread([diffused.at[0], diffused.at[1]], matrix)
    rows_of(to_near)[...] = sums[:, :BCOLS]
    rows_of(to_far)[...] = sums[:, BCOLS:]


def level_pieces(levels):
    return [slice(levels * part // PIECES, levels * (part + 1) // PIECES) for part in range(PIECES)]


def blocks(like, *count):
    return jax.ShapeDtypeStruct((*count, *like.shape[-3:-1], BCOLS), F32)


def first(step, all_blocks, fields, inverses, routes, points, weights):
    one, two = blocks(fields), blocks(fields, REACH)
    return call(
        functools.partial(first_kernel, step, all_blocks),
        (fields, inverses, routes, points, weights),
        [HBM] * 5,
        (
            one,
            one,
            two,
            jax.ShapeDtypeStruct(inverses.shape[1:], F32),
            jax.ShapeDtypeStruct(points.shape, jnp.int32),
            jax.ShapeDtypeStruct(weights.shape, F32),
        ),
        (VMEM,) * 6,
        [
            pltpu.VMEM(two.shape, F32),
            pltpu.SMEM(routes.shape, jnp.int32),
            pltpu.VMEM(points.shape, jnp.int32),
            pltpu.VMEM(weights.shape, F32),
            pltpu.SemaphoreType.DMA((6,)),
        ],
        400_000_000,
        f"first_step{step}",
    )


def inner_kernel(
    step, fields, z_diffused, inverse, targets, weights, inverses, own, next_inverse, *refs
):
    to_core, (field, tall, sems) = refs[:-3], refs[-3:]
    block_count = inverse.shape[1]
    near, far, _, _ = z_blocks(block_count)
    side, first_target = core_side(block_count)
    copies = start_copies(
        sems,
        [(fields.at[:, :, lanes(side + j)], field.at[j]) for j in range(REACH)]
        + [(inverses.at[step - 1], next_inverse)],
    )
    columns = (first_target * BCOLS, (first_target + 1) * BCOLS)
    core_matrix = side_matrix(targets, weights, step, (side, side + 1), columns)
    matrix = spread_matrix(targets[step], weights[step], 0, block_count * BCOLS)
    tall[near] = z_diffused[0]
    tall[far] = z_diffused[1]
    for j in range(REACH):
        copies[j].wait()
        diffuse(inverse[:, side + j, :], field.at[j], tall.at[side + j])
    sums = spread([tall.at[side + j] for j in range(REACH)], core_matrix)
    variables = field.shape[2]
    for piece, levels in zip(to_core, level_pieces(field.shape[1])):
        rows = slice(levels.start * variables, levels.stop * variables)
        for j in range(REACH):
            rows_of(piece.at[j])[...] = sums[rows, j * BCOLS : (j + 1) * BCOLS]
    sums = spread([tall.at[j] for j in range(block_count)], matrix)
    for j in range(block_count):
        rows_of(own.at[j])[...] = sums[:, j * BCOLS : (j + 1) * BCOLS]
    copies[REACH].wait()


def inner(step, fields, z_diffused, inverse, targets, weights, inverses):
    two, whole = blocks(fields, REACH), blocks(fields, inverse.shape[1])
    pieces = [
        jax.ShapeDtypeStruct((REACH, levels.stop - levels.start, *two.shape[2:]), F32)
        for levels in level_pieces(fields.shape[0])
    ]
    own, inverse, *pieces = call(
        functools.partial(inner_kernel, step),
        (fields, z_diffused, inverse, targets, weights, inverses),
        [HBM] + [VMEM] * 4 + [HBM],
        (whole, jax.ShapeDtypeStruct(inverse.shape, F32), *pieces),
        (VMEM,) * (2 + PIECES),
        [
            pltpu.VMEM(two.shape, F32),
            pltpu.VMEM(whole.shape, F32),
            pltpu.SemaphoreType.DMA((REACH + 1,)),
        ],
        2_000_000_000,
        f"inner_step{step}",
    )
    return own, inverse, pieces


def add_pieces(pieces, block, out):
    for piece, levels in zip(pieces, level_pieces(out.shape[0])):
        out[levels] += piece[block]


def core_kernel(step, own, inverse, targets, weights, _, *refs):
    core_in, (to_core, diffused, field) = refs[:PIECES], refs[PIECES:]
    side, first_target = core_side(own.shape[0])
    columns = (first_target * BCOLS, (first_target + 1) * BCOLS)
    matrix = side_matrix(targets, weights, step, (side, side + 1), columns)
    for j in range(REACH):
        field[j] = own[side + j]
        add_pieces(core_in, j, field.at[j])
        diffuse(inverse[:, side + j, :], field.at[j], diffused.at[j])
    sums = spread([diffused.at[j] for j in range(REACH)], matrix)
    for j in range(REACH):
        rows_of(to_core.at[j])[...] = sums[:, j * BCOLS : (j + 1) * BCOLS]


def core(step, own, core_in, inverse, targets, weights, behind):
    two = blocks(own, REACH)
    return call(
        functools.partial(core_kernel, step),
        (own, inverse, targets, weights, behind, *core_in),
        [VMEM] * 4 + [ANY] + [VMEM] * PIECES,
        (two, two),
        (VMEM,) * 2,
        [pltpu.VMEM(two.shape, F32)],
        300_000_000,
        f"core_step{step}",
    )


def near_kernel(step, own, near_in, inverse, targets, weights, to_far, to_near, diffused, field):
    block_count = inverse.shape[1]
    near, _, target_near, target_far = z_blocks(block_count)
    cols = lanes(near)
    field[...] = own[near] + near_in[...]
    diffuse(inverse[:, near, :], field, diffused)
    halves = [
        spread_matrix(targets[step, :, cols], weights[step, :, cols], target * BCOLS)
        for target in (target_far, target_near)
    ]
    sums = spread([diffused], [jnp.concatenate(half, axis=0) for half in zip(*halves)])
    rows_of(to_far)[...] = sums[:, :BCOLS]
    rows_of(to_near)[...] = sums[:, BCOLS:]


def near(step, own, near_in, inverse, targets, weights):
    one = blocks(own)
    return call(
        functools.partial(near_kernel, step),
        (own, near_in, inverse, targets, weights),
        [VMEM] * 5,
        (one, one, one),
        (VMEM,) * 3,
        [pltpu.VMEM(one.shape, F32)],
        300_000_000,
        f"near_step{step}",
    )


def far_kernel(step, own, far_in, partial, inverse, targets, weights, _, to_near, diffused, field):
    block_count = inverse.shape[1]
    _, far, target_near, _ = z_blocks(block_count)
    cols = lanes(far)
    field[...] = own[far] + far_in[...]
    diffuse(inverse[:, far, :], field, diffused)
    matrix = spread_matrix(targets[step, :, cols], weights[step, :, cols], target_near * BCOLS)
    rows_of(to_near)[...] = rows_of(partial)[...] + spread([diffused], matrix)


def far(step, own, far_in, partial, inverse, targets, weights, behind):
    one = blocks(own)
    return call(
        functools.partial(far_kernel, step),
        (own, far_in, partial, inverse, targets, weights, behind),
        [VMEM] * 6 + [ANY],
        (one, one),
        (VMEM,) * 2,
        [pltpu.VMEM(one.shape, F32)],
        300_000_000,
        f"far_step{step}",
    )


def outer_kernel(
    step, own, near_in, far_in, diffused_core, diffused_near, diffused_far, targets, weights, *refs
):
    core_in, (sums, mid, field, tall, sems) = refs[:PIECES], refs[PIECES:]
    block_count = own.shape[0]
    near, far, _, _ = z_blocks(block_count)
    side = core_side(block_count)[0]
    for j in range(REACH):
        field[side + j] = own[side + j]
        add_pieces(core_in, j, field.at[side + j])
        tall[side + j] = diffused_core[j]
    field[near] = own[near] + near_in[...]
    field[far] = own[far] + far_in[...]
    tall[near] = diffused_near[...]
    tall[far] = diffused_far[...]
    copies = start_copies(sems, [(field.at[j], mid.at[:, :, lanes(j)]) for j in range(block_count)])
    matrix = spread_matrix(targets[step], weights[step], 0, block_count * BCOLS)
    total = spread([tall.at[j] for j in range(block_count)], matrix)
    for j in range(block_count):
        rows_of(sums.at[j])[...] = total[:, j * BCOLS : (j + 1) * BCOLS]
    for copy in copies:
        copy.wait()


def outer(step, own, near_in, far_in, core_in, diffused, targets, weights):
    block_count, levels, variables, _ = own.shape
    return call(
        functools.partial(outer_kernel, step),
        (own, near_in, far_in, *diffused, targets, weights, *core_in),
        [VMEM] * (8 + PIECES),
        (
            blocks(own, block_count),
            jax.ShapeDtypeStruct((levels, variables, block_count * BCOLS), F32),
        ),
        (VMEM, HBM),
        [
            pltpu.VMEM(own.shape, F32),
            pltpu.VMEM(own.shape, F32),
            pltpu.SemaphoreType.DMA((block_count,)),
        ],
        2_000_000_000,
        f"outer_step{step}",
    )


def squares(value):
    rows = value.reshape(value.shape[0] * value.shape[1], value.shape[2])
    return jnp.sum(rows * rows, axis=0, keepdims=True)


def most_kernel(own, core_in, far_in, start, lane_sums):
    block_count = own.shape[0]
    near, far, _, _ = z_blocks(block_count)
    side = core_side(block_count)[0]
    value = own[far] + far_in[...]
    start[far] = value
    start[near] = own[near]
    total = squares(value)
    for j in range(REACH):
        value = own[side + j] + core_in[j]
        start[side + j] = value
        total += squares(value)
    lane_sums[...] = total


def most(own, core_in, far_in):
    return call(
        most_kernel,
        (own, core_in, far_in),
        [VMEM] * 3,
        (jax.ShapeDtypeStruct(own.shape, F32), jax.ShapeDtypeStruct((1, BCOLS), F32)),
        (VMEM, VMEM),
        [],
        1_000_000,
        "squares_of_most_blocks",
    )


def last_kernel(start, near_in, lane_sums, shares):
    near = z_blocks(start.shape[0])[0]
    shares[...] = lane_sums[...] + squares(start[near] + near_in[...])


def last(start, near_in, lane_sums):
    return call(
        last_kernel,
        (start, near_in, lane_sums),
        [VMEM] * 3,
        jax.ShapeDtypeStruct(lane_sums.shape, F32),
        VMEM,
        [],
        1_000_000,
        "squares_of_last_block",
    )


def scale_kernel(cells, start, near_in, *refs):
    *shares, out, held, sems = refs
    block_count = start.shape[0]
    near = z_blocks(block_count)[0]
    total = shares[0][...]
    for share in shares[1:]:
        total += share[...]
    energy = jnp.sum(total) / cells
    factor = 1.0 / jnp.sqrt(jnp.full((1, 1, 1), energy + eps_energy, F32))
    levels = start.shape[1]
    parts = 5
    copies = []
    for part in range(parts):
        rows = slice(levels * part // parts, levels * (part + 1) // parts)
        for j in range(block_count):
            cols = slice(j * BCOLS, (j + 1) * BCOLS)
            held[rows, :, cols] = (start[j, rows] + jnp.where(near == j, near_in[rows], 0.0)) * factor
        copies.append(pltpu.make_async_copy(held.at[rows], out.at[rows], sems.at[part]))
        copies[-1].start()
    for copy in copies:
        copy.wait()


def scale(start, near_in, shares, cells):
    return call(
        functools.partial(scale_kernel, cells),
        (start, near_in, *shares),
        [VMEM] * (2 + len(shares)),
        jax.ShapeDtypeStruct((*start.shape[1:3], start.shape[0] * BCOLS), F32),
        HBM,
        [pltpu.VMEM((*start.shape[1:3], start.shape[0] * BCOLS), F32), pltpu.SemaphoreType.DMA((5,))],
        1_000_000,
        "scale_start",
    )


def add_kernel(*refs):
    *parts, out = refs
    total = parts[0][...]
    for part in parts[1:]:
        total += part[...]
    out[...] = total


def add(parts):
    return call(
        add_kernel, parts, [VMEM] * len(parts), jax.ShapeDtypeStruct(parts[0].shape, F32), VMEM, [], 1, "add_shares"
    )


def share_out(share):
    count = lax.axis_size("col")
    if count > 8:
        return [lax.all_to_all(jnp.broadcast_to(share, (count, BCOLS)), "col", 0, 0, tiled=True)]
    share = add([share, core_exchange(share)])
    return [share] + [lax.ppermute(share, "col", [(i, i ^ s) for i in range(count)]) for s in (2, 4, 6)]


def core_exchange(value):
    count = lax.axis_size("col")
    return lax.ppermute(value, "col", [(i, i ^ 1) for i in range(count)])


def z_exchange(value):
    count = lax.axis_size("col")
    pairs = [(i, (i + 1) % count if i % 2 else (i - 1) % count) for i in range(count)]
    return lax.ppermute(value, "col", pairs)


def shards(adj_final, inverses, dep_lists, dep_points, weights):
    count = lax.axis_size("col")
    all_blocks = count * inverses.shape[1]
    fields = jnp.transpose(adj_final, (1, 0, 2))
    inverses = jnp.transpose(inverses, (0, 2, 1, 3))
    fields, inverses, dep_lists, dep_points, weights = (
        pltpu.with_memory_space_constraint(value, pltpu.HBM)
        for value in (fields, inverses, dep_lists, dep_points, weights)
    )

    to_near, to_far, z_diffused, inverse, targets, merged = first(
        1, all_blocks, fields, inverses, dep_lists, dep_points, weights
    )
    near_in = z_exchange(to_near)
    far_in = z_exchange(to_far)
    own, inverse, pieces = inner(1, fields, z_diffused, inverse, targets, merged, inverses)
    core_in = [core_exchange(piece) for piece in pieces]

    to_far, partial, diffused_near = near(0, own, near_in, inverse, targets, merged)
    next_far_in = z_exchange(to_far)
    to_core, diffused_core = core(0, own, core_in, inverse, targets, merged, partial)
    next_core_in = core_exchange(to_core)
    to_near, diffused_far = far(0, own, far_in, partial, inverse, targets, merged, diffused_core)
    next_near_in = z_exchange(to_near)
    diffused = (diffused_core, diffused_near, diffused_far)
    own, mid = outer(0, own, near_in, far_in, core_in, diffused, targets, merged)

    start, lane_sums = most(own, next_core_in, next_far_in)
    shares = share_out(last(start, next_near_in, lane_sums))
    lanczos = scale(start, next_near_in, shares, adj_final.size * count)
    return jnp.transpose(mid, (1, 0, 2)), jnp.transpose(lanczos, (1, 0, 2))


def solution(mesh):
    in_specs = (
        P("mem", None, "col"),
        P("mem", "col", None, None),
        P("mem", "col", None),
        P("mem", None, "col"),
        P("mem", None, "col"),
    )
    out_specs = (P("mem", None, "col"), P("mem", None, "col"))
    return jax.shard_map(shards, mesh=mesh, in_specs=in_specs, out_specs=out_specs, check_vma=False)
```

```python
import functools

import jax
import jax.numpy as jnp
from jax import lax
from jax.experimental import pallas as pl
from jax.experimental.pallas import tpu as pltpu
from jax.sharding import PartitionSpec as P

BCOLS = 128
REACH = 2
SLOTS = 5
POINTS = 4
STEPS = 2
VMEM_LIMIT = 32 * 1024 * 1024
NOWHERE = -(1 << 14)
PIECES = 3

eps_energy = 1e-06

F32 = jnp.float32
BF16 = jnp.bfloat16
ANY = pl.BlockSpec(memory_space=pl.ANY)
HBM = pl.BlockSpec(memory_space=pltpu.HBM)
VMEM = pl.BlockSpec(memory_space=pltpu.VMEM)


def z_blocks(block_count):
    follows = lax.rem(lax.axis_index("col"), 2)
    near = follows * (block_count - 1)
    away = 2 * follows - 1
    return near, near - away, near + away, near + 2 * away


def core_side(block_count):
    follows = 1 - lax.rem(lax.axis_index("col"), 2)
    return follows * (block_count - REACH), follows * (block_count + REACH) - REACH


def lanes(block, count=1):
    return pl.ds(pl.multiple_of(block * BCOLS, BCOLS), count * BCOLS)


def split(value):
    high = value.astype(BF16)
    return high, (value - high.astype(F32)).astype(BF16)


def target_columns(points, routes, step, block, block_count, all_blocks):
    slots = points // BCOLS
    here = lax.axis_index("col") * block_count + block
    found = jnp.zeros_like(points)
    for slot in range(SLOTS):
        offset = lax.rem(routes[step, block, slot] - here + REACH + all_blocks, all_blocks) - REACH
        found = jnp.where(slots == slot, (block + offset) * BCOLS, found)
    return found + points % BCOLS


def merge_points(targets, weights):
    targets = [targets[p : p + 1] for p in range(POINTS)]
    weights = [weights[p : p + 1] for p in range(POINTS)]
    for point in range(1, POINTS):
        for earlier in range(point):
            same = targets[point] == targets[earlier]
            weights[earlier] = weights[earlier] + jnp.where(same, weights[point], 0.0)
            targets[point] = jnp.where(same, NOWHERE, targets[point])
    return jnp.concatenate(targets, axis=0), jnp.concatenate(weights, axis=0)


def spread_matrix(targets, weights, first_column, rows=BCOLS):
    row = lax.broadcasted_iota(jnp.int32, (rows, targets.shape[1]), 0) + first_column
    total = jnp.zeros(row.shape, F32)
    for point in range(POINTS):
        total = jnp.where(row == targets[point : point + 1], weights[point : point + 1], total)
    return split(total)


def product(left, right, dims):
    return lax.dot_general(left, right, (dims, ((), ())), preferred_element_type=F32)


def rows_of(ref):
    levels, variables, columns = ref.shape
    return ref.reshape(levels * variables, columns)


def diffuse(turned, field, out):
    levels, variables, columns = field.shape
    source, result = rows_of(field), rows_of(out)
    every = [pl.ds(v, levels, stride=variables) for v in range(variables)]
    wide = split(jnp.concatenate([source[rows, :] for rows in every], axis=1))
    turned = split(turned)
    dims = ((1,), (0,))
    total = product(turned[0], wide[0], dims) + (
        product(turned[0], wide[1], dims) + product(turned[1], wide[0], dims)
    )
    for v, rows in enumerate(every):
        result[rows, :] = total[:, v * columns : (v + 1) * columns]


def spread(diffused, matrix):
    high, low = split(jnp.concatenate([rows_of(block)[...] for block in diffused], axis=1))
    left = jnp.concatenate([high, low, high], axis=1)
    right = jnp.concatenate([matrix[0], matrix[0], matrix[1]], axis=1)
    return product(left, right, ((1,), (1,)))


def side_matrix(targets, weights, step, blocks, first_columns):
    parts = []
    for block in blocks:
        cols = lanes(block)
        halves = [spread_matrix(targets[step, :, cols], weights[step, :, cols], column) for column in first_columns]
        parts.append([jnp.concatenate(half, axis=0) for half in zip(*halves)])
    return [jnp.concatenate(part, axis=1) for part in zip(*parts)]


def call(kernel, operands, in_specs, outs, out_specs, scratch, flops, name, limit=VMEM_LIMIT):
    return pl.pallas_call(
        kernel,
        out_shape=outs,
        in_specs=in_specs,
        out_specs=out_specs,
        scratch_shapes=scratch,
        compiler_params=pltpu.CompilerParams(vmem_limit_bytes=limit),
        cost_estimate=pl.CostEstimate(flops=flops, bytes_accessed=min(flops, 1_000_000), transcendentals=0),
        name=name,
    )(*operands)


def start_copies(sems, pairs):
    copies = [pltpu.make_async_copy(source, target, sems.at[i]) for i, (source, target) in enumerate(pairs)]
    for copy in copies:
        copy.start()
    return copies


def first_kernel(
    step, all_blocks, fields, inverses, routes, points, weights,
    to_near, to_far, diffused, inverse, targets, merged, field, route, point, weight, sems,
):
    block_count = inverses.shape[2]
    near, far, target_near, target_far = z_blocks(block_count)
    copies = start_copies(
        sems,
        [
            (routes, route),
            (points, point),
            (weights, weight),
            (inverses.at[step], inverse),
            (fields.at[:, :, lanes(near)], field.at[0]),
            (fields.at[:, :, lanes(far)], field.at[1]),
        ],
    )
    for copy in copies[:3]:
        copy.wait()
    for number in range(STEPS):
        for j in range(block_count):
            cols = slice(j * BCOLS, (j + 1) * BCOLS)
            found = target_columns(point[number, :, cols], route, number, j, block_count, all_blocks)
            targets[number, :, cols], merged[number, :, cols] = merge_points(found, weight[number, :, cols])
    matrix = side_matrix(targets, merged, step, (near, far), (target_near * BCOLS, target_far * BCOLS))
    copies[3].wait()
    for j, block in enumerate((near, far)):
        copies[4 + j].wait()
        diffuse(inverse[:, block, :].T, field.at[j], diffused.at[j])
    sums = spread([diffused.at[0], diffused.at[1]], matrix)
    rows_of(to_near)[...] = sums[:, :BCOLS]
    rows_of(to_far)[...] = sums[:, BCOLS:]


def level_pieces(levels):
    return [slice(levels * part // PIECES, levels * (part + 1) // PIECES) for part in range(PIECES)]


def piece_shapes(whole):
    return [
        jax.ShapeDtypeStruct((whole.shape[0], levels.stop - levels.start, *whole.shape[2:]), F32)
        for levels in level_pieces(whole.shape[1])
    ]


def store_pieces(sums, pieces, levels):
    for piece, part in zip(pieces, level_pieces(levels)):
        variables = piece.shape[2]
        rows = slice(part.start * variables, part.stop * variables)
        for j in range(REACH):
            rows_of(piece.at[j])[...] = sums[rows, j * BCOLS : (j + 1) * BCOLS]


def add_pieces(pieces, block, out):
    for piece, levels in zip(pieces, level_pieces(out.shape[0])):
        out[levels] += piece[block]


def blocks(like, *count):
    return jax.ShapeDtypeStruct((*count, *like.shape[-3:-1], BCOLS), F32)


def first(step, all_blocks, fields, inverses, routes, points, weights):
    one, two = blocks(fields), blocks(fields, REACH)
    return call(
        functools.partial(first_kernel, step, all_blocks),
        (fields, inverses, routes, points, weights),
        [HBM] * 5,
        (
            one,
            one,
            two,
            jax.ShapeDtypeStruct(inverses.shape[1:], F32),
            jax.ShapeDtypeStruct(points.shape, jnp.int32),
            jax.ShapeDtypeStruct(weights.shape, F32),
        ),
        (VMEM,) * 6,
        [
            pltpu.VMEM(two.shape, F32),
            pltpu.SMEM(routes.shape, jnp.int32),
            pltpu.VMEM(points.shape, jnp.int32),
            pltpu.VMEM(weights.shape, F32),
            pltpu.SemaphoreType.DMA((6,)),
        ],
        400_000_000,
        f"first_step{step}",
    )


def side_kernel(step, fields, inverse, targets, weights, inverses, diffused, turned, *refs):
    to_core, (field, next_inverse, sems) = refs[:-3], refs[-3:]
    block_count = inverse.shape[1]
    side, first_target = core_side(block_count)
    copies = start_copies(
        sems,
        [(fields.at[:, :, lanes(side + j)], field.at[j]) for j in range(REACH)]
        + [(inverses.at[step - 1], next_inverse)],
    )
    columns = (first_target * BCOLS, (first_target + 1) * BCOLS)
    matrix = side_matrix(targets, weights, step, (side, side + 1), columns)
    for j in range(REACH):
        copies[j].wait()
        diffuse(inverse[:, side + j, :].T, field.at[j], diffused.at[j])
    store_pieces(spread([diffused.at[j] for j in range(REACH)], matrix), to_core, field.shape[1])
    copies[REACH].wait()
    for j in range(block_count):
        turned[j] = next_inverse[:, j, :].T


def side(step, fields, inverse, targets, weights, inverses):
    two = blocks(fields, REACH)
    levels, block_count, _ = inverse.shape
    diffused, turned, *pieces = call(
        functools.partial(side_kernel, step),
        (fields, inverse, targets, weights, inverses),
        [HBM] + [VMEM] * 3 + [HBM],
        (two, jax.ShapeDtypeStruct((block_count, levels, levels), F32), *piece_shapes(two)),
        (VMEM,) * (2 + PIECES),
        [
            pltpu.VMEM(two.shape, F32),
            pltpu.VMEM(inverse.shape, F32),
            pltpu.SemaphoreType.DMA((REACH + 1,)),
        ],
        2_000_000_000,
        f"side_step{step}",
    )
    return diffused, turned, pieces


def inner_kernel(step, z_diffused, core_diffused, targets, weights, own, tall):
    block_count = own.shape[0]
    near, far, _, _ = z_blocks(block_count)
    first = core_side(block_count)[0]
    tall[near] = z_diffused[0]
    tall[far] = z_diffused[1]
    for j in range(REACH):
        tall[first + j] = core_diffused[j]
    matrix = spread_matrix(targets[step], weights[step], 0, block_count * BCOLS)
    sums = spread([tall.at[j] for j in range(block_count)], matrix)
    for j in range(block_count):
        rows_of(own.at[j])[...] = sums[:, j * BCOLS : (j + 1) * BCOLS]


def inner(step, z_diffused, core_diffused, targets, weights):
    whole = blocks(z_diffused, targets.shape[2] // BCOLS)
    return call(
        functools.partial(inner_kernel, step),
        (z_diffused, core_diffused, targets, weights),
        [VMEM] * 4,
        whole,
        VMEM,
        [pltpu.VMEM(whole.shape, F32)],
        2_000_000_000,
        f"inner_step{step}",
    )


def near_kernel(step, own, near_in, turned, targets, weights, to_far, to_near, diffused, field):
    block_count = own.shape[0]
    near, _, target_near, target_far = z_blocks(block_count)
    cols = lanes(near)
    field[...] = own[near] + near_in[...]
    diffuse(turned[near], field, diffused)
    halves = [
        spread_matrix(targets[step, :, cols], weights[step, :, cols], target * BCOLS)
        for target in (target_far, target_near)
    ]
    sums = spread([diffused], [jnp.concatenate(half, axis=0) for half in zip(*halves)])
    rows_of(to_far)[...] = sums[:, :BCOLS]
    rows_of(to_near)[...] = sums[:, BCOLS:]


def near(step, own, near_in, turned, targets, weights):
    one = blocks(own)
    return call(
        functools.partial(near_kernel, step),
        (own, near_in, turned, targets, weights),
        [VMEM] * 5,
        (one, one, one),
        (VMEM,) * 3,
        [pltpu.VMEM(one.shape, F32)],
        300_000_000,
        f"near_step{step}",
    )


def far_kernel(step, own, far_in, partial, turned, targets, weights, to_near, diffused, field):
    block_count = own.shape[0]
    _, far, target_near, _ = z_blocks(block_count)
    cols = lanes(far)
    field[...] = own[far] + far_in[...]
    diffuse(turned[far], field, diffused)
    matrix = spread_matrix(targets[step, :, cols], weights[step, :, cols], target_near * BCOLS)
    rows_of(to_near)[...] = rows_of(partial)[...] + spread([diffused], matrix)


def far(step, own, far_in, partial, turned, targets, weights):
    one = blocks(own)
    return call(
        functools.partial(far_kernel, step),
        (own, far_in, partial, turned, targets, weights),
        [VMEM] * 6,
        (one, one),
        (VMEM,) * 2,
        [pltpu.VMEM(one.shape, F32)],
        300_000_000,
        f"far_step{step}",
    )


def core_kernel(step, own, turned, targets, weights, _, *refs):
    core_in, (diffused, *to_core, field) = refs[:PIECES], refs[PIECES:]
    side, first_target = core_side(own.shape[0])
    columns = (first_target * BCOLS, (first_target + 1) * BCOLS)
    matrix = side_matrix(targets, weights, step, (side, side + 1), columns)
    for j in range(REACH):
        field[...] = own[side + j]
        add_pieces(core_in, j, field)
        diffuse(turned[side + j], field, diffused.at[j])
    store_pieces(spread([diffused.at[j] for j in range(REACH)], matrix), to_core, own.shape[1])


def core(step, own, turned, targets, weights, core_in, behind):
    one, two = blocks(own), blocks(own, REACH)
    diffused, *to_core = call(
        functools.partial(core_kernel, step),
        (own, turned, targets, weights, behind, *core_in),
        [VMEM] * 4 + [ANY] + [VMEM] * PIECES,
        (two, *piece_shapes(two)),
        (VMEM,) * (1 + PIECES),
        [pltpu.VMEM(one.shape, F32)],
        1,
        f"core_step{step}",
    )
    return diffused, to_core


def outer_kernel(
    step, own, near_in, far_in, diffused_core, diffused_near, diffused_far, targets, weights, *refs
):
    core_in, (sums, mid, field, tall, sems) = refs[:PIECES], refs[PIECES:]
    block_count = own.shape[0]
    near, far, _, _ = z_blocks(block_count)
    side = core_side(block_count)[0]
    for j in range(REACH):
        field[side + j] = own[side + j]
        add_pieces(core_in, j, field.at[side + j])
        tall[side + j] = diffused_core[j]
    field[near] = own[near] + near_in[...]
    field[far] = own[far] + far_in[...]
    tall[near] = diffused_near[...]
    tall[far] = diffused_far[...]
    copies = start_copies(sems, [(field.at[j], mid.at[:, :, lanes(j)]) for j in range(block_count)])
    matrix = spread_matrix(targets[step], weights[step], 0, block_count * BCOLS)
    total = spread([tall.at[j] for j in range(block_count)], matrix)
    for j in range(block_count):
        rows_of(sums.at[j])[...] = total[:, j * BCOLS : (j + 1) * BCOLS]
    for copy in copies:
        copy.wait()


def outer(step, own, near_in, far_in, core_in, diffused, targets, weights):
    block_count, levels, variables, _ = own.shape
    return call(
        functools.partial(outer_kernel, step),
        (own, near_in, far_in, *diffused, targets, weights, *core_in),
        [VMEM] * (8 + PIECES),
        (
            blocks(own, block_count),
            jax.ShapeDtypeStruct((levels, variables, block_count * BCOLS), F32),
        ),
        (VMEM, HBM),
        [
            pltpu.VMEM(own.shape, F32),
            pltpu.VMEM(own.shape, F32),
            pltpu.SemaphoreType.DMA((block_count,)),
        ],
        1,
        f"outer_step{step}",
    )


def squares(value):
    rows = value.reshape(value.shape[0] * value.shape[1], value.shape[2])
    return jnp.sum(rows * rows, axis=0, keepdims=True)


def most_kernel(own, far_in, *refs):
    core_in, (start, lane_sums) = refs[:PIECES], refs[PIECES:]
    block_count = own.shape[0]
    near, far, _, _ = z_blocks(block_count)
    side = core_side(block_count)[0]
    value = own[far] + far_in[...]
    start[far] = value
    start[near] = own[near]
    total = squares(value)
    for j in range(REACH):
        start[side + j] = own[side + j]
        add_pieces(core_in, j, start.at[side + j])
        total += squares(start[side + j])
    lane_sums[...] = total


def most(own, core_in, far_in):
    return call(
        most_kernel,
        (own, far_in, *core_in),
        [VMEM] * (2 + PIECES),
        (jax.ShapeDtypeStruct(own.shape, F32), jax.ShapeDtypeStruct((1, BCOLS), F32)),
        (VMEM, VMEM),
        [],
        1_000_000,
        "squares_of_most_blocks",
    )


def last_kernel(start, near_in, lane_sums, shares):
    near = z_blocks(start.shape[0])[0]
    shares[...] = lane_sums[...] + squares(start[near] + near_in[...])


def last(start, near_in, lane_sums):
    return call(
        last_kernel,
        (start, near_in, lane_sums),
        [VMEM] * 3,
        jax.ShapeDtypeStruct(lane_sums.shape, F32),
        VMEM,
        [],
        1_000_000,
        "squares_of_last_block",
    )


def scale_kernel(cells, start, near_in, *refs):
    *shares, out, held, sems = refs
    block_count = start.shape[0]
    near = z_blocks(block_count)[0]
    total = shares[0][...]
    for share in shares[1:]:
        total += share[...]
    energy = jnp.sum(total) / cells
    factor = 1.0 / jnp.sqrt(jnp.full((1, 1, 1), energy + eps_energy, F32))
    levels = start.shape[1]
    parts = 5
    copies = []
    for part in range(parts):
        rows = slice(levels * part // parts, levels * (part + 1) // parts)
        for j in range(block_count):
            cols = slice(j * BCOLS, (j + 1) * BCOLS)
            held[rows, :, cols] = (start[j, rows] + jnp.where(near == j, near_in[rows], 0.0)) * factor
        copies.append(pltpu.make_async_copy(held.at[rows], out.at[rows], sems.at[part]))
        copies[-1].start()
    for copy in copies:
        copy.wait()


def scale(start, near_in, shares, cells):
    return call(
        functools.partial(scale_kernel, cells),
        (start, near_in, *shares),
        [VMEM] * (2 + len(shares)),
        jax.ShapeDtypeStruct((*start.shape[1:3], start.shape[0] * BCOLS), F32),
        HBM,
        [pltpu.VMEM((*start.shape[1:3], start.shape[0] * BCOLS), F32), pltpu.SemaphoreType.DMA((5,))],
        1_000_000,
        "scale_start",
    )


def add_kernel(*refs):
    *parts, out = refs
    total = parts[0][...]
    for part in parts[1:]:
        total += part[...]
    out[...] = total


def add(parts):
    return call(
        add_kernel, parts, [VMEM] * len(parts), jax.ShapeDtypeStruct(parts[0].shape, F32), VMEM, [], 1, "add_shares"
    )


def share_out(share):
    count = lax.axis_size("col")
    if count != 8:
        return [lax.all_to_all(jnp.broadcast_to(share, (count, BCOLS)), "col", 0, 0, tiled=True)]
    share = add([share, core_exchange(share)])
    beside = lax.ppermute(share, "col", [(i, i ^ (6 if i % 2 else 6)) for i in range(count)])
    apart = lax.ppermute(share, "col", [(i, i ^ (4 if i % 2 else 2)) for i in range(count)])
    return [share, beside, apart, core_exchange(apart)]

def core_exchange(value):
    count = lax.axis_size("col")
    return lax.ppermute(value, "col", [(i, i ^ 1) for i in range(count)])


def z_exchange(value):
    count = lax.axis_size("col")
    pairs = [(i, (i + 1) % count if i % 2 else (i - 1) % count) for i in range(count)]
    return lax.ppermute(value, "col", pairs)


def shards(adj_final, inverses, dep_lists, dep_points, weights):
    count = lax.axis_size("col")
    all_blocks = count * inverses.shape[1]
    fields = jnp.transpose(adj_final, (1, 0, 2))
    inverses = jnp.transpose(inverses, (0, 2, 1, 3))
    fields, inverses, dep_lists, dep_points, weights = (
        pltpu.with_memory_space_constraint(value, pltpu.HBM)
        for value in (fields, inverses, dep_lists, dep_points, weights)
    )

    to_near, to_far, z_diffused, inverse, targets, merged = first(
        1, all_blocks, fields, inverses, dep_lists, dep_points, weights
    )
    near_in = z_exchange(to_near)
    far_in = z_exchange(to_far)
    core_diffused, turned, pieces = side(1, fields, inverse, targets, merged, inverses)
    core_in = [core_exchange(piece) for piece in pieces]
    own = inner(1, z_diffused, core_diffused, targets, merged)

    to_far, partial, diffused_near = near(0, own, near_in, turned, targets, merged)
    next_far_in = z_exchange(to_far)
    to_near, diffused_far = far(0, own, far_in, partial, turned, targets, merged)
    next_near_in = z_exchange(to_near)
    diffused_core, pieces = core(0, own, turned, targets, merged, core_in, to_near)
    next_core_in = [core_exchange(piece) for piece in pieces]
    diffused = (diffused_core, diffused_near, diffused_far)
    own, mid = outer(0, own, near_in, far_in, core_in, diffused, targets, merged)

    start, lane_sums = most(own, next_core_in, next_far_in)
    shares = share_out(last(start, next_near_in, lane_sums))
    lanczos = scale(start, next_near_in, shares, adj_final.size * count)
    return jnp.transpose(mid, (1, 0, 2)), jnp.transpose(lanczos, (1, 0, 2))


def solution(mesh):
    in_specs = (
        P("mem", None, "col"),
        P("mem", "col", None, None),
        P("mem", "col", None),
        P("mem", None, "col"),
        P("mem", None, "col"),
    )
    out_specs = (P("mem", None, "col"), P("mem", None, "col"))
    return jax.shard_map(shards, mesh=mesh, in_specs=in_specs, out_specs=out_specs, check_vma=False)
```

```python
import functools

import jax
import jax.numpy as jnp
from jax import lax
from jax.experimental import pallas as pl
from jax.experimental.pallas import tpu as pltpu
from jax.sharding import PartitionSpec as P

BCOLS = 128
REACH = 2
SLOTS = 5
POINTS = 4
STEPS = 2
VMEM_LIMIT = 32 * 1024 * 1024
NOWHERE = -(1 << 14)
PIECES = 3

eps_energy = 1e-06

F32 = jnp.float32
BF16 = jnp.bfloat16
ANY = pl.BlockSpec(memory_space=pl.ANY)
HBM = pl.BlockSpec(memory_space=pltpu.HBM)
VMEM = pl.BlockSpec(memory_space=pltpu.VMEM)


def z_blocks(block_count):
    follows = lax.rem(lax.axis_index("col"), 2)
    near = follows * (block_count - 1)
    away = 2 * follows - 1
    return near, near - away, near + away, near + 2 * away


def core_side(block_count):
    follows = 1 - lax.rem(lax.axis_index("col"), 2)
    return follows * (block_count - REACH), follows * (block_count + REACH) - REACH


def lanes(block, count=1):
    return pl.ds(pl.multiple_of(block * BCOLS, BCOLS), count * BCOLS)


def split(value):
    high = value.astype(BF16)
    return high, (value - high.astype(F32)).astype(BF16)


def target_columns(points, routes, step, block, block_count, all_blocks):
    slots = points // BCOLS
    here = lax.axis_index("col") * block_count + block
    found = jnp.zeros_like(points)
    for slot in range(SLOTS):
        offset = lax.rem(routes[step, block, slot] - here + REACH + all_blocks, all_blocks) - REACH
        found = jnp.where(slots == slot, (block + offset) * BCOLS, found)
    return found + points % BCOLS


def merge_points(targets, weights):
    targets = [targets[p : p + 1] for p in range(POINTS)]
    weights = [weights[p : p + 1] for p in range(POINTS)]
    for point in range(1, POINTS):
        for earlier in range(point):
            same = targets[point] == targets[earlier]
            weights[earlier] = weights[earlier] + jnp.where(same, weights[point], 0.0)
            targets[point] = jnp.where(same, NOWHERE, targets[point])
    return jnp.concatenate(targets, axis=0), jnp.concatenate(weights, axis=0)


def spread_matrix(targets, weights, first_column, rows=BCOLS):
    row = lax.broadcasted_iota(jnp.int32, (rows, targets.shape[1]), 0) + first_column
    total = jnp.zeros(row.shape, F32)
    for point in range(POINTS):
        total = jnp.where(row == targets[point : point + 1], weights[point : point + 1], total)
    return split(total)


def product(left, right, dims):
    return lax.dot_general(left, right, (dims, ((), ())), preferred_element_type=F32)


def rows_of(ref):
    levels, variables, columns = ref.shape
    return ref.reshape(levels * variables, columns)


def diffuse(turned, field, out):
    levels, variables, columns = field.shape
    source, result = rows_of(field), rows_of(out)
    every = [pl.ds(v, levels, stride=variables) for v in range(variables)]
    wide = split(jnp.concatenate([source[rows, :] for rows in every], axis=1))
    turned = split(turned)
    dims = ((1,), (0,))
    total = product(turned[0], wide[0], dims) + (
        product(turned[0], wide[1], dims) + product(turned[1], wide[0], dims)
    )
    for v, rows in enumerate(every):
        result[rows, :] = total[:, v * columns : (v + 1) * columns]


def spread(diffused, matrix):
    high, low = split(jnp.concatenate([rows_of(block)[...] for block in diffused], axis=1))
    left = jnp.concatenate([high, low, high], axis=1)
    right = jnp.concatenate([matrix[0], matrix[0], matrix[1]], axis=1)
    return product(left, right, ((1,), (1,)))


def side_matrix(targets, weights, step, blocks, first_columns):
    parts = []
    for block in blocks:
        cols = lanes(block)
        halves = [spread_matrix(targets[step, :, cols], weights[step, :, cols], column) for column in first_columns]
        parts.append([jnp.concatenate(half, axis=0) for half in zip(*halves)])
    return [jnp.concatenate(part, axis=1) for part in zip(*parts)]


def call(kernel, operands, in_specs, outs, out_specs, scratch, flops, name, limit=VMEM_LIMIT):
    return pl.pallas_call(
        kernel,
        out_shape=outs,
        in_specs=in_specs,
        out_specs=out_specs,
        scratch_shapes=scratch,
        compiler_params=pltpu.CompilerParams(vmem_limit_bytes=limit),
        cost_estimate=pl.CostEstimate(flops=flops, bytes_accessed=min(flops, 1_000_000), transcendentals=0),
        name=name,
    )(*operands)


def start_copies(sems, pairs):
    copies = [pltpu.make_async_copy(source, target, sems.at[i]) for i, (source, target) in enumerate(pairs)]
    for copy in copies:
        copy.start()
    return copies


def first_kernel(
    step, all_blocks, fields, inverses, routes, points, weights,
    to_near, to_far, diffused, targets, merged, field, inverse, route, point, weight, sems,
):
    block_count = inverses.shape[2]
    near, far, target_near, target_far = z_blocks(block_count)
    copies = start_copies(
        sems,
        [
            (routes, route),
            (points, point),
            (weights, weight),
            (inverses.at[step, :, near], inverse.at[0]),
            (inverses.at[step, :, far], inverse.at[1]),
            (fields.at[:, :, lanes(near)], field.at[0]),
            (fields.at[:, :, lanes(far)], field.at[1]),
        ],
    )
    for copy in copies[:3]:
        copy.wait()
    for number in range(STEPS):
        for j in range(block_count):
            cols = slice(j * BCOLS, (j + 1) * BCOLS)
            found = target_columns(point[number, :, cols], route, number, j, block_count, all_blocks)
            targets[number, :, cols], merged[number, :, cols] = merge_points(found, weight[number, :, cols])
    matrix = side_matrix(targets, merged, step, (near, far), (target_near * BCOLS, target_far * BCOLS))
    for copy in copies[3:5]:
        copy.wait()
    turned = [inverse[j].T for j in range(REACH)]
    for j in range(REACH):
        copies[5 + j].wait()
        diffuse(turned[j], field.at[j], diffused.at[j])
    sums = spread([diffused.at[0], diffused.at[1]], matrix)
    rows_of(to_near)[...] = sums[:, :BCOLS]
    rows_of(to_far)[...] = sums[:, BCOLS:]


def level_pieces(levels):
    return [slice(levels * part // PIECES, levels * (part + 1) // PIECES) for part in range(PIECES)]


def piece_shapes(whole):
    return [
        jax.ShapeDtypeStruct((whole.shape[0], levels.stop - levels.start, *whole.shape[2:]), F32)
        for levels in level_pieces(whole.shape[1])
    ]


def store_pieces(sums, pieces, levels):
    for piece, part in zip(pieces, level_pieces(levels)):
        variables = piece.shape[2]
        rows = slice(part.start * variables, part.stop * variables)
        for j in range(REACH):
            rows_of(piece.at[j])[...] = sums[rows, j * BCOLS : (j + 1) * BCOLS]


def add_pieces(pieces, block, out):
    for piece, levels in zip(pieces, level_pieces(out.shape[0])):
        out[levels] += piece[block]


def blocks(like, *count):
    return jax.ShapeDtypeStruct((*count, *like.shape[-3:-1], BCOLS), F32)


def first(step, all_blocks, fields, inverses, routes, points, weights):
    one, two = blocks(fields), blocks(fields, REACH)
    return call(
        functools.partial(first_kernel, step, all_blocks),
        (fields, inverses, routes, points, weights),
        [HBM] * 5,
        (
            one,
            one,
            two,
            jax.ShapeDtypeStruct(points.shape, jnp.int32),
            jax.ShapeDtypeStruct(weights.shape, F32),
        ),
        (VMEM,) * 5,
        [
            pltpu.VMEM(two.shape, F32),
            pltpu.VMEM((REACH, inverses.shape[1], inverses.shape[3]), F32),
            pltpu.SMEM(routes.shape, jnp.int32),
            pltpu.VMEM(points.shape, jnp.int32),
            pltpu.VMEM(weights.shape, F32),
            pltpu.SemaphoreType.DMA((7,)),
        ],
        400_000_000,
        f"first_step{step}",
    )


def side_kernel(step, fields, targets, weights, inverses, diffused, turned, *refs):
    to_core, (field, inverse, next_inverse, sems) = refs[:-4], refs[-4:]
    block_count = inverse.shape[1]
    side, first_target = core_side(block_count)
    copies = start_copies(
        sems,
        [(fields.at[:, :, lanes(side + j)], field.at[j]) for j in range(REACH)]
        + [(inverses.at[step], inverse), (inverses.at[step - 1], next_inverse)],
    )
    columns = (first_target * BCOLS, (first_target + 1) * BCOLS)
    matrix = side_matrix(targets, weights, step, (side, side + 1), columns)
    copies[REACH].wait()
    for j in range(REACH):
        copies[j].wait()
        diffuse(inverse[:, side + j, :].T, field.at[j], diffused.at[j])
    store_pieces(spread([diffused.at[j] for j in range(REACH)], matrix), to_core, field.shape[1])
    copies[REACH + 1].wait()
    for j in range(block_count):
        turned[j] = next_inverse[:, j, :].T


def side(step, fields, targets, weights, inverses):
    two = blocks(fields, REACH)
    _, levels, block_count, _ = inverses.shape
    diffused, turned, *pieces = call(
        functools.partial(side_kernel, step),
        (fields, targets, weights, inverses),
        [HBM] + [VMEM] * 2 + [HBM],
        (two, jax.ShapeDtypeStruct((block_count, levels, levels), F32), *piece_shapes(two)),
        (VMEM,) * (2 + PIECES),
        [
            pltpu.VMEM(two.shape, F32),
            pltpu.VMEM(inverses.shape[1:], F32),
            pltpu.VMEM(inverses.shape[1:], F32),
            pltpu.SemaphoreType.DMA((REACH + 2,)),
        ],
        2_000_000_000,
        f"side_step{step}",
    )
    return diffused, turned, pieces


def inner_kernel(step, z_diffused, core_diffused, targets, weights, own, tall):
    block_count = own.shape[0]
    near, far, _, _ = z_blocks(block_count)
    first = core_side(block_count)[0]
    tall[near] = z_diffused[0]
    tall[far] = z_diffused[1]
    for j in range(REACH):
        tall[first + j] = core_diffused[j]
    matrix = spread_matrix(targets[step], weights[step], 0, block_count * BCOLS)
    sums = spread([tall.at[j] for j in range(block_count)], matrix)
    for j in range(block_count):
        rows_of(own.at[j])[...] = sums[:, j * BCOLS : (j + 1) * BCOLS]


def inner(step, z_diffused, core_diffused, targets, weights):
    whole = blocks(z_diffused, targets.shape[2] // BCOLS)
    return call(
        functools.partial(inner_kernel, step),
        (z_diffused, core_diffused, targets, weights),
        [VMEM] * 4,
        whole,
        VMEM,
        [pltpu.VMEM(whole.shape, F32)],
        2_000_000_000,
        f"inner_step{step}",
    )


def near_kernel(step, own, near_in, turned, targets, weights, to_far, to_near, diffused, field):
    block_count = own.shape[0]
    near, _, target_near, target_far = z_blocks(block_count)
    cols = lanes(near)
    field[...] = own[near] + near_in[...]
    diffuse(turned[near], field, diffused)
    halves = [
        spread_matrix(targets[step, :, cols], weights[step, :, cols], target * BCOLS)
        for target in (target_far, target_near)
    ]
    sums = spread([diffused], [jnp.concatenate(half, axis=0) for half in zip(*halves)])
    rows_of(to_far)[...] = sums[:, :BCOLS]
    rows_of(to_near)[...] = sums[:, BCOLS:]


def near(step, own, near_in, turned, targets, weights):
    one = blocks(own)
    return call(
        functools.partial(near_kernel, step),
        (own, near_in, turned, targets, weights),
        [VMEM] * 5,
        (one, one, one),
        (VMEM,) * 3,
        [pltpu.VMEM(one.shape, F32)],
        300_000_000,
        f"near_step{step}",
    )


def far_kernel(step, own, far_in, partial, turned, targets, weights, to_near, diffused, field):
    block_count = own.shape[0]
    _, far, target_near, _ = z_blocks(block_count)
    cols = lanes(far)
    field[...] = own[far] + far_in[...]
    diffuse(turned[far], field, diffused)
    matrix = spread_matrix(targets[step, :, cols], weights[step, :, cols], target_near * BCOLS)
    rows_of(to_near)[...] = rows_of(partial)[...] + spread([diffused], matrix)


def far(step, own, far_in, partial, turned, targets, weights):
    one = blocks(own)
    return call(
        functools.partial(far_kernel, step),
        (own, far_in, partial, turned, targets, weights),
        [VMEM] * 6,
        (one, one),
        (VMEM,) * 2,
        [pltpu.VMEM(one.shape, F32)],
        300_000_000,
        f"far_step{step}",
    )


def core_kernel(step, own, turned, targets, weights, _, *refs):
    core_in, (diffused, *to_core, field) = refs[:PIECES], refs[PIECES:]
    side, first_target = core_side(own.shape[0])
    columns = (first_target * BCOLS, (first_target + 1) * BCOLS)
    matrix = side_matrix(targets, weights, step, (side, side + 1), columns)
    for j in range(REACH):
        field[...] = own[side + j]
        add_pieces(core_in, j, field)
        diffuse(turned[side + j], field, diffused.at[j])
    store_pieces(spread([diffused.at[j] for j in range(REACH)], matrix), to_core, own.shape[1])


def core(step, own, turned, targets, weights, core_in, behind):
    one, two = blocks(own), blocks(own, REACH)
    diffused, *to_core = call(
        functools.partial(core_kernel, step),
        (own, turned, targets, weights, behind, *core_in),
        [VMEM] * 4 + [ANY] + [VMEM] * PIECES,
        (two, *piece_shapes(two)),
        (VMEM,) * (1 + PIECES),
        [pltpu.VMEM(one.shape, F32)],
        1,
        f"core_step{step}",
    )
    return diffused, to_core


def outer_kernel(
    step, own, near_in, far_in, diffused_core, diffused_near, diffused_far, targets, weights, *refs
):
    core_in, (sums, mid, field, tall, sems) = refs[:PIECES], refs[PIECES:]
    block_count = own.shape[0]
    near, far, _, _ = z_blocks(block_count)
    side = core_side(block_count)[0]
    for j in range(REACH):
        field[side + j] = own[side + j]
        add_pieces(core_in, j, field.at[side + j])
        tall[side + j] = diffused_core[j]
    field[near] = own[near] + near_in[...]
    field[far] = own[far] + far_in[...]
    tall[near] = diffused_near[...]
    tall[far] = diffused_far[...]
    copies = start_copies(sems, [(field.at[j], mid.at[:, :, lanes(j)]) for j in range(block_count)])
    matrix = spread_matrix(targets[step], weights[step], 0, block_count * BCOLS)
    total = spread([tall.at[j] for j in range(block_count)], matrix)
    for j in range(block_count):
        rows_of(sums.at[j])[...] = total[:, j * BCOLS : (j + 1) * BCOLS]
    for copy in copies:
        copy.wait()


def outer(step, own, near_in, far_in, core_in, diffused, targets, weights):
    block_count, levels, variables, _ = own.shape
    return call(
        functools.partial(outer_kernel, step),
        (own, near_in, far_in, *diffused, targets, weights, *core_in),
        [VMEM] * (8 + PIECES),
        (
            blocks(own, block_count),
            jax.ShapeDtypeStruct((levels, variables, block_count * BCOLS), F32),
        ),
        (VMEM, HBM),
        [
            pltpu.VMEM(own.shape, F32),
            pltpu.VMEM(own.shape, F32),
            pltpu.SemaphoreType.DMA((block_count,)),
        ],
        1,
        f"outer_step{step}",
    )


def squares(value):
    rows = value.reshape(value.shape[0] * value.shape[1], value.shape[2])
    return jnp.sum(rows * rows, axis=0, keepdims=True)


def most_kernel(own, far_in, *refs):
    core_in, (start, lane_sums) = refs[:PIECES], refs[PIECES:]
    block_count = own.shape[0]
    near, far, _, _ = z_blocks(block_count)
    side = core_side(block_count)[0]
    value = own[far] + far_in[...]
    start[far] = value
    start[near] = own[near]
    total = squares(value)
    for j in range(REACH):
        start[side + j] = own[side + j]
        add_pieces(core_in, j, start.at[side + j])
        total += squares(start[side + j])
    lane_sums[...] = total


def most(own, core_in, far_in):
    return call(
        most_kernel,
        (own, far_in, *core_in),
        [VMEM] * (2 + PIECES),
        (jax.ShapeDtypeStruct(own.shape, F32), jax.ShapeDtypeStruct((1, BCOLS), F32)),
        (VMEM, VMEM),
        [],
        1_000_000,
        "squares_of_most_blocks",
    )


def last_kernel(start, near_in, lane_sums, shares):
    near = z_blocks(start.shape[0])[0]
    shares[...] = lane_sums[...] + squares(start[near] + near_in[...])


def last(start, near_in, lane_sums):
    return call(
        last_kernel,
        (start, near_in, lane_sums),
        [VMEM] * 3,
        jax.ShapeDtypeStruct(lane_sums.shape, F32),
        VMEM,
        [],
        1_000_000,
        "squares_of_last_block",
    )


def scale_kernel(cells, start, near_in, *refs):
    *shares, out, held, sems = refs
    block_count = start.shape[0]
    near = z_blocks(block_count)[0]
    total = shares[0][...]
    for share in shares[1:]:
        total += share[...]
    energy = jnp.sum(total) / cells
    factor = 1.0 / jnp.sqrt(jnp.full((1, 1, 1), energy + eps_energy, F32))
    levels = start.shape[1]
    parts = 5
    copies = []
    for part in range(parts):
        rows = slice(levels * part // parts, levels * (part + 1) // parts)
        for j in range(block_count):
            cols = slice(j * BCOLS, (j + 1) * BCOLS)
            held[rows, :, cols] = (start[j, rows] + jnp.where(near == j, near_in[rows], 0.0)) * factor
        copies.append(pltpu.make_async_copy(held.at[rows], out.at[rows], sems.at[part]))
        copies[-1].start()
    for copy in copies:
        copy.wait()


def scale(start, near_in, shares, cells):
    return call(
        functools.partial(scale_kernel, cells),
        (start, near_in, *shares),
        [VMEM] * (2 + len(shares)),
        jax.ShapeDtypeStruct((*start.shape[1:3], start.shape[0] * BCOLS), F32),
        HBM,
        [pltpu.VMEM((*start.shape[1:3], start.shape[0] * BCOLS), F32), pltpu.SemaphoreType.DMA((5,))],
        1_000_000,
        "scale_start",
    )


def add_kernel(*refs):
    *parts, out = refs
    total = parts[0][...]
    for part in parts[1:]:
        total += part[...]
    out[...] = total


def add(parts):
    return call(
        add_kernel, parts, [VMEM] * len(parts), jax.ShapeDtypeStruct(parts[0].shape, F32), VMEM, [], 1, "add_shares"
    )


def share_out(share):
    count = lax.axis_size("col")
    if count != 8:
        return [lax.all_to_all(jnp.broadcast_to(share, (count, BCOLS)), "col", 0, 0, tiled=True)]
    share = add([share, core_exchange(share)])
    beside = lax.ppermute(share, "col", [(i, (i - 2) % count) for i in range(count)])
    apart = lax.ppermute(share, "col", [(i, (i + 2) % count if i % 2 else i ^ 4) for i in range(count)])
    return [share, beside, apart, core_exchange(apart)]

def core_exchange(value):
    count = lax.axis_size("col")
    return lax.ppermute(value, "col", [(i, i ^ 1) for i in range(count)])


def z_exchange(value):
    count = lax.axis_size("col")
    pairs = [(i, (i + 1) % count if i % 2 else (i - 1) % count) for i in range(count)]
    return lax.ppermute(value, "col", pairs)


def shards(adj_final, inverses, dep_lists, dep_points, weights):
    count = lax.axis_size("col")
    all_blocks = count * inverses.shape[1]
    fields = jnp.transpose(adj_final, (1, 0, 2))
    inverses = jnp.transpose(inverses, (0, 2, 1, 3))
    fields, inverses, dep_lists, dep_points, weights = (
        pltpu.with_memory_space_constraint(value, pltpu.HBM)
        for value in (fields, inverses, dep_lists, dep_points, weights)
    )

    to_near, to_far, z_diffused, targets, merged = first(
        1, all_blocks, fields, inverses, dep_lists, dep_points, weights
    )
    near_in = z_exchange(to_near)
    far_in = z_exchange(to_far)
    core_diffused, turned, pieces = side(1, fields, targets, merged, inverses)
    core_in = [core_exchange(piece) for piece in pieces]
    own = inner(1, z_diffused, core_diffused, targets, merged)

    to_far, partial, diffused_near = near(0, own, near_in, turned, targets, merged)
    next_far_in = z_exchange(to_far)
    to_near, diffused_far = far(0, own, far_in, partial, turned, targets, merged)
    next_near_in = z_exchange(to_near)
    diffused_core, pieces = core(0, own, turned, targets, merged, core_in, to_near)
    next_core_in = [core_exchange(piece) for piece in pieces]
    diffused = (diffused_core, diffused_near, diffused_far)
    own, mid = outer(0, own, near_in, far_in, core_in, diffused, targets, merged)

    start, lane_sums = most(own, next_core_in, next_far_in)
    shares = share_out(last(start, next_near_in, lane_sums))
    lanczos = scale(start, next_near_in, shares, adj_final.size * count)
    return jnp.transpose(mid, (1, 0, 2)), jnp.transpose(lanczos, (1, 0, 2))


def solution(mesh):
    in_specs = (
        P("mem", None, "col"),
        P("mem", "col", None, None),
        P("mem", "col", None),
        P("mem", None, "col"),
        P("mem", None, "col"),
    )
    out_specs = (P("mem", None, "col"), P("mem", None, "col"))
    return jax.shard_map(shards, mesh=mesh, in_specs=in_specs, out_specs=out_specs, check_vma=False)
```

```python
import functools

import jax
import jax.numpy as jnp
from jax import lax
from jax.experimental import pallas as pl
from jax.experimental.pallas import tpu as pltpu
from jax.sharding import PartitionSpec as P

BCOLS = 128
REACH = 2
SLOTS = 5
POINTS = 4
STEPS = 2
VMEM_LIMIT = 32 * 1024 * 1024
NOWHERE = -(1 << 14)
PIECES = 3

eps_energy = 1e-06

F32 = jnp.float32
BF16 = jnp.bfloat16
ANY = pl.BlockSpec(memory_space=pl.ANY)
HBM = pl.BlockSpec(memory_space=pltpu.HBM)
VMEM = pl.BlockSpec(memory_space=pltpu.VMEM)


def z_blocks(block_count):
    follows = lax.rem(lax.axis_index("col"), 2)
    near = follows * (block_count - 1)
    away = 2 * follows - 1
    return near, near - away, near + away, near + 2 * away


def core_side(block_count):
    follows = 1 - lax.rem(lax.axis_index("col"), 2)
    return follows * (block_count - REACH), follows * (block_count + REACH) - REACH


def lanes(block, count=1):
    return pl.ds(pl.multiple_of(block * BCOLS, BCOLS), count * BCOLS)


def split(value):
    high = value.astype(BF16)
    return high, (value - high.astype(F32)).astype(BF16)


def target_columns(points, routes, step, block, block_count, all_blocks):
    slots = points // BCOLS
    here = lax.axis_index("col") * block_count + block
    found = jnp.zeros_like(points)
    for slot in range(SLOTS):
        offset = lax.rem(routes[step, block, slot] - here + REACH + all_blocks, all_blocks) - REACH
        found = jnp.where(slots == slot, (block + offset) * BCOLS, found)
    return found + points % BCOLS


def merge_points(targets, weights):
    targets = [targets[p : p + 1] for p in range(POINTS)]
    weights = [weights[p : p + 1] for p in range(POINTS)]
    for point in range(1, POINTS):
        for earlier in range(point):
            same = targets[point] == targets[earlier]
            weights[earlier] = weights[earlier] + jnp.where(same, weights[point], 0.0)
            targets[point] = jnp.where(same, NOWHERE, targets[point])
    return jnp.concatenate(targets, axis=0), jnp.concatenate(weights, axis=0)


def spread_matrix(targets, weights, first_column, rows=BCOLS):
    row = lax.broadcasted_iota(jnp.int32, (rows, targets.shape[1]), 0) + first_column
    total = jnp.zeros(row.shape, F32)
    for point in range(POINTS):
        total = jnp.where(row == targets[point : point + 1], weights[point : point + 1], total)
    return split(total)


def product(left, right, dims):
    return lax.dot_general(left, right, (dims, ((), ())), preferred_element_type=F32)


def rows_of(ref):
    levels, variables, columns = ref.shape
    return ref.reshape(levels * variables, columns)


def diffuse(turned, field, out):
    levels, variables, columns = field.shape
    source, result = rows_of(field), rows_of(out)
    every = [pl.ds(v, levels, stride=variables) for v in range(variables)]
    wide = split(jnp.concatenate([source[rows, :] for rows in every], axis=1))
    turned = split(turned)
    dims = ((1,), (0,))
    total = product(turned[0], wide[0], dims) + (
        product(turned[0], wide[1], dims) + product(turned[1], wide[0], dims)
    )
    for v, rows in enumerate(every):
        result[rows, :] = total[:, v * columns : (v + 1) * columns]


def spread(diffused, matrix):
    high, low = split(jnp.concatenate([rows_of(block)[...] for block in diffused], axis=1))
    left = jnp.concatenate([high, low, high], axis=1)
    right = jnp.concatenate([matrix[0], matrix[0], matrix[1]], axis=1)
    return product(left, right, ((1,), (1,)))


def side_matrix(targets, weights, step, blocks, first_columns):
    parts = []
    for block in blocks:
        cols = lanes(block)
        halves = [spread_matrix(targets[step, :, cols], weights[step, :, cols], column) for column in first_columns]
        parts.append([jnp.concatenate(half, axis=0) for half in zip(*halves)])
    return [jnp.concatenate(part, axis=1) for part in zip(*parts)]


def call(kernel, operands, in_specs, outs, out_specs, scratch, flops, name, limit=VMEM_LIMIT):
    return pl.pallas_call(
        kernel,
        out_shape=outs,
        in_specs=in_specs,
        out_specs=out_specs,
        scratch_shapes=scratch,
        compiler_params=pltpu.CompilerParams(vmem_limit_bytes=limit),
        cost_estimate=pl.CostEstimate(flops=flops, bytes_accessed=min(flops, 1_000_000), transcendentals=0),
        name=name,
    )(*operands)


def start_copies(sems, pairs):
    copies = [pltpu.make_async_copy(source, target, sems.at[i]) for i, (source, target) in enumerate(pairs)]
    for copy in copies:
        copy.start()
    return copies


def first_kernel(
    step, all_blocks, fields, inverses, routes, points, weights,
    to_near, to_far, diffused, targets, merged, field, inverse, route, point, weight, sems,
):
    block_count = inverses.shape[2]
    near, far, target_near, target_far = z_blocks(block_count)
    copies = start_copies(
        sems,
        [
            (routes, route),
            (points, point),
            (weights, weight),
            (inverses.at[step, :, near], inverse.at[0]),
            (inverses.at[step, :, far], inverse.at[1]),
            (fields.at[:, :, lanes(near)], field.at[0]),
            (fields.at[:, :, lanes(far)], field.at[1]),
        ],
    )
    for copy in copies[:3]:
        copy.wait()
    for number in range(STEPS):
        for j in range(block_count):
            cols = slice(j * BCOLS, (j + 1) * BCOLS)
            found = target_columns(point[number, :, cols], route, number, j, block_count, all_blocks)
            targets[number, :, cols], merged[number, :, cols] = merge_points(found, weight[number, :, cols])
    matrix = side_matrix(targets, merged, step, (near, far), (target_near * BCOLS, target_far * BCOLS))
    for copy in copies[3:5]:
        copy.wait()
    turned = [inverse[j].T for j in range(REACH)]
    for j in range(REACH):
        copies[5 + j].wait()
        diffuse(turned[j], field.at[j], diffused.at[j])
    sums = spread([diffused.at[0], diffused.at[1]], matrix)
    rows_of(to_near)[...] = sums[:, :BCOLS]
    rows_of(to_far)[...] = sums[:, BCOLS:]


def level_pieces(levels):
    return [slice(levels * part // PIECES, levels * (part + 1) // PIECES) for part in range(PIECES)]


def piece_shapes(whole):
    return [
        jax.ShapeDtypeStruct((whole.shape[0], levels.stop - levels.start, *whole.shape[2:]), F32)
        for levels in level_pieces(whole.shape[1])
    ]


def store_pieces(sums, pieces, levels):
    for piece, part in zip(pieces, level_pieces(levels)):
        variables = piece.shape[2]
        rows = slice(part.start * variables, part.stop * variables)
        for j in range(REACH):
            rows_of(piece.at[j])[...] = sums[rows, j * BCOLS : (j + 1) * BCOLS]


def add_pieces(pieces, block, out):
    for piece, levels in zip(pieces, level_pieces(out.shape[0])):
        out[levels] += piece[block]


def blocks(like, *count):
    return jax.ShapeDtypeStruct((*count, *like.shape[-3:-1], BCOLS), F32)


def first(step, all_blocks, fields, inverses, routes, points, weights):
    one, two = blocks(fields), blocks(fields, REACH)
    return call(
        functools.partial(first_kernel, step, all_blocks),
        (fields, inverses, routes, points, weights),
        [HBM] * 5,
        (
            one,
            one,
            two,
            jax.ShapeDtypeStruct(points.shape, jnp.int32),
            jax.ShapeDtypeStruct(weights.shape, F32),
        ),
        (VMEM,) * 5,
        [
            pltpu.VMEM(two.shape, F32),
            pltpu.VMEM((REACH, inverses.shape[1], inverses.shape[3]), F32),
            pltpu.SMEM(routes.shape, jnp.int32),
            pltpu.VMEM(points.shape, jnp.int32),
            pltpu.VMEM(weights.shape, F32),
            pltpu.SemaphoreType.DMA((7,)),
        ],
        400_000_000,
        f"first_step{step}",
    )


def side_kernel(step, fields, targets, weights, inverses, diffused, turned, *refs):
    to_core, (field, inverse, next_inverse, sems) = refs[:-4], refs[-4:]
    block_count = inverse.shape[1]
    side, first_target = core_side(block_count)
    copies = start_copies(
        sems,
        [(fields.at[:, :, lanes(side + j)], field.at[j]) for j in range(REACH)]
        + [(inverses.at[step], inverse), (inverses.at[step - 1], next_inverse)],
    )
    columns = (first_target * BCOLS, (first_target + 1) * BCOLS)
    matrix = side_matrix(targets, weights, step, (side, side + 1), columns)
    copies[REACH].wait()
    for j in range(REACH):
        copies[j].wait()
        diffuse(inverse[:, side + j, :].T, field.at[j], diffused.at[j])
    store_pieces(spread([diffused.at[j] for j in range(REACH)], matrix), to_core, field.shape[1])
    copies[REACH + 1].wait()
    for j in range(block_count):
        turned[j] = next_inverse[:, j, :].T


def side(step, fields, targets, weights, inverses):
    two = blocks(fields, REACH)
    _, levels, block_count, _ = inverses.shape
    diffused, turned, *pieces = call(
        functools.partial(side_kernel, step),
        (fields, targets, weights, inverses),
        [HBM] + [VMEM] * 2 + [HBM],
        (two, jax.ShapeDtypeStruct((block_count, levels, levels), F32), *piece_shapes(two)),
        (VMEM,) * (2 + PIECES),
        [
            pltpu.VMEM(two.shape, F32),
            pltpu.VMEM(inverses.shape[1:], F32),
            pltpu.VMEM(inverses.shape[1:], F32),
            pltpu.SemaphoreType.DMA((REACH + 2,)),
        ],
        2_000_000_000,
        f"side_step{step}",
    )
    return diffused, turned, pieces


def inner_kernel(step, z_diffused, core_diffused, targets, weights, own, tall):
    block_count = own.shape[0]
    near, far, _, _ = z_blocks(block_count)
    first = core_side(block_count)[0]
    tall[near] = z_diffused[0]
    tall[far] = z_diffused[1]
    for j in range(REACH):
        tall[first + j] = core_diffused[j]
    matrix = spread_matrix(targets[step], weights[step], 0, block_count * BCOLS)
    sums = spread([tall.at[j] for j in range(block_count)], matrix)
    for j in range(block_count):
        rows_of(own.at[j])[...] = sums[:, j * BCOLS : (j + 1) * BCOLS]


def inner(step, z_diffused, core_diffused, targets, weights):
    whole = blocks(z_diffused, targets.shape[2] // BCOLS)
    return call(
        functools.partial(inner_kernel, step),
        (z_diffused, core_diffused, targets, weights),
        [VMEM] * 4,
        whole,
        VMEM,
        [pltpu.VMEM(whole.shape, F32)],
        2_000_000_000,
        f"inner_step{step}",
    )


def near_kernel(step, own, near_in, turned, targets, weights, to_far, to_near, diffused, field):
    block_count = own.shape[0]
    near, _, target_near, target_far = z_blocks(block_count)
    cols = lanes(near)
    field[...] = own[near] + near_in[...]
    diffuse(turned[near], field, diffused)
    halves = [
        spread_matrix(targets[step, :, cols], weights[step, :, cols], target * BCOLS)
        for target in (target_far, target_near)
    ]
    sums = spread([diffused], [jnp.concatenate(half, axis=0) for half in zip(*halves)])
    rows_of(to_far)[...] = sums[:, :BCOLS]
    rows_of(to_near)[...] = sums[:, BCOLS:]


def near(step, own, near_in, turned, targets, weights):
    one = blocks(own)
    return call(
        functools.partial(near_kernel, step),
        (own, near_in, turned, targets, weights),
        [VMEM] * 5,
        (one, one, one),
        (VMEM,) * 3,
        [pltpu.VMEM(one.shape, F32)],
        300_000_000,
        f"near_step{step}",
    )


def far_kernel(step, own, far_in, partial, turned, targets, weights, to_near, diffused, field):
    block_count = own.shape[0]
    _, far, target_near, _ = z_blocks(block_count)
    cols = lanes(far)
    field[...] = own[far] + far_in[...]
    diffuse(turned[far], field, diffused)
    matrix = spread_matrix(targets[step, :, cols], weights[step, :, cols], target_near * BCOLS)
    rows_of(to_near)[...] = rows_of(partial)[...] + spread([diffused], matrix)


def far(step, own, far_in, partial, turned, targets, weights):
    one = blocks(own)
    return call(
        functools.partial(far_kernel, step),
        (own, far_in, partial, turned, targets, weights),
        [VMEM] * 6,
        (one, one),
        (VMEM,) * 2,
        [pltpu.VMEM(one.shape, F32)],
        300_000_000,
        f"far_step{step}",
    )


def core_kernel(step, own, turned, targets, weights, _, *refs):
    core_in, (diffused, *to_core, field) = refs[:PIECES], refs[PIECES:]
    side, first_target = core_side(own.shape[0])
    columns = (first_target * BCOLS, (first_target + 1) * BCOLS)
    matrix = side_matrix(targets, weights, step, (side, side + 1), columns)
    for j in range(REACH):
        field[...] = own[side + j]
        add_pieces(core_in, j, field)
        diffuse(turned[side + j], field, diffused.at[j])
    store_pieces(spread([diffused.at[j] for j in range(REACH)], matrix), to_core, own.shape[1])


def core(step, own, turned, targets, weights, core_in, behind):
    one, two = blocks(own), blocks(own, REACH)
    diffused, *to_core = call(
        functools.partial(core_kernel, step),
        (own, turned, targets, weights, behind, *core_in),
        [VMEM] * 4 + [ANY] + [VMEM] * PIECES,
        (two, *piece_shapes(two)),
        (VMEM,) * (1 + PIECES),
        [pltpu.VMEM(one.shape, F32)],
        1,
        f"core_step{step}",
    )
    return diffused, to_core


def outer_kernel(
    step, own, near_in, far_in, diffused_core, diffused_near, diffused_far, targets, weights, *refs
):
    core_in, (sums, mid, field, tall, sems) = refs[:PIECES], refs[PIECES:]
    block_count = own.shape[0]
    near, far, _, _ = z_blocks(block_count)
    side = core_side(block_count)[0]
    for j in range(REACH):
        field[side + j] = own[side + j]
        add_pieces(core_in, j, field.at[side + j])
        tall[side + j] = diffused_core[j]
    field[near] = own[near] + near_in[...]
    field[far] = own[far] + far_in[...]
    tall[near] = diffused_near[...]
    tall[far] = diffused_far[...]
    copies = start_copies(sems, [(field.at[j], mid.at[:, :, lanes(j)]) for j in range(block_count)])
    matrix = spread_matrix(targets[step], weights[step], 0, block_count * BCOLS)
    total = spread([tall.at[j] for j in range(block_count)], matrix)
    for j in range(block_count):
        rows_of(sums.at[j])[...] = total[:, j * BCOLS : (j + 1) * BCOLS]
    for copy in copies:
        copy.wait()


def outer(step, own, near_in, far_in, core_in, diffused, targets, weights):
    block_count, levels, variables, _ = own.shape
    return call(
        functools.partial(outer_kernel, step),
        (own, near_in, far_in, *diffused, targets, weights, *core_in),
        [VMEM] * (8 + PIECES),
        (
            blocks(own, block_count),
            jax.ShapeDtypeStruct((levels, variables, block_count * BCOLS), F32),
        ),
        (VMEM, HBM),
        [
            pltpu.VMEM(own.shape, F32),
            pltpu.VMEM(own.shape, F32),
            pltpu.SemaphoreType.DMA((block_count,)),
        ],
        1,
        f"outer_step{step}",
    )


def squares(value):
    rows = value.reshape(value.shape[0] * value.shape[1], value.shape[2])
    return jnp.sum(rows * rows, axis=0, keepdims=True)


def most_kernel(own, far_in, *refs):
    core_in, (start, lane_sums) = refs[:PIECES], refs[PIECES:]
    block_count = own.shape[0]
    near, far, _, _ = z_blocks(block_count)
    side = core_side(block_count)[0]
    value = own[far] + far_in[...]
    start[far] = value
    start[near] = own[near]
    total = squares(value)
    for j in range(REACH):
        start[side + j] = own[side + j]
        add_pieces(core_in, j, start.at[side + j])
        total += squares(start[side + j])
    lane_sums[...] = total


def most(own, core_in, far_in):
    return call(
        most_kernel,
        (own, far_in, *core_in),
        [VMEM] * (2 + PIECES),
        (jax.ShapeDtypeStruct(own.shape, F32), jax.ShapeDtypeStruct((1, BCOLS), F32)),
        (VMEM, VMEM),
        [],
        1_000_000,
        "squares_of_most_blocks",
    )


def last_kernel(start, near_in, lane_sums, shares):
    near = z_blocks(start.shape[0])[0]
    shares[...] = lane_sums[...] + squares(start[near] + near_in[...])


def last(start, near_in, lane_sums):
    return call(
        last_kernel,
        (start, near_in, lane_sums),
        [VMEM] * 3,
        jax.ShapeDtypeStruct(lane_sums.shape, F32),
        VMEM,
        [],
        1_000_000,
        "squares_of_last_block",
    )


def scale_kernel(cells, start, near_in, *refs):
    *shares, out, held, sems = refs
    block_count = start.shape[0]
    near = z_blocks(block_count)[0]
    total = shares[0][...]
    for share in shares[1:]:
        total += share[...]
    energy = jnp.sum(total) / cells
    factor = 1.0 / jnp.sqrt(jnp.full((1, 1, 1), energy + eps_energy, F32))
    levels = start.shape[1]
    parts = 5
    copies = []
    for part in range(parts):
        rows = slice(levels * part // parts, levels * (part + 1) // parts)
        for j in range(block_count):
            cols = slice(j * BCOLS, (j + 1) * BCOLS)
            held[rows, :, cols] = (start[j, rows] + jnp.where(near == j, near_in[rows], 0.0)) * factor
        copies.append(pltpu.make_async_copy(held.at[rows], out.at[rows], sems.at[part]))
        copies[-1].start()
    for copy in copies:
        copy.wait()


def scale(start, near_in, shares, cells):
    return call(
        functools.partial(scale_kernel, cells),
        (start, near_in, *shares),
        [VMEM] * (2 + len(shares)),
        jax.ShapeDtypeStruct((*start.shape[1:3], start.shape[0] * BCOLS), F32),
        HBM,
        [pltpu.VMEM((*start.shape[1:3], start.shape[0] * BCOLS), F32), pltpu.SemaphoreType.DMA((5,))],
        1_000_000,
        "scale_start",
    )


def add_kernel(*refs):
    *parts, out = refs
    total = parts[0][...]
    for part in parts[1:]:
        total += part[...]
    out[...] = total


def add(parts):
    return call(
        add_kernel, parts, [VMEM] * len(parts), jax.ShapeDtypeStruct(parts[0].shape, F32), VMEM, [], 1, "add_shares"
    )


def share_out(share):
    count = lax.axis_size("col")
    if count != 8:
        return [lax.all_to_all(jnp.broadcast_to(share, (count, BCOLS)), "col", 0, 0, tiled=True)]
    share = add([share, core_exchange(share)])
    beside = lax.ppermute(share, "col", [(i, i ^ 4) for i in range(count)])
    apart = lax.ppermute(share, "col", [(i, i ^ (6 if i % 2 else 2)) for i in range(count)])
    return [share, beside, apart, core_exchange(apart)]

def core_exchange(value):
    count = lax.axis_size("col")
    return lax.ppermute(value, "col", [(i, i ^ 1) for i in range(count)])


def z_exchange(value):
    count = lax.axis_size("col")
    pairs = [(i, (i + 1) % count if i % 2 else (i - 1) % count) for i in range(count)]
    return lax.ppermute(value, "col", pairs)


def shards(adj_final, inverses, dep_lists, dep_points, weights):
    count = lax.axis_size("col")
    all_blocks = count * inverses.shape[1]
    fields = jnp.transpose(adj_final, (1, 0, 2))
    inverses = jnp.transpose(inverses, (0, 2, 1, 3))
    fields, inverses, dep_lists, dep_points, weights = (
        pltpu.with_memory_space_constraint(value, pltpu.HBM)
        for value in (fields, inverses, dep_lists, dep_points, weights)
    )

    to_near, to_far, z_diffused, targets, merged = first(
        1, all_blocks, fields, inverses, dep_lists, dep_points, weights
    )
    near_in = z_exchange(to_near)
    far_in = z_exchange(to_far)
    core_diffused, turned, pieces = side(1, fields, targets, merged, inverses)
    core_in = [core_exchange(piece) for piece in pieces]
    own = inner(1, z_diffused, core_diffused, targets, merged)

    to_far, partial, diffused_near = near(0, own, near_in, turned, targets, merged)
    next_far_in = z_exchange(to_far)
    to_near, diffused_far = far(0, own, far_in, partial, turned, targets, merged)
    next_near_in = z_exchange(to_near)
    diffused_core, pieces = core(0, own, turned, targets, merged, core_in, to_near)
    next_core_in = [core_exchange(piece) for piece in pieces]
    diffused = (diffused_core, diffused_near, diffused_far)
    own, mid = outer(0, own, near_in, far_in, core_in, diffused, targets, merged)

    start, lane_sums = most(own, next_core_in, next_far_in)
    shares = share_out(last(start, next_near_in, lane_sums))
    lanczos = scale(start, next_near_in, shares, adj_final.size * count)
    return jnp.transpose(mid, (1, 0, 2)), jnp.transpose(lanczos, (1, 0, 2))


def solution(mesh):
    in_specs = (
        P("mem", None, "col"),
        P("mem", "col", None, None),
        P("mem", "col", None),
        P("mem", None, "col"),
        P("mem", None, "col"),
    )
    out_specs = (P("mem", None, "col"), P("mem", None, "col"))
    return jax.shard_map(shards, mesh=mesh, in_specs=in_specs, out_specs=out_specs, check_vma=False)
```

```python
import functools

import jax
import jax.numpy as jnp
from jax import lax
from jax.experimental import pallas as pl
from jax.experimental.pallas import tpu as pltpu
from jax.sharding import PartitionSpec as P

BCOLS = 128
REACH = 2
SLOTS = 5
POINTS = 4
STEPS = 2
VMEM_LIMIT = 32 * 1024 * 1024
NOWHERE = -(1 << 14)
PIECES = 3

eps_energy = 1e-06

F32 = jnp.float32
BF16 = jnp.bfloat16
ANY = pl.BlockSpec(memory_space=pl.ANY)
HBM = pl.BlockSpec(memory_space=pltpu.HBM)
VMEM = pl.BlockSpec(memory_space=pltpu.VMEM)


def z_blocks(block_count):
    follows = lax.rem(lax.axis_index("col"), 2)
    near = follows * (block_count - 1)
    away = 2 * follows - 1
    return near, near - away, near + away, near + 2 * away


def core_side(block_count):
    follows = 1 - lax.rem(lax.axis_index("col"), 2)
    return follows * (block_count - REACH), follows * (block_count + REACH) - REACH


def lanes(block, count=1):
    return pl.ds(pl.multiple_of(block * BCOLS, BCOLS), count * BCOLS)


def split(value):
    high = value.astype(BF16)
    return high, (value - high.astype(F32)).astype(BF16)


def target_columns(points, routes, step, block, block_count, all_blocks):
    slots = points // BCOLS
    here = lax.axis_index("col") * block_count + block
    found = jnp.zeros_like(points)
    for slot in range(SLOTS):
        offset = lax.rem(routes[step, block, slot] - here + REACH + all_blocks, all_blocks) - REACH
        found = jnp.where(slots == slot, (block + offset) * BCOLS, found)
    return found + points % BCOLS


def merge_points(targets, weights):
    targets = [targets[p : p + 1] for p in range(POINTS)]
    weights = [weights[p : p + 1] for p in range(POINTS)]
    for point in range(1, POINTS):
        for earlier in range(point):
            same = targets[point] == targets[earlier]
            weights[earlier] = weights[earlier] + jnp.where(same, weights[point], 0.0)
            targets[point] = jnp.where(same, NOWHERE, targets[point])
    return jnp.concatenate(targets, axis=0), jnp.concatenate(weights, axis=0)


def whole_matrix(targets, weights, first_column, rows=BCOLS):
    row = lax.broadcasted_iota(jnp.int32, (rows, targets.shape[1]), 0) + first_column
    total = jnp.zeros(row.shape, F32)
    for point in range(POINTS):
        total = jnp.where(row == targets[point : point + 1], weights[point : point + 1], total)
    return total


def spread_matrix(targets, weights, first_column, rows=BCOLS):
    return split(whole_matrix(targets, weights, first_column, rows))


def product(left, right, dims):
    return lax.dot_general(left, right, (dims, ((), ())), preferred_element_type=F32)


def rows_of(ref):
    levels, variables, columns = ref.shape
    return ref.reshape(levels * variables, columns)


def diffuse(turned, field, out):
    levels, variables, columns = field.shape
    source, result = rows_of(field), rows_of(out)
    every = [pl.ds(v, levels, stride=variables) for v in range(variables)]
    wide = split(jnp.concatenate([source[rows, :] for rows in every], axis=1))
    turned = split(turned)
    dims = ((1,), (0,))
    total = product(turned[0], wide[0], dims) + (
        product(turned[0], wide[1], dims) + product(turned[1], wide[0], dims)
    )
    for v, rows in enumerate(every):
        result[rows, :] = total[:, v * columns : (v + 1) * columns]


def spread(diffused, matrix):
    high, low = split(jnp.concatenate([rows_of(block)[...] for block in diffused], axis=1))
    left = jnp.concatenate([high, low, high], axis=1)
    right = jnp.concatenate([matrix[0], matrix[0], matrix[1]], axis=1)
    return product(left, right, ((1,), (1,)))


def side_matrix(targets, weights, step, blocks, first_columns):
    parts = []
    for block in blocks:
        cols = lanes(block)
        halves = [spread_matrix(targets[step, :, cols], weights[step, :, cols], column) for column in first_columns]
        parts.append([jnp.concatenate(half, axis=0) for half in zip(*halves)])
    return [jnp.concatenate(part, axis=1) for part in zip(*parts)]


def call(kernel, operands, in_specs, outs, out_specs, scratch, flops, name, limit=VMEM_LIMIT):
    return pl.pallas_call(
        kernel,
        out_shape=outs,
        in_specs=in_specs,
        out_specs=out_specs,
        scratch_shapes=scratch,
        compiler_params=pltpu.CompilerParams(vmem_limit_bytes=limit),
        cost_estimate=pl.CostEstimate(flops=flops, bytes_accessed=min(flops, 1_000_000), transcendentals=0),
        name=name,
    )(*operands)


def start_copies(sems, pairs):
    copies = [pltpu.make_async_copy(source, target, sems.at[i]) for i, (source, target) in enumerate(pairs)]
    for copy in copies:
        copy.start()
    return copies


def first_kernel(
    step, all_blocks, fields, inverses, routes, points, weights,
    to_near, to_far, diffused, targets, merged, field, inverse, route, point, weight, sems,
):
    block_count = inverses.shape[2]
    near, far, target_near, target_far = z_blocks(block_count)
    copies = start_copies(
        sems,
        [
            (routes, route),
            (points, point),
            (weights, weight),
            (inverses.at[step, :, near], inverse.at[0]),
            (inverses.at[step, :, far], inverse.at[1]),
            (fields.at[:, :, lanes(near)], field.at[0]),
            (fields.at[:, :, lanes(far)], field.at[1]),
        ],
    )
    for copy in copies[:3]:
        copy.wait()
    for number in range(STEPS):
        for j in range(block_count):
            cols = slice(j * BCOLS, (j + 1) * BCOLS)
            found = target_columns(point[number, :, cols], route, number, j, block_count, all_blocks)
            targets[number, :, cols], merged[number, :, cols] = merge_points(found, weight[number, :, cols])
    matrix = side_matrix(targets, merged, step, (near, far), (target_near * BCOLS, target_far * BCOLS))
    for copy in copies[3:5]:
        copy.wait()
    turned = [inverse[j].T for j in range(REACH)]
    for j in range(REACH):
        copies[5 + j].wait()
        diffuse(turned[j], field.at[j], diffused.at[j])
    sums = spread([diffused.at[0], diffused.at[1]], matrix)
    rows_of(to_near)[...] = sums[:, :BCOLS]
    rows_of(to_far)[...] = sums[:, BCOLS:]


def level_pieces(levels):
    return [slice(levels * part // PIECES, levels * (part + 1) // PIECES) for part in range(PIECES)]


def piece_shapes(whole):
    return [
        jax.ShapeDtypeStruct((whole.shape[0], levels.stop - levels.start, *whole.shape[2:]), F32)
        for levels in level_pieces(whole.shape[1])
    ]


def store_pieces(sums, pieces, levels):
    for piece, part in zip(pieces, level_pieces(levels)):
        variables = piece.shape[2]
        rows = slice(part.start * variables, part.stop * variables)
        for j in range(REACH):
            rows_of(piece.at[j])[...] = sums[rows, j * BCOLS : (j + 1) * BCOLS]


def add_pieces(pieces, block, out):
    for piece, levels in zip(pieces, level_pieces(out.shape[0])):
        out[levels] += piece[block]


def blocks(like, *count):
    return jax.ShapeDtypeStruct((*count, *like.shape[-3:-1], BCOLS), F32)


def first(step, all_blocks, fields, inverses, routes, points, weights):
    one, two = blocks(fields), blocks(fields, REACH)
    return call(
        functools.partial(first_kernel, step, all_blocks),
        (fields, inverses, routes, points, weights),
        [HBM] * 5,
        (
            one,
            one,
            two,
            jax.ShapeDtypeStruct(points.shape, jnp.int32),
            jax.ShapeDtypeStruct(weights.shape, F32),
        ),
        (VMEM,) * 5,
        [
            pltpu.VMEM(two.shape, F32),
            pltpu.VMEM((REACH, inverses.shape[1], inverses.shape[3]), F32),
            pltpu.SMEM(routes.shape, jnp.int32),
            pltpu.VMEM(points.shape, jnp.int32),
            pltpu.VMEM(weights.shape, F32),
            pltpu.SemaphoreType.DMA((7,)),
        ],
        400_000_000,
        f"first_step{step}",
    )


def side_kernel(step, fields, targets, weights, inverses, diffused, turned, matrices, *refs):
    to_core, (field, inverse, next_inverse, sems) = refs[:-4], refs[-4:]
    block_count = inverse.shape[1]
    side, first_target = core_side(block_count)
    copies = start_copies(
        sems,
        [(fields.at[:, :, lanes(side + j)], field.at[j]) for j in range(REACH)]
        + [(inverses.at[step], inverse), (inverses.at[step - 1], next_inverse)],
    )
    columns = (first_target * BCOLS, (first_target + 1) * BCOLS)
    matrix = side_matrix(targets, weights, step, (side, side + 1), columns)
    copies[REACH].wait()
    for j in range(REACH):
        copies[j].wait()
        diffuse(inverse[:, side + j, :].T, field.at[j], diffused.at[j])
    store_pieces(spread([diffused.at[j] for j in range(REACH)], matrix), to_core, field.shape[1])
    near, far, target_near, target_far = z_blocks(block_count)
    for row, (block, target) in enumerate(((near, target_far), (near, target_near), (far, target_near))):
        cols = lanes(block)
        matrices[row * BCOLS : (row + 1) * BCOLS] = whole_matrix(
            targets[step - 1, :, cols], weights[step - 1, :, cols], target * BCOLS
        )
    copies[REACH + 1].wait()
    for j in range(block_count):
        turned[j] = next_inverse[:, j, :].T


def side(step, fields, targets, weights, inverses):
    two = blocks(fields, REACH)
    _, levels, block_count, _ = inverses.shape
    diffused, turned, matrices, *pieces = call(
        functools.partial(side_kernel, step),
        (fields, targets, weights, inverses),
        [HBM] + [VMEM] * 2 + [HBM],
        (
            two,
            jax.ShapeDtypeStruct((block_count, levels, levels), F32),
            jax.ShapeDtypeStruct((3 * BCOLS, BCOLS), F32),
            *piece_shapes(two),
        ),
        (VMEM,) * (3 + PIECES),
        [
            pltpu.VMEM(two.shape, F32),
            pltpu.VMEM(inverses.shape[1:], F32),
            pltpu.VMEM(inverses.shape[1:], F32),
            pltpu.SemaphoreType.DMA((REACH + 2,)),
        ],
        2_000_000_000,
        f"side_step{step}",
    )
    return diffused, turned, matrices, pieces


def inner_kernel(step, z_diffused, core_diffused, targets, weights, own, tall):
    block_count = own.shape[0]
    near, far, _, _ = z_blocks(block_count)
    first = core_side(block_count)[0]
    tall[near] = z_diffused[0]
    tall[far] = z_diffused[1]
    for j in range(REACH):
        tall[first + j] = core_diffused[j]
    matrix = spread_matrix(targets[step], weights[step], 0, block_count * BCOLS)
    sums = spread([tall.at[j] for j in range(block_count)], matrix)
    for j in range(block_count):
        rows_of(own.at[j])[...] = sums[:, j * BCOLS : (j + 1) * BCOLS]


def inner(step, z_diffused, core_diffused, targets, weights):
    whole = blocks(z_diffused, targets.shape[2] // BCOLS)
    return call(
        functools.partial(inner_kernel, step),
        (z_diffused, core_diffused, targets, weights),
        [VMEM] * 4,
        whole,
        VMEM,
        [pltpu.VMEM(whole.shape, F32)],
        2_000_000_000,
        f"inner_step{step}",
    )


def near_kernel(own, near_in, turned, matrices, to_far, to_near, diffused, field):
    near = z_blocks(own.shape[0])[0]
    field[...] = own[near] + near_in[...]
    diffuse(turned[near], field, diffused)
    sums = spread([diffused], split(matrices[: 2 * BCOLS]))
    rows_of(to_far)[...] = sums[:, :BCOLS]
    rows_of(to_near)[...] = sums[:, BCOLS:]


def near(step, own, near_in, turned, matrices):
    one = blocks(own)
    return call(
        near_kernel,
        (own, near_in, turned, matrices),
        [VMEM] * 4,
        (one, one, one),
        (VMEM,) * 3,
        [pltpu.VMEM(one.shape, F32)],
        300_000_000,
        f"near_step{step}",
    )


def far_kernel(own, far_in, partial, turned, matrices, to_near, diffused, field):
    far = z_blocks(own.shape[0])[1]
    field[...] = own[far] + far_in[...]
    diffuse(turned[far], field, diffused)
    rows_of(to_near)[...] = rows_of(partial)[...] + spread([diffused], split(matrices[2 * BCOLS :]))


def far(step, own, far_in, partial, turned, matrices):
    one = blocks(own)
    return call(
        far_kernel,
        (own, far_in, partial, turned, matrices),
        [VMEM] * 5,
        (one, one),
        (VMEM,) * 2,
        [pltpu.VMEM(one.shape, F32)],
        300_000_000,
        f"far_step{step}",
    )


def core_kernel(step, own, turned, targets, weights, _, *refs):
    core_in, (diffused, *to_core, field) = refs[:PIECES], refs[PIECES:]
    side, first_target = core_side(own.shape[0])
    columns = (first_target * BCOLS, (first_target + 1) * BCOLS)
    matrix = side_matrix(targets, weights, step, (side, side + 1), columns)
    for j in range(REACH):
        field[...] = own[side + j]
        add_pieces(core_in, j, field)
        diffuse(turned[side + j], field, diffused.at[j])
    store_pieces(spread([diffused.at[j] for j in range(REACH)], matrix), to_core, own.shape[1])


def core(step, own, turned, targets, weights, core_in, behind):
    one, two = blocks(own), blocks(own, REACH)
    diffused, *to_core = call(
        functools.partial(core_kernel, step),
        (own, turned, targets, weights, behind, *core_in),
        [VMEM] * 4 + [ANY] + [VMEM] * PIECES,
        (two, *piece_shapes(two)),
        (VMEM,) * (1 + PIECES),
        [pltpu.VMEM(one.shape, F32)],
        1,
        f"core_step{step}",
    )
    return diffused, to_core


def outer_kernel(
    step, own, near_in, far_in, diffused_core, diffused_near, diffused_far, targets, weights, *refs
):
    core_in, (sums, mid, field, tall, sems) = refs[:PIECES], refs[PIECES:]
    block_count = own.shape[0]
    near, far, _, _ = z_blocks(block_count)
    side = core_side(block_count)[0]
    for j in range(REACH):
        field[side + j] = own[side + j]
        add_pieces(core_in, j, field.at[side + j])
        tall[side + j] = diffused_core[j]
    field[near] = own[near] + near_in[...]
    field[far] = own[far] + far_in[...]
    tall[near] = diffused_near[...]
    tall[far] = diffused_far[...]
    copies = start_copies(sems, [(field.at[j], mid.at[:, :, lanes(j)]) for j in range(block_count)])
    matrix = spread_matrix(targets[step], weights[step], 0, block_count * BCOLS)
    total = spread([tall.at[j] for j in range(block_count)], matrix)
    for j in range(block_count):
        rows_of(sums.at[j])[...] = total[:, j * BCOLS : (j + 1) * BCOLS]
    for copy in copies:
        copy.wait()


def outer(step, own, near_in, far_in, core_in, diffused, targets, weights):
    block_count, levels, variables, _ = own.shape
    return call(
        functools.partial(outer_kernel, step),
        (own, near_in, far_in, *diffused, targets, weights, *core_in),
        [VMEM] * (8 + PIECES),
        (
            blocks(own, block_count),
            jax.ShapeDtypeStruct((levels, variables, block_count * BCOLS), F32),
        ),
        (VMEM, HBM),
        [
            pltpu.VMEM(own.shape, F32),
            pltpu.VMEM(own.shape, F32),
            pltpu.SemaphoreType.DMA((block_count,)),
        ],
        1,
        f"outer_step{step}",
    )


def squares(value):
    rows = value.reshape(value.shape[0] * value.shape[1], value.shape[2])
    return jnp.sum(rows * rows, axis=0, keepdims=True)


def most_kernel(own, far_in, *refs):
    core_in, (start, lane_sums) = refs[:PIECES], refs[PIECES:]
    block_count = own.shape[0]
    near, far, _, _ = z_blocks(block_count)
    side = core_side(block_count)[0]
    value = own[far] + far_in[...]
    start[far] = value
    start[near] = own[near]
    total = squares(value)
    for j in range(REACH):
        start[side + j] = own[side + j]
        add_pieces(core_in, j, start.at[side + j])
        total += squares(start[side + j])
    lane_sums[...] = total


def most(own, core_in, far_in):
    return call(
        most_kernel,
        (own, far_in, *core_in),
        [VMEM] * (2 + PIECES),
        (jax.ShapeDtypeStruct(own.shape, F32), jax.ShapeDtypeStruct((1, BCOLS), F32)),
        (VMEM, VMEM),
        [],
        1_000_000,
        "squares_of_most_blocks",
    )


def last_kernel(start, near_in, lane_sums, shares):
    near = z_blocks(start.shape[0])[0]
    shares[...] = lane_sums[...] + squares(start[near] + near_in[...])


def last(start, near_in, lane_sums):
    return call(
        last_kernel,
        (start, near_in, lane_sums),
        [VMEM] * 3,
        jax.ShapeDtypeStruct(lane_sums.shape, F32),
        VMEM,
        [],
        1_000_000,
        "squares_of_last_block",
    )


def scale_kernel(cells, start, near_in, *refs):
    *shares, out, held, sems = refs
    block_count = start.shape[0]
    near = z_blocks(block_count)[0]
    total = shares[0][...]
    for share in shares[1:]:
        total += share[...]
    energy = jnp.sum(total) / cells
    factor = 1.0 / jnp.sqrt(jnp.full((1, 1, 1), energy + eps_energy, F32))
    levels = start.shape[1]
    parts = 5
    copies = []
    for part in range(parts):
        rows = slice(levels * part // parts, levels * (part + 1) // parts)
        for j in range(block_count):
            cols = slice(j * BCOLS, (j + 1) * BCOLS)
            held[rows, :, cols] = (start[j, rows] + jnp.where(near == j, near_in[rows], 0.0)) * factor
        copies.append(pltpu.make_async_copy(held.at[rows], out.at[rows], sems.at[part]))
        copies[-1].start()
    for copy in copies:
        copy.wait()


def scale(start, near_in, shares, cells):
    return call(
        functools.partial(scale_kernel, cells),
        (start, near_in, *shares),
        [VMEM] * (2 + len(shares)),
        jax.ShapeDtypeStruct((*start.shape[1:3], start.shape[0] * BCOLS), F32),
        HBM,
        [pltpu.VMEM((*start.shape[1:3], start.shape[0] * BCOLS), F32), pltpu.SemaphoreType.DMA((5,))],
        1_000_000,
        "scale_start",
    )


def add_kernel(*refs):
    *parts, out = refs
    total = parts[0][...]
    for part in parts[1:]:
        total += part[...]
    out[...] = total


def add(parts):
    return call(
        add_kernel, parts, [VMEM] * len(parts), jax.ShapeDtypeStruct(parts[0].shape, F32), VMEM, [], 1, "add_shares"
    )


def share_out(share):
    count = lax.axis_size("col")
    if count != 8:
        return [lax.all_to_all(jnp.broadcast_to(share, (count, BCOLS)), "col", 0, 0, tiled=True)]
    share = add([share, core_exchange(share)])
    beside = lax.ppermute(share, "col", [(i, i ^ 4) for i in range(count)])
    apart = lax.ppermute(share, "col", [(i, i ^ (6 if i % 2 else 2)) for i in range(count)])
    return [share, beside, apart, core_exchange(apart)]

def core_exchange(value):
    count = lax.axis_size("col")
    return lax.ppermute(value, "col", [(i, i ^ 1) for i in range(count)])


def z_exchange(value):
    count = lax.axis_size("col")
    pairs = [(i, (i + 1) % count if i % 2 else (i - 1) % count) for i in range(count)]
    return lax.ppermute(value, "col", pairs)


def shards(adj_final, inverses, dep_lists, dep_points, weights):
    count = lax.axis_size("col")
    all_blocks = count * inverses.shape[1]
    fields = jnp.transpose(adj_final, (1, 0, 2))
    inverses = jnp.transpose(inverses, (0, 2, 1, 3))
    fields, inverses, dep_lists, dep_points, weights = (
        pltpu.with_memory_space_constraint(value, pltpu.HBM)
        for value in (fields, inverses, dep_lists, dep_points, weights)
    )

    to_near, to_far, z_diffused, targets, merged = first(
        1, all_blocks, fields, inverses, dep_lists, dep_points, weights
    )
    near_in = z_exchange(to_near)
    far_in = z_exchange(to_far)
    core_diffused, turned, matrices, pieces = side(1, fields, targets, merged, inverses)
    core_in = [core_exchange(piece) for piece in pieces]
    own = inner(1, z_diffused, core_diffused, targets, merged)

    to_far, partial, diffused_near = near(0, own, near_in, turned, matrices)
    next_far_in = z_exchange(to_far)
    to_near, diffused_far = far(0, own, far_in, partial, turned, matrices)
    next_near_in = z_exchange(to_near)
    diffused_core, pieces = core(0, own, turned, targets, merged, core_in, to_near)
    next_core_in = [core_exchange(piece) for piece in pieces]
    diffused = (diffused_core, diffused_near, diffused_far)
    own, mid = outer(0, own, near_in, far_in, core_in, diffused, targets, merged)

    start, lane_sums = most(own, next_core_in, next_far_in)
    shares = share_out(last(start, next_near_in, lane_sums))
    lanczos = scale(start, next_near_in, shares, adj_final.size * count)
    return jnp.transpose(mid, (1, 0, 2)), jnp.transpose(lanczos, (1, 0, 2))


def solution(mesh):
    in_specs = (
        P("mem", None, "col"),
        P("mem", "col", None, None),
        P("mem", "col", None),
        P("mem", None, "col"),
        P("mem", None, "col"),
    )
    out_specs = (P("mem", None, "col"), P("mem", None, "col"))
    return jax.shard_map(shards, mesh=mesh, in_specs=in_specs, out_specs=out_specs, check_vma=False)
```
